256 devices in a mesh: row: 8 (over x, core), col: 32 (over y, z).
Axes of the slice: x: 4, y: 4, z: 8, core: 2. Of those that a mesh axis runs over, the one named last changes fastest.
Arguments:
- src_emb: bfloat16 [4096, 1024], P('row', 'col'), may hold values from -6 to 6
- tgt_emb: bfloat16 [16384, 1024], P('col', 'row'), may hold values from -8.5 to 8.5
- rotation: bfloat16 [1024, 1024], replicated, may hold values from -1.1 to 1.1
- src_ids: int32 [4096], P('row'), may hold values from 0 to 99999
- tgt_ids: int32 [16384], P('col'), may hold values from 0 to 99999
Outputs:
- polar_step: float32 [1024, 1024], P(('row', 'col'))
The draws below stay inside these ranges and needn't reach their ends.
All inputs are finite; a program needn't handle non-finite values.
Results may differ from the reference program's by a relative error of at most 0.01.
Values may be sent and summed in bfloat16 or wider, within the bound.
A program may use at most 64 MiB of HBM per device.

```python
import math
import jax
import jax.numpy as jnp
from jax import lax

D = 1024
SB = 512
ITERS = 3
NS = 4096
NT = 16384


def shared_source(key):
    values = jax.random.normal(jax.random.fold_in(key, 101), (NS, D), jnp.float32)
    return jnp.clip(values, -6.0, 6.0)


def shared_features(key):
    order = jax.random.permutation(jax.random.fold_in(key, 102), D).astype(jnp.int32)
    flips = jax.random.randint(jax.random.fold_in(key, 103), (D,), 0, 2)
    signs = (2 * flips - 1).astype(jnp.float32)
    return (order, signs)


def draw_src_emb(key, part):
    source = shared_source(key)
    return source.astype(jnp.bfloat16)


def draw_tgt_emb(key, part):
    source = shared_source(key)
    order, signs = shared_features(key)
    key = jax.random.fold_in(key, 7)
    partner = jax.random.randint(jax.random.fold_in(key, 1), (NT,), 0, NS).astype(jnp.int32)
    matched = (jax.random.randint(jax.random.fold_in(key, 2), (NT,), 0, 10) < 7).astype(jnp.float32)
    strength = jax.random.uniform(jax.random.fold_in(key, 3), (NT,), jnp.float32, 0.35, 0.95)
    noise = jnp.clip(jax.random.normal(jax.random.fold_in(key, 4), (NT, D), jnp.float32), -6.0, 6.0)
    strength = strength * matched
    inverse = jnp.argsort(order, stable=True).astype(jnp.int32)
    flipped = source * signs[None, :]
    image = jnp.take(jnp.take(flipped, partner, axis=0), inverse, axis=1)
    rest = jnp.sqrt(jnp.maximum(1.0 - strength * strength, 0.0))
    target = strength[:, None] * image + rest[:, None] * noise
    return target.astype(jnp.bfloat16)


def draw_rotation(key, part):
    order, signs = shared_features(key)
    key = jax.random.fold_in(key, 9)
    noise = jnp.clip(jax.random.normal(key, (D, D), jnp.float32), -6.0, 6.0)
    hits = (order[:, None] == jnp.arange(D, dtype=jnp.int32)[None, :]).astype(jnp.float32)
    mapping = 0.9 * signs[:, None] * hits + 0.45 * noise / math.sqrt(D)
    return mapping.astype(jnp.bfloat16)


def with_ends(drawn, rng, smallest, largest):
    dims = drawn.shape
    spot = [jax.random.randint(jax.random.fold_in(rng, axis), (), 0, dims[axis]) for axis in range(len(dims))]
    drawn = drawn.at[tuple(spot)].set(smallest)
    longest = dims.index(max(dims))
    spot[longest] = (spot[longest] + 1) % dims[longest]
    return drawn.at[tuple(spot)].set(largest)


def setup_inputs(seed: int = 0) -> dict:
    key_list = jax.random.split(jax.random.key(seed), 6)
    return {
        "src_emb": draw_src_emb(jax.random.fold_in(key_list[5], 71), 0),
        "tgt_emb": draw_tgt_emb(jax.random.fold_in(key_list[5], 71), 0),
        "rotation": draw_rotation(jax.random.fold_in(key_list[5], 71), 0),
        "src_ids": with_ends(jax.random.randint(key_list[3], (NS,), 0, 100000), jax.random.fold_in(key_list[3], 1), 0, 99999).astype(jnp.int32),
        "tgt_ids": with_ends(jax.random.randint(key_list[4], (NT,), 0, 100000), jax.random.fold_in(key_list[4], 1), 0, 99999).astype(jnp.int32),
    }


def unit_rows(emb):
    values = emb.astype(jnp.float32)
    scale = lax.rsqrt(lax.optimization_barrier(jnp.mean(values * values, axis=1, keepdims=True)) + 1e-06) / math.sqrt(D)
    return (values * scale).astype(jnp.bfloat16)

def reference(src_emb, tgt_emb, rotation, src_ids, tgt_ids):
    src_unit = unit_rows(src_emb)
    tgt_unit = unit_rows(tgt_emb)
    rotated = jnp.dot(src_unit, rotation, preferred_element_type=jnp.float32).astype(jnp.bfloat16)
    blocks = rotated.reshape(NS // SB, SB, D)

    def kernel_block(block):
        return jnp.exp(jnp.dot(block, tgt_unit.T, preferred_element_type=jnp.float32) / 0.03)
    kernel = lax.map(kernel_block, blocks).reshape(NS, NT)
    src_mass = lax.rsqrt(1000.0 + src_ids.astype(jnp.float32))
    tgt_mass = lax.rsqrt(1000.0 + tgt_ids.astype(jnp.float32))
    tgt_scale = jnp.ones((NT,), jnp.float32)
    for step in range(ITERS):
        src_scale = src_mass / jnp.dot(kernel, tgt_scale, precision=lax.Precision.HIGHEST)
        tgt_scale = tgt_mass / jnp.dot(src_scale, kernel, precision=lax.Precision.HIGHEST)

    def cross_block(items):
        ker, scl, units = items
        plan = (scl[:, None] * ker * tgt_scale[None, :]).astype(jnp.bfloat16)
        carried = jnp.dot(plan, tgt_unit, preferred_element_type=jnp.float32).astype(jnp.bfloat16)
        return jnp.dot(units.T, carried, preferred_element_type=jnp.float32)
    terms = lax.map(cross_block, (kernel.reshape(NS // SB, SB, NT), src_scale.reshape(NS // SB, SB), src_unit.reshape(NS // SB, SB, D)))
    cross = lax.optimization_barrier(jnp.sum(terms, axis=0))
    normed = cross * lax.rsqrt(jnp.mean(cross * cross) + 1e-30) / (2.0 * math.sqrt(D))
    gram = jnp.dot(normed, normed.T, precision=lax.Precision.HIGHEST)
    cubic = jnp.dot(gram, normed, precision=lax.Precision.HIGHEST)
    return math.sqrt(D) * (1.5 * normed - 0.5 * cubic)
```

```python
import math

import jax
import jax.numpy as jnp
from jax import lax
from jax.experimental import pallas as pl
from jax.experimental.pallas import tpu as pltpu
from jax.sharding import PartitionSpec as P

MESH = pl.DeviceIdType.MESH
F32 = jnp.float32
BF16 = jnp.bfloat16
D = 1024
W = 512
ITERS = 3
X, Y, Z = 4, 4, 8
ROWS, COLS = 2 * X, Y * Z
NN = (((1,), (0,)), ((), ()))
NT = (((1,), (1,)), ((), ()))


def dot(a, b, dims):
    return lax.dot_general(a, b, dims, preferred_element_type=F32)


def send(src, dst, send_sem, recv_sem, device):
    pltpu.make_async_remote_copy(
        src_ref=src, dst_ref=dst, send_sem=send_sem, recv_sem=recv_sem,
        device_id=device, device_id_type=MESH,
    ).start()


def wait(ref, sem):
    pltpu.make_async_copy(ref, ref, sem).wait()


def block(i, size):
    return pl.ds(pl.multiple_of(i * size, size), size)


def body(src_hbm, tgt_hbm, rot_hbm, src_ids, tgt_ids, out_ref,
         src_v, src_t, tgt, rot, u, kt, colbuf, rowbuf,
         a_mine, a_mate, a_x, a_out, yb, y_out, zb, z_out, xf,
         local, zs, xs, ss, rs):
    r, c = lax.axis_index("row"), lax.axis_index("col")
    x, core = r // 2, r % 2
    y, z = c // Z, c % Z
    mate = (2 * x + (1 - core), c)

    def xpeer(k):
        return (2 * ((x + k) % X) + core, c)

    def ypeer(k):
        return (r, Z * ((y + k) % Y) + z)

    def zpeer(k):
        return (r, Z * y + (z + k) % Z)

    def colpeer(k):
        return (r, (c + k) % COLS)

    def rowpeer(k):
        return ((r + k) % ROWS, c)

    load_src = pltpu.make_async_copy(src_hbm, src_v, local.at[0])
    load_src.start()
    my_tgt = tgt.at[:, block(r, 128)]
    load_tgt = pltpu.make_async_copy(tgt_hbm, my_tgt, local.at[1])
    load_tgt.start()
    load_rot = pltpu.make_async_copy(rot_hbm, rot, local.at[2])
    load_rot.start()
    bar = pltpu.get_barrier_semaphore()

    def greet_col(k, _):
        pl.semaphore_signal(bar, inc=1, device_id=colpeer(k), device_id_type=MESH)
        return 0

    def greet_row(k, _):
        pl.semaphore_signal(bar, inc=1, device_id=rowpeer(k), device_id_type=MESH)
        return 0

    lax.fori_loop(1, COLS, greet_col, 0)
    lax.fori_loop(1, ROWS, greet_row, 0)
    load_src.wait()
    eye = (lax.broadcasted_iota(jnp.int32, (32, 32), 0)
           == lax.broadcasted_iota(jnp.int32, (32, 32), 1)).astype(BF16)
    src_t[block(c, 32), :] = dot(eye, src_v[...], NT).astype(BF16)
    load_tgt.wait()
    pl.semaphore_wait(bar, COLS + ROWS - 2)

    mine = src_t.at[block(c, 32), :]
    for k in (1, 7, 2, 6, 3, 5, 4):
        send(mine, mine, ss.at[0], zs.at[k], zpeer(k))
    for k in (1, 3, 2):
        send(my_tgt, my_tgt, ss.at[1], xs.at[k], xpeer(k))
        send(mine, mine, ss.at[2], rs.at[2], ypeer(k))
    send(my_tgt, my_tgt, ss.at[3], rs.at[3], mate)

    def forward_src(k):
        got = src_t.at[block(Z * y + (z + Z - k) % Z, 32), :]
        wait(got, zs.at[k])
        for j in (1, 3, 2):
            send(got, got, ss.at[2], rs.at[2], ypeer(j))

    def forward_tgt(k):
        got = tgt.at[:, block(2 * ((x + X - k) % X) + core, 128)]
        wait(got, xs.at[k])
        send(got, got, ss.at[3], rs.at[3], mate)

    forward_src(1)
    forward_src(7)
    forward_tgt(1)
    forward_tgt(3)
    forward_src(2)
    forward_src(6)
    forward_tgt(2)
    forward_src(3)
    forward_src(5)
    forward_src(4)

    wait(tgt.at[:, pl.ds(0, 512)], rs.at[3])
    load_rot.wait()
    tv = tgt[...].astype(F32)
    tsum = jnp.sum(tv * tv, axis=1, keepdims=True)
    tscale = lax.rsqrt(tsum * (1.0 / D) + 1e-06) * (1.0 / math.sqrt(D))
    u[...] = (dot(tgt[...], rot[...], NT) * tscale).astype(BF16)
    tscale_l = jnp.transpose(jnp.broadcast_to(tscale, (W, 128)))[0:1, :]
    src_mass = lax.rsqrt(1000.0 + src_ids[...].astype(F32))
    tgt_mass = lax.rsqrt(1000.0 + tgt_ids[...].astype(F32))

    wait(src_t.at[pl.ds(0, 24 * 32), :], rs.at[2])
    sv = src_t[...].astype(F32)
    ssum = jnp.sum(sv * sv, axis=0, keepdims=True)
    sscale = lax.rsqrt(ssum * (1.0 / D) + 1e-06) * (1.0 / math.sqrt(D))
    kt[...] = jnp.exp(dot(u[...], src_t[...], NN) * (sscale * (1.0 / 0.03))).astype(BF16)

    row8 = lax.broadcasted_iota(jnp.int32, (8, W), 0)

    def matvec(v, dims):
        high = v.astype(BF16).astype(F32)
        both = jnp.where(row8 == 0, high, jnp.where(row8 == 1, v - high, 0.0)).astype(BF16)
        return jnp.sum(dot(both, kt[...], dims), axis=0, keepdims=True)

    def sum_col(part, it):
        colbuf[it, c] = part

        def one(k, _):
            send(colbuf.at[it, c], colbuf.at[it, c], ss.at[4 + it], rs.at[4 + it], colpeer(k))
            return 0

        lax.fori_loop(1, COLS, one, 0)
        wait(colbuf.at[it, pl.ds(0, COLS - 1)], rs.at[4 + it])
        return jnp.sum(colbuf[it], axis=0)

    def start_row(part, it):
        rowbuf[it, r] = part
        for k in range(1, ROWS):
            send(rowbuf.at[it, r], rowbuf.at[it, r], ss.at[7 + it], rs.at[7 + it], rowpeer(k))

    def end_row(it):
        wait(rowbuf.at[it, pl.ds(0, ROWS - 1)], rs.at[7 + it])
        return jnp.sum(rowbuf[it], axis=0)

    tgt_scale = jnp.ones((1, W), F32)
    for it in range(ITERS):
        src_scale = src_mass / sum_col(matvec(tgt_scale, NN), it)
        start_row(matvec(src_scale, NT), it)
        if it < ITERS - 1:
            tgt_scale = tgt_mass / end_row(it)

    kt[...] = (kt[...].astype(F32) * (src_scale * sscale)).astype(BF16)
    for j in range(X):
        a_out[j] = dot(src_t[block(2 * j + (1 - core), 128), :], kt[...], NT).astype(BF16)
        send(a_out.at[j], a_mate.at[j], ss.at[10], rs.at[10], mate)
    for j in range(X):
        a_mine[j] = dot(src_t[block(2 * j + core, 128), :], kt[...], NT)
    wait(a_mate, rs.at[10])
    for j in range(X):
        a_out[X + j] = (a_mine[j] + a_mate[j].astype(F32)).astype(BF16)
    for k in (2, 1, 3):
        send(a_out.at[X + (x + k) % X], a_x.at[k - 1], ss.at[11], rs.at[11], xpeer(k))
    tgt_scale = tgt_mass / end_row(ITERS - 1)
    wait(a_x, rs.at[11])
    total = (a_mine[x] + a_mate[x].astype(F32)) + (
        a_x[0].astype(F32) + a_x[1].astype(F32) + a_x[2].astype(F32))
    total = (total * (tgt_scale * tscale_l)).astype(BF16)

    cross = dot(total, tgt[...], NN)
    for j in range(Y):
        y_out[j] = cross[:, 256 * j:256 * (j + 1)].astype(BF16)
    for k in (2, 1, 3):
        send(y_out.at[(y + k) % Y], yb.at[k - 1], ss.at[12], rs.at[12], ypeer(k))
    wait(yb, rs.at[12])
    part = (y_out[y].astype(F32) + yb[0].astype(F32)) + (yb[1].astype(F32) + yb[2].astype(F32))
    z_out[...] = part.astype(BF16).reshape(Z, 16, 256)
    for k in (4, 3, 5, 2, 6, 1, 7):
        send(z_out.at[(z + k) % Z], zb.at[k - 1], ss.at[13], rs.at[13], zpeer(k))
    wait(zb, rs.at[13])
    own = z_out[z].astype(F32) + jnp.sum(zb[...].astype(F32), axis=0)

    def part_ref(row, first, count, col, rows=1):
        return xf.at[pl.ds(pl.multiple_of(row * 128 + first, 16), count),
                     pl.ds(pl.multiple_of(col * 256, 256), 256)]

    xf[pl.ds(pl.multiple_of(r * 128 + z * 16, 16), 16), block(y, 256)] = own.astype(BF16)
    mine = part_ref(r, z * 16, 16, y)
    for k in (4, 3, 5, 2, 6, 1, 7):
        send(mine, mine, ss.at[14], rs.at[14], zpeer(k))
    wait(xf.at[pl.ds(0, 112), pl.ds(0, 256)], rs.at[14])

    first_half, second_half = part_ref(r, 0, 64, y), part_ref(r, 64, 64, y)
    for k in (2, 1, 3):
        send(first_half, first_half, ss.at[15], zs.at[8 + k], xpeer(k))
        send(second_half, second_half, ss.at[16], zs.at[12 + k], ypeer(k))
    for k in (1, 3, 2):
        send(first_half, first_half, ss.at[17], rs.at[17], ypeer(k))
        send(second_half, second_half, ss.at[18], rs.at[18], xpeer(k))
    both = part_ref(r, 0, 128, y)
    send(both, both, ss.at[19], rs.at[19], mate)
    for k in (1, 3, 2):
        got = part_ref(2 * ((x + X - k) % X) + core, 0, 64, y)
        wait(got, zs.at[8 + k])
        for j in (1, 3, 2):
            send(got, got, ss.at[17], rs.at[17], ypeer(j))
        send(got, got, ss.at[19], rs.at[19], mate)
        got = part_ref(r, 64, 64, (y + Y - k) % Y)
        wait(got, zs.at[12 + k])
        for j in (1, 3, 2):
            send(got, got, ss.at[18], rs.at[18], xpeer(j))
        send(got, got, ss.at[19], rs.at[19], mate)
    wait(xf.at[pl.ds(0, 192), :], rs.at[17])
    wait(xf.at[pl.ds(0, 192), :], rs.at[18])
    for k in range(1, X):
        for j in range(1, Y):
            got = part_ref(2 * ((x + k) % X) + core, 0, 64, (y + j) % Y)
            send(got, got, ss.at[19], rs.at[19], mate)
            got = part_ref(2 * ((x + k) % X) + core, 64, 64, (y + j) % Y)
            send(got, got, ss.at[19], rs.at[19], mate)
    for k in range(1, Y):
        got = part_ref(r, 0, 64, (y + k) % Y)
        send(got, got, ss.at[19], rs.at[19], mate)
        got = part_ref(2 * ((x + k) % X) + core, 64, 64, y)
        send(got, got, ss.at[19], rs.at[19], mate)
    wait(xf.at[pl.ds(0, 512), :], rs.at[19])

    pick = (lax.broadcasted_iota(jnp.int32, (8, 128), 1)
            == 4 * c + lax.broadcasted_iota(jnp.int32, (8, 128), 0) % 4).astype(BF16)
    rows = dot(pick, xf[block(r, 128), :], NN)
    full = xf[...].astype(F32)
    mean = jnp.sum(full * full, keepdims=True) * (1.0 / (D * D))
    scale = lax.rsqrt(mean + 1e-30) * (1.0 / (2.0 * math.sqrt(D)))
    gram = dot(rows.astype(BF16), xf[...], NT) * (scale * scale)
    cubic = dot(gram.astype(BF16), xf[...], NN) * scale
    result = math.sqrt(D) * (1.5 * (rows * scale) - 0.5 * cubic)
    out_ref[...] = result[0:4, :]

    wait(src_t.at[pl.ds(0, 224), :], ss.at[0])
    wait(tgt.at[:, pl.ds(0, 384)], ss.at[1])
    wait(src_t.at[pl.ds(0, 768), :], ss.at[2])
    wait(tgt.at[:, pl.ds(0, 512)], ss.at[3])
    for it in range(ITERS):
        wait(colbuf.at[it, pl.ds(0, COLS - 1)], ss.at[4 + it])
        wait(rowbuf.at[it, pl.ds(0, ROWS - 1)], ss.at[7 + it])
    wait(a_mate, ss.at[10])
    wait(a_x, ss.at[11])
    wait(yb, ss.at[12])
    wait(zb, ss.at[13])
    wait(xf.at[pl.ds(0, 112), pl.ds(0, 256)], ss.at[14])
    wait(xf.at[pl.ds(0, 192), pl.ds(0, 256)], ss.at[15])
    wait(xf.at[pl.ds(0, 192), pl.ds(0, 256)], ss.at[16])
    wait(xf.at[pl.ds(0, 192), :], ss.at[17])
    wait(xf.at[pl.ds(0, 192), :], ss.at[18])
    wait(xf.at[pl.ds(0, 512), :], ss.at[19])


def shards(src_emb, tgt_emb, rotation, src_ids, tgt_ids):
    vmem = pltpu.VMEM
    scratch = [
        vmem((W, 32), BF16),
        vmem((D, W), BF16),
        vmem((W, D), BF16),
        vmem((D, D), BF16),
        vmem((W, D), BF16),
        vmem((W, W), BF16),
        vmem((ITERS, COLS, 1, W), F32),
        vmem((ITERS, ROWS, 1, W), F32),
        vmem((X, 128, W), F32),
        vmem((X, 128, W), BF16),
        vmem((X - 1, 128, W), BF16),
        vmem((2 * X, 128, W), BF16),
        vmem((Y - 1, 128, 256), BF16),
        vmem((Y, 128, 256), BF16),
        vmem((Z - 1, 16, 256), BF16),
        vmem((Z, 16, 256), BF16),
        vmem((D, D), BF16),
        pltpu.SemaphoreType.DMA((3,)),
        pltpu.SemaphoreType.DMA((16,)),
        pltpu.SemaphoreType.DMA((4,)),
        pltpu.SemaphoreType.DMA((20,)),
        pltpu.SemaphoreType.DMA((20,)),
    ]
    hbm = pl.BlockSpec(memory_space=pl.ANY)
    here = pl.BlockSpec(memory_space=pltpu.VMEM)
    return pl.pallas_call(
        body,
        out_shape=jax.ShapeDtypeStruct((4, D), F32),
        in_specs=[hbm, hbm, hbm, here, here],
        out_specs=here,
        scratch_shapes=scratch,
        compiler_params=pltpu.CompilerParams(
            collective_id=0, has_side_effects=True, vmem_limit_bytes=48 * 2**20
        ),
        name="procrustes",
    )(src_emb, tgt_emb, rotation, src_ids.reshape(1, W), tgt_ids.reshape(1, W))


def solution(mesh):
    return jax.shard_map(
        shards,
        mesh=mesh,
        in_specs=(P("row", "col"), P("col", "row"), P(), P("row"), P("col")),
        out_specs=P(("row", "col"), None),
        check_vma=False,
    )
```

```python
import math

import jax
import jax.numpy as jnp
from jax import lax
from jax.experimental import pallas as pl
from jax.experimental.pallas import tpu as pltpu
from jax.sharding import PartitionSpec as P

MESH = pl.DeviceIdType.MESH
F32 = jnp.float32
BF16 = jnp.bfloat16
D = 1024
W = 512
ITERS = 3
X, Y, Z = 4, 4, 8
ROWS, COLS = 2 * X, Y * Z


def hops(step, size):
    return min(step, size - step)


COL_ORDER = sorted(
    ((dy, dz) for dy in range(Y) for dz in range(Z) if dy or dz),
    key=lambda d: -hops(d[0], Y) - hops(d[1], Z))
PLANE_ORDER = sorted(
    ((dx, dk, dy) for dx in range(X) for dk in range(2) for dy in range(Y) if dx or dk or dy),
    key=lambda d: -2 * hops(d[0], X) - 3 * d[1] - 2 * hops(d[2], Y))
ROW_ORDER = [d[:2] for d in PLANE_ORDER if d[2] == 0]
Z_ORDER = (4, 3, 5, 2, 6, 1, 7)
XY_ORDER = (2, 1, 3)
NN = (((1,), (0,)), ((), ()))
NT = (((1,), (1,)), ((), ()))


def dot(a, b, dims):
    return lax.dot_general(a, b, dims, preferred_element_type=F32)


def send(src, dst, send_sem, recv_sem, device):
    pltpu.make_async_remote_copy(
        src_ref=src, dst_ref=dst, send_sem=send_sem, recv_sem=recv_sem,
        device_id=device, device_id_type=MESH,
    ).start()


def wait(ref, sem):
    pltpu.make_async_copy(ref, ref, sem).wait()


def block(i, size):
    return pl.ds(pl.multiple_of(i * size, size), size)


def body(src_hbm, tgt_hbm, rot_hbm, src_ids, tgt_ids, out_ref,
         src_t, tgt, rot, u, kt, ids, colbuf, rowbuf,
         a_mate, a_x, a_out, yb, y_out, zb, z_out, xr, own4, req, rows, c_out, c_in,
         local, zs, xs, ss, rs):
    sent = []

    def finish():
        for ref, sem in sent:
            wait(ref, sem)

    r, c = lax.axis_index("row"), lax.axis_index("col")
    x, core = r // 2, r % 2
    y, z = c // Z, c % Z
    mate = (2 * x + (1 - core), c)

    def xpeer(k):
        return (2 * ((x + k) % X) + core, c)

    def ypeer(k):
        return (r, Z * ((y + k) % Y) + z)

    def zpeer(k):
        return (r, Z * y + (z + k) % Z)

    def colpeer(d):
        return (r, Z * ((y + d[0]) % Y) + (z + d[1]) % Z)

    def rowpeer(d):
        return (2 * ((x + d[0]) % X) + (core + d[1]) % 2, c)

    def planepeer(d):
        return (rowpeer(d)[0], Z * ((y + d[2]) % Y) + z)

    mine = src_t.at[block(c, 32), :]
    load_src = pltpu.make_async_copy(src_hbm, mine, local.at[0])
    load_src.start()
    my_tgt = tgt.at[:, block(r, 128)]
    load_tgt = pltpu.make_async_copy(tgt_hbm, my_tgt, local.at[1])
    load_tgt.start()
    load_rot = pltpu.make_async_copy(rot_hbm, rot, local.at[2])
    load_rot.start()
    load_ids = [pltpu.make_async_copy(ref, ids.at[i], local.at[3 + i]) for i, ref in enumerate((src_ids, tgt_ids))]
    for load in load_ids:
        load.start()
    bar = pltpu.get_barrier_semaphore()

    near = [zpeer(k) for k in Z_ORDER] + [xpeer(k) for k in XY_ORDER] + [ypeer(k) for k in XY_ORDER] + [mate]
    for device in near:
        pl.semaphore_signal(bar, inc=1, device_id=device, device_id_type=MESH)
    load_src.wait()
    load_tgt.wait()
    pl.semaphore_wait(bar, len(near))

    for k in (1, 7, 2, 6, 3, 5, 4):
        send(mine, mine, ss.at[0], zs.at[k], zpeer(k))
    for k in (1, 3, 2):
        send(my_tgt, my_tgt, ss.at[1], xs.at[k], xpeer(k))
        send(mine, mine, ss.at[2], rs.at[2], ypeer(k))
    send(my_tgt, my_tgt, ss.at[3], rs.at[3], mate)
    sent.append((src_t.at[pl.ds(0, 224), :], ss.at[0]))
    sent.append((tgt.at[:, pl.ds(0, 384)], ss.at[1]))
    sent.append((src_t.at[pl.ds(0, 768), :], ss.at[2]))
    sent.append((tgt.at[:, pl.ds(0, 512)], ss.at[3]))

    def forward_src(k):
        got = src_t.at[block(Z * y + (z + Z - k) % Z, 32), :]
        wait(got, zs.at[k])
        for j in (1, 3, 2):
            send(got, got, ss.at[2], rs.at[2], ypeer(j))

    def forward_tgt(k):
        got = tgt.at[:, block(2 * ((x + X - k) % X) + core, 128)]
        wait(got, xs.at[k])
        send(got, got, ss.at[3], rs.at[3], mate)

    forward_src(1)
    forward_src(7)
    forward_tgt(1)
    forward_tgt(3)
    forward_src(2)
    forward_src(6)
    forward_tgt(2)
    forward_src(3)
    forward_src(5)
    forward_src(4)

    wait(tgt.at[:, pl.ds(0, 512)], rs.at[3])
    load_rot.wait()
    tv = tgt[...].astype(F32)
    tsum = jnp.sum(tv * tv, axis=1, keepdims=True)
    tscale = lax.rsqrt(tsum * (1.0 / D) + 1e-06) * (1.0 / math.sqrt(D))
    u[...] = (dot(tgt[...], rot[...], NT) * tscale).astype(BF16)
    tscale_l = jnp.transpose(jnp.broadcast_to(tscale, (W, 128)))[0:1, :]
    for load in load_ids:
        load.wait()
    src_mass = lax.rsqrt(1000.0 + ids[0].astype(F32))
    tgt_mass = lax.rsqrt(1000.0 + ids[1].astype(F32))

    wait(src_t.at[pl.ds(0, 24 * 32), :], rs.at[2])
    sv = src_t[...].astype(F32)
    ssum = jnp.sum(sv * sv, axis=0, keepdims=True)
    sscale = lax.rsqrt(ssum * (1.0 / D) + 1e-06) * (1.0 / math.sqrt(D))
    kt[...] = jnp.exp(dot(u[...], src_t[...], NN) * (sscale * (1.0 / 0.03))).astype(BF16)

    row8 = lax.broadcasted_iota(jnp.int32, (8, W), 0)

    def matvec(v, dims):
        high = v.astype(BF16).astype(F32)
        both = jnp.where(row8 == 0, high, jnp.where(row8 == 1, v - high, 0.0)).astype(BF16)
        return jnp.sum(dot(both, kt[...], dims), axis=0, keepdims=True)

    def sum_col(part, it):
        colbuf[it, c] = part

        for d in COL_ORDER:
            send(colbuf.at[it, c], colbuf.at[it, c], ss.at[4 + it], rs.at[4 + it], colpeer(d))
        sent.append((colbuf.at[it, pl.ds(0, COLS - 1)], ss.at[4 + it]))
        wait(colbuf.at[it, pl.ds(0, COLS - 1)], rs.at[4 + it])
        return jnp.sum(colbuf[it], axis=0)

    def start_row(part, it):
        rowbuf[it, r] = part
        for d in ROW_ORDER:
            send(rowbuf.at[it, r], rowbuf.at[it, r], ss.at[7 + it], rs.at[7 + it], rowpeer(d))
        sent.append((rowbuf.at[it, pl.ds(0, ROWS - 1)], ss.at[7 + it]))

    def end_row(it):
        wait(rowbuf.at[it, pl.ds(0, ROWS - 1)], rs.at[7 + it])
        return jnp.sum(rowbuf[it], axis=0)

    tgt_scale = jnp.ones((1, W), F32)
    for it in range(ITERS):
        src_scale = src_mass / sum_col(matvec(tgt_scale, NN), it)
        start_row(matvec(src_scale, NT), it)
        if it < ITERS - 1:
            tgt_scale = tgt_mass / end_row(it)

    kt[...] = (kt[...].astype(F32) * (src_scale * sscale)).astype(BF16)
    for k in (2, 1, 3, 0):
        a_out[k] = dot(src_t[block(2 * ((x + k) % X) + (1 - core), 128), :], kt[...], NT).astype(BF16)
        send(a_out.at[k], a_mate.at[k], ss.at[10], xs.at[4 + k], mate)
    sent.append((a_mate, ss.at[10]))
    for k in (2, 1, 3, 0):
        half = dot(src_t[block(2 * ((x + k) % X) + core, 128), :], kt[...], NT)
        wait(a_mate.at[k], xs.at[4 + k])
        half = half + a_mate[k].astype(F32)
        if k:
            a_out[X + k] = half.astype(BF16)
            send(a_out.at[X + k], a_x.at[k - 1], ss.at[11], rs.at[11], xpeer(k))
    sent.append((a_x, ss.at[11]))
    tgt_scale = tgt_mass / end_row(ITERS - 1)
    wait(a_x, rs.at[11])
    total = half + ((a_x[0].astype(F32) + a_x[1].astype(F32)) + a_x[2].astype(F32))
    total = (total * (tgt_scale * tscale_l)).astype(BF16)
    to = lax.broadcasted_iota(jnp.int32, (128, 128), 0)
    to = 32 * (to // 4 % 4) + 4 * (to // 16) + to % 4
    order = (lax.broadcasted_iota(jnp.int32, (128, 128), 1) == to).astype(BF16)
    total = dot(order, total, NN).astype(BF16)

    def rows16(i):
        return pl.ds(pl.multiple_of(16 * i, 16), 16)

    cross = dot(total, tgt[...], NN)
    for j in range(Y):
        y_out[j] = cross[:, 256 * j:256 * (j + 1)].astype(BF16)
    for k in Z_ORDER + (0,):
        chunk = rows16((z + k) % Z)
        for j in XY_ORDER:
            send(y_out.at[(y + j) % Y, chunk], yb.at[j - 1, chunk], ss.at[12], zs.at[8 + k], ypeer(j))
    sent.append((yb, ss.at[12]))
    for k in Z_ORDER + (0,):
        chunk = rows16((z + k) % Z)
        wait(yb.at[:, chunk], zs.at[8 + k])
        part = (y_out[y, chunk].astype(F32) + yb[0, chunk].astype(F32)) + (
            yb[1, chunk].astype(F32) + yb[2, chunk].astype(F32))
        if k:
            z_out[k - 1] = part.astype(BF16)
            send(z_out.at[k - 1], zb.at[k - 1], ss.at[13], rs.at[13], zpeer(k))
    sent.append((zb, ss.at[13]))
    wait(zb, rs.at[13])
    own = part + jnp.sum(zb[...].astype(F32), axis=0)

    def cell(i, j):
        return xr.at[rows16(i), block(j, 256)]

    xr[rows16(z), block(y, 256)] = own.astype(BF16)
    for k in Z_ORDER:
        send(cell(z, y), cell(z, y), ss.at[14], zs.at[16 + k], zpeer(k))
    sent.append((xr.at[pl.ds(0, 112), pl.ds(0, 256)], ss.at[14]))
    for j in range(Y):
        own4[j] = own[4 * j:4 * (j + 1)]
    for d in PLANE_ORDER:
        send(own4.at[(y + d[2]) % Y], req.at[Y * r + y], ss.at[15], rs.at[15], planepeer(d))
    sent.append((req.at[pl.ds(0, ROWS * Y - 1)], ss.at[15]))
    req[Y * r + y] = own4[y]
    for j in XY_ORDER:
        send(cell(z, y), cell(z, y), ss.at[16], rs.at[16], ypeer(j))
    for k in (1, 7, 2, 6, 3, 5, 4):
        got = cell((z + Z - k) % Z, y)
        wait(got, zs.at[16 + k])
        for j in XY_ORDER:
            send(got, got, ss.at[16], rs.at[16], ypeer(j))
    sent.append((xr.at[pl.ds(0, 96), :], ss.at[16]))
    wait(req.at[pl.ds(0, ROWS * Y - 1)], rs.at[15])
    for i in range(ROWS):
        for j in range(Y):
            rows[4 * i:4 * (i + 1), 256 * j:256 * (j + 1)] = req[Y * i + j]
    wait(xr.at[pl.ds(0, 96), :], rs.at[16])

    xv = xr[...].astype(F32)
    square = jnp.sum(jnp.sum(xv * xv, axis=0, keepdims=True), axis=1, keepdims=True)
    gram = dot(rows[...].astype(BF16), xr[...], NT) * (1.0 / (square * (1.0 / (128 * D)) + 1e-30))
    cubic = dot(gram.astype(BF16), xr[...], NN)
    for i in range(ROWS):
        c_out[i, :, 0:D] = cubic[4 * i:4 * (i + 1)]
        c_out[i, :, D:] = jnp.broadcast_to(square, (4, 128))
    for d in ROW_ORDER:
        peer = rowpeer(d)
        send(c_out.at[peer[0]], c_in.at[r], ss.at[17], rs.at[17], peer)
    sent.append((c_in.at[pl.ds(0, ROWS - 1)], ss.at[17]))
    c_in[r] = c_out[r]
    linear = jnp.concatenate([req[Y * r + j] for j in range(Y)], axis=1)
    wait(c_in.at[pl.ds(0, ROWS - 1)], rs.at[17])
    squares = [c_in[i, 0:1, D:D + 1] for i in range(ROWS)]
    mean = sum(squares) * (1.0 / (D * D)) + 1e-30
    inverse = 1.0 / (mean * (4.0 * D))
    cubic = sum(
        c_in[i, :, 0:D] * ((squares[i] * (1.0 / (128 * D)) + 1e-30) * inverse) for i in range(ROWS))
    scale = lax.rsqrt(mean) * (1.0 / (2.0 * math.sqrt(D)))
    out_ref[...] = (math.sqrt(D) * scale) * (1.5 * linear - 0.5 * cubic)
    finish()


def shards(src_emb, tgt_emb, rotation, src_ids, tgt_ids):
    vmem = pltpu.VMEM
    scratch = [
        vmem((D, W), BF16),
        vmem((W, D), BF16),
        vmem((D, D), BF16),
        vmem((W, D), BF16),
        vmem((W, W), BF16),
        vmem((2, 1, W), jnp.int32),
        vmem((ITERS, COLS, 1, W), F32),
        vmem((ITERS, ROWS, 1, W), F32),
        vmem((X, 128, W), BF16),
        vmem((X - 1, 128, W), BF16),
        vmem((2 * X, 128, W), BF16),
        vmem((Y - 1, 128, 256), BF16),
        vmem((Y, 128, 256), BF16),
        vmem((Z - 1, 16, 256), BF16),
        vmem((Z - 1, 16, 256), BF16),
        vmem((128, D), BF16),
        vmem((Y, 4, 256), F32),
        vmem((ROWS * Y, 4, 256), F32),
        vmem((32, D), F32),
        vmem((ROWS, 4, D + 128), F32),
        vmem((ROWS, 4, D + 128), F32),
        pltpu.SemaphoreType.DMA((5,)),
        pltpu.SemaphoreType.DMA((24,)),
        pltpu.SemaphoreType.DMA((8,)),
        pltpu.SemaphoreType.DMA((18,)),
        pltpu.SemaphoreType.DMA((18,)),
    ]
    hbm = pl.BlockSpec(memory_space=pltpu.HBM)
    here = pl.BlockSpec(memory_space=pltpu.VMEM)
    return pl.pallas_call(
        body,
        out_shape=jax.ShapeDtypeStruct((4, D), F32),
        in_specs=[hbm] * 5,
        out_specs=here,
        scratch_shapes=scratch,
        compiler_params=pltpu.CompilerParams(
            collective_id=0, has_side_effects=True, vmem_limit_bytes=63 * 2**20
        ),
        name="procrustes",
    )(src_emb.T, tgt_emb, rotation, src_ids.reshape(1, W), tgt_ids.reshape(1, W))


def solution(mesh):
    return jax.shard_map(
        shards,
        mesh=mesh,
        in_specs=(P("row", "col"), P("col", "row"), P(), P("row"), P("col")),
        out_specs=P(("row", "col"), None),
        check_vma=False,
    )
```

```python
import math

import jax
import jax.numpy as jnp
from jax import lax
from jax.experimental import pallas as pl
from jax.experimental.pallas import tpu as pltpu
from jax.sharding import PartitionSpec as P

MESH = pl.DeviceIdType.MESH
F32 = jnp.float32
BF16 = jnp.bfloat16
D = 1024
W = 512
ITERS = 3
X, Y, Z = 4, 4, 8
ROWS, COLS = 2 * X, Y * Z


def hops(step, size):
    return min(step, size - step)


COL_ORDER = sorted(
    ((dy, dz) for dy in range(Y) for dz in range(Z) if dy or dz),
    key=lambda d: -hops(d[0], Y) - hops(d[1], Z))
PLANE_ORDER = sorted(
    ((dx, dk, dy) for dx in range(X) for dk in range(2) for dy in range(Y) if dx or dk or dy),
    key=lambda d: -2 * hops(d[0], X) - 3 * d[1] - 2 * hops(d[2], Y))
ROW_ORDER = [d[:2] for d in PLANE_ORDER if d[2] == 0]
Z_ORDER = (4, 3, 5, 2, 6, 1, 7)
Z_NEAR = (0, 1, 7, 2, 6, 3, 5, 4)
UP, DOWN = (0, 7, 6), (1, 2)
XY_ORDER = (2, 1, 3)
NN = (((1,), (0,)), ((), ()))
NT = (((1,), (1,)), ((), ()))


def dot(a, b, dims):
    return lax.dot_general(a, b, dims, preferred_element_type=F32)


def send(src, dst, send_sem, recv_sem, device):
    pltpu.make_async_remote_copy(
        src_ref=src, dst_ref=dst, send_sem=send_sem, recv_sem=recv_sem,
        device_id=device, device_id_type=MESH,
    ).start()


def wait(ref, sem):
    pltpu.make_async_copy(ref, ref, sem).wait()


def block(i, size):
    return pl.ds(pl.multiple_of(i * size, size), size)


def body(src_hbm, tgt_hbm, rot_hbm, src_ids, tgt_ids, out_ref,
         src_t, ordered, tgt, rot, u, kt, ids, colbuf, rowbuf,
         a_mate, a_x, a_out, yb, y_out, y_mine, zb, z_out, xr, own4, req, rows, c_out, c_in,
         local, zs, xs, ss, rs):
    sent = []

    def finish():
        for ref, sem in sent:
            wait(ref, sem)

    r, c = lax.axis_index("row"), lax.axis_index("col")
    x, core = r // 2, r % 2
    y, z = c // Z, c % Z
    mate = (2 * x + (1 - core), c)

    def xpeer(k):
        return (2 * ((x + k) % X) + core, c)

    def ypeer(k):
        return (r, Z * ((y + k) % Y) + z)

    def zpeer(k):
        return (r, Z * y + (z + k) % Z)

    def colpeer(d):
        return (r, Z * ((y + d[0]) % Y) + (z + d[1]) % Z)

    def rowpeer(d):
        return (2 * ((x + d[0]) % X) + (core + d[1]) % 2, c)

    def planepeer(d):
        return (rowpeer(d)[0], Z * ((y + d[2]) % Y) + z)

    def feature(i, j):
        return pl.ds(pl.multiple_of(128 * i + 32 * j, 32), 32)

    mine = src_t.at[feature(z, y)]
    load_src = pltpu.make_async_copy(src_hbm, mine, local.at[0])
    load_src.start()
    my_tgt = tgt.at[:, block(r, 128)]
    load_tgt = pltpu.make_async_copy(tgt_hbm, my_tgt, local.at[1])
    load_tgt.start()
    for i in range(Z):
        for j in range(Y):
            pltpu.make_async_copy(
                rot_hbm.at[pl.ds(32 * (Z * j + i), 32)], rot.at[pl.ds(128 * i + 32 * j, 32)], local.at[2]).start()
    load_ids = [pltpu.make_async_copy(ref, ids.at[i], local.at[3 + i]) for i, ref in enumerate((src_ids, tgt_ids))]
    for load in load_ids:
        load.start()
    bar = pltpu.get_barrier_semaphore()

    near = [zpeer(k) for k in Z_ORDER] + [xpeer(k) for k in XY_ORDER] + [ypeer(k) for k in XY_ORDER] + [mate]
    for device in near:
        pl.semaphore_signal(bar, inc=1, device_id=device, device_id_type=MESH)
    load_src.wait()
    load_tgt.wait()
    pl.semaphore_wait(bar, len(near))

    def over_y(k):
        got = src_t.at[feature((z + Z - k) % Z, y)]
        passed = zs.at[24 + k]
        rest = zs.at[32 + k]
        send(got, got, ss.at[2], passed if k in UP else rest, ypeer(1))
        send(got, got, ss.at[2], passed if k in DOWN else rest, ypeer(3))
        if k not in UP + DOWN:
            send(got, got, ss.at[2], rest, ypeer(2))

    def forward_src(k):
        wait(mine, zs.at[k])
        over_y(k)

    def pass_on(k):
        step = 1 if k in UP else 3
        got = src_t.at[feature((z + Z - k) % Z, (y + Y - step) % Y)]
        wait(got, zs.at[24 + k])
        send(got, got, ss.at[2], zs.at[32 + k], ypeer(step))

    for k in (1, 7):
        send(mine, mine, ss.at[0], zs.at[k], zpeer(k))
    over_y(0)
    for k in (1, 3, 2):
        send(my_tgt, my_tgt, ss.at[1], xs.at[k], xpeer(k))
    for k in (2, 6, 3, 5, 4):
        send(mine, mine, ss.at[0], zs.at[k], zpeer(k))
    send(my_tgt, my_tgt, ss.at[3], rs.at[3], mate)
    sent.append((src_t.at[pl.ds(0, 224), :], ss.at[0]))
    sent.append((tgt.at[:, pl.ds(0, 384)], ss.at[1]))
    sent.append((src_t.at[pl.ds(0, 768), :], ss.at[2]))
    sent.append((tgt.at[:, pl.ds(0, 512)], ss.at[3]))

    def forward_tgt(k):
        got = tgt.at[:, block(2 * ((x + X - k) % X) + core, 128)]
        wait(got, xs.at[k])
        send(got, got, ss.at[3], rs.at[3], mate)

    forward_src(1)
    forward_src(7)
    pass_on(0)
    forward_tgt(1)
    forward_tgt(3)
    forward_src(2)
    forward_src(6)
    pass_on(1)
    pass_on(7)
    forward_tgt(2)
    forward_src(3)
    forward_src(5)
    pass_on(2)
    pass_on(6)
    forward_src(4)

    wait(tgt.at[:, pl.ds(0, 512)], rs.at[3])
    wait(rot, local.at[2])
    tv = tgt[...].astype(F32)
    tsum = jnp.sum(tv * tv, axis=1, keepdims=True)
    tscale = lax.rsqrt(tsum * (1.0 / D) + 1e-06) * (1.0 / math.sqrt(D))
    u[...] = (dot(tgt[...], rot[...], NT) * tscale).astype(BF16)
    for load in load_ids:
        load.wait()
    logits = jnp.zeros((W, W), F32)
    square = jnp.zeros((1, W), F32)
    for k in Z_NEAR:
        i = (z + Z - k) % Z
        here = src_t.at[block(i, 128)]
        wait(src_t.at[pl.ds(0, 64 if k in UP + DOWN else 96)], zs.at[32 + k])
        part = here[...]
        logits = logits + dot(u[:, block(i, 128)], part, NN)
        part = part.astype(F32)
        square = square + jnp.sum(part * part, axis=0, keepdims=True)
    sscale = lax.rsqrt(square * (1.0 / D) + 1e-06) * (1.0 / math.sqrt(D))
    kt[...] = jnp.exp(logits * (sscale * (1.0 / 0.03))).astype(BF16)

    row8 = lax.broadcasted_iota(jnp.int32, (8, W), 0)

    def matvec(v, dims):
        high = v.astype(BF16).astype(F32)
        both = jnp.where(row8 == 0, high, jnp.where(row8 == 1, v - high, 0.0)).astype(BF16)
        return jnp.sum(dot(both, kt[...], dims), axis=0, keepdims=True)

    def meanwhile():
        to = lax.broadcasted_iota(jnp.int32, (128, 128), 0)
        to = 32 * (to // 4 % 4) + 4 * (to // 16) + to % 4
        order = (lax.broadcasted_iota(jnp.int32, (128, 128), 1) == to).astype(BF16)
        for i in range(ROWS):
            natural = [src_t[128 * j + 32 * (i // 2):128 * j + 32 * (i // 2) + 32]
                       for j in range(4 * (i % 2), 4 * (i % 2) + 4)]
            ordered[i] = dot(order, jnp.concatenate(natural, axis=0), NN).astype(BF16)

    def sum_col(part, it):
        colbuf[it, c] = part

        for d in COL_ORDER:
            send(colbuf.at[it, c], colbuf.at[it, c], ss.at[4 + it], rs.at[4 + it], colpeer(d))
        sent.append((colbuf.at[it, pl.ds(0, COLS - 1)], ss.at[4 + it]))
        if it == 0:
            meanwhile()
        wait(colbuf.at[it, pl.ds(0, COLS - 1)], rs.at[4 + it])
        return jnp.sum(colbuf[it], axis=0)

    def start_row(part, it):
        rowbuf[it, r] = part
        for d in ROW_ORDER:
            send(rowbuf.at[it, r], rowbuf.at[it, r], ss.at[7 + it], rs.at[7 + it], rowpeer(d))
        sent.append((rowbuf.at[it, pl.ds(0, ROWS - 1)], ss.at[7 + it]))

    def end_row(it):
        wait(rowbuf.at[it, pl.ds(0, ROWS - 1)], rs.at[7 + it])
        return jnp.sum(rowbuf[it], axis=0)

    src_mass = lax.rsqrt(1000.0 + ids[0].astype(F32))
    tgt_mass = lax.rsqrt(1000.0 + ids[1].astype(F32))
    tgt_scale = jnp.ones((1, W), F32)
    for it in range(ITERS):
        src_scale = src_mass / sum_col(matvec(tgt_scale, NN), it)
        if it < ITERS - 1:
            start_row(matvec(src_scale, NT), it)
            tgt_scale = tgt_mass / end_row(it)

    plan = (kt[...].astype(F32) * (src_scale * sscale)).astype(BF16)
    for k in (2, 1, 3, 0):
        a_out[k] = dot(ordered[2 * ((x + k) % X) + (1 - core)], plan, NT).astype(BF16)
        send(a_out.at[k], a_mate.at[k], ss.at[10], xs.at[4 + k], mate)
    sent.append((a_mate, ss.at[10]))
    for k in (2, 1, 3, 0):
        half = dot(ordered[2 * ((x + k) % X) + core], plan, NT)
        wait(a_mate.at[k], xs.at[4 + k])
        half = half + a_mate[k].astype(F32)
        if k:
            a_out[X + k] = half.astype(BF16)
            send(a_out.at[X + k], a_x.at[k - 1], ss.at[11], rs.at[11], xpeer(k))
    sent.append((a_x, ss.at[11]))
    start_row(matvec(src_scale, NT), ITERS - 1)
    tscale_l = jnp.transpose(jnp.broadcast_to(tscale, (W, 128)))[0:1, :]
    tgt_scale = tgt_mass / end_row(ITERS - 1)
    wait(a_x, rs.at[11])
    total = half + ((a_x[0].astype(F32) + a_x[1].astype(F32)) + a_x[2].astype(F32))
    total = (total * (tgt_scale * tscale_l)).astype(BF16)

    def rows16(i):
        return pl.ds(pl.multiple_of(16 * i, 16), 16)

    for j in XY_ORDER:
        y_out[j - 1] = dot(total, tgt[:, block((y + j) % Y, 256)], NN).astype(BF16)
        for k in Z_ORDER + (0,):
            chunk = rows16((z + k) % Z)
            send(y_out.at[j - 1, chunk], yb.at[j - 1, chunk], ss.at[12], zs.at[8 + k], ypeer(j))
    y_mine[...] = dot(total, tgt[:, block(y, 256)], NN)
    sent.append((yb, ss.at[12]))
    for k in Z_ORDER + (0,):
        chunk = rows16((z + k) % Z)
        wait(yb.at[:, chunk], zs.at[8 + k])
        part = (y_mine[chunk] + yb[0, chunk].astype(F32)) + (
            yb[1, chunk].astype(F32) + yb[2, chunk].astype(F32))
        if k:
            z_out[k - 1] = part.astype(BF16)
            send(z_out.at[k - 1], zb.at[k - 1], ss.at[13], rs.at[13], zpeer(k))
    sent.append((zb, ss.at[13]))
    wait(zb, rs.at[13])
    own = part + jnp.sum(zb[...].astype(F32), axis=0)

    def cell(i, j):
        return xr.at[rows16(i), block(j, 256)]

    xr[rows16(z), block(y, 256)] = own.astype(BF16)
    for k in Z_ORDER:
        send(cell(z, y), cell(z, y), ss.at[14], zs.at[16 + k], zpeer(k))
    sent.append((xr.at[pl.ds(0, 112), pl.ds(0, 256)], ss.at[14]))
    for j in range(Y):
        own4[j] = own[4 * j:4 * (j + 1)]
    for d in PLANE_ORDER:
        send(own4.at[(y + d[2]) % Y], req.at[Y * r + y], ss.at[15], rs.at[15], planepeer(d))
    sent.append((req.at[pl.ds(0, ROWS * Y - 1)], ss.at[15]))
    req[Y * r + y] = own4[y]
    for j in XY_ORDER:
        send(cell(z, y), cell(z, y), ss.at[16], rs.at[16], ypeer(j))
    for k in (1, 7, 2, 6, 3, 5, 4):
        got = cell((z + Z - k) % Z, y)
        wait(got, zs.at[16 + k])
        for j in XY_ORDER:
            send(got, got, ss.at[16], rs.at[16], ypeer(j))
    sent.append((xr.at[pl.ds(0, 96), :], ss.at[16]))
    wait(req.at[pl.ds(0, ROWS * Y - 1)], rs.at[15])
    for i in range(ROWS):
        for j in range(Y):
            rows[4 * i:4 * (i + 1), 256 * j:256 * (j + 1)] = req[Y * i + j]
    wait(xr.at[pl.ds(0, 96), :], rs.at[16])

    xv = xr[...].astype(F32)
    square = jnp.sum(jnp.sum(xv * xv, axis=0, keepdims=True), axis=1, keepdims=True)
    gram = dot(rows[...].astype(BF16), xr[...], NT) * (1.0 / (square * (1.0 / (128 * D)) + 1e-30))
    cubic = dot(gram.astype(BF16), xr[...], NN)
    for i in range(ROWS):
        c_out[i, :, 0:D] = cubic[4 * i:4 * (i + 1)]
        c_out[i, :, D:] = jnp.broadcast_to(square, (4, 128))
    for d in ROW_ORDER:
        peer = rowpeer(d)
        send(c_out.at[peer[0]], c_in.at[r], ss.at[17], rs.at[17], peer)
    sent.append((c_in.at[pl.ds(0, ROWS - 1)], ss.at[17]))
    c_in[r] = c_out[r]
    linear = jnp.concatenate([req[Y * r + j] for j in range(Y)], axis=1)
    wait(c_in.at[pl.ds(0, ROWS - 1)], rs.at[17])
    squares = [c_in[i, 0:1, D:D + 1] for i in range(ROWS)]
    mean = sum(squares) * (1.0 / (D * D)) + 1e-30
    inverse = 1.0 / (mean * (4.0 * D))
    cubic = sum(
        c_in[i, :, 0:D] * ((squares[i] * (1.0 / (128 * D)) + 1e-30) * inverse) for i in range(ROWS))
    scale = lax.rsqrt(mean) * (1.0 / (2.0 * math.sqrt(D)))
    out_ref[...] = (math.sqrt(D) * scale) * (1.5 * linear - 0.5 * cubic)
    finish()


def shards(src_emb, tgt_emb, rotation, src_ids, tgt_ids):
    vmem = pltpu.VMEM
    scratch = [
        vmem((D, W), BF16),
        vmem((ROWS, 128, W), BF16),
        vmem((W, D), BF16),
        vmem((D, D), BF16),
        vmem((W, D), BF16),
        vmem((W, W), BF16),
        vmem((2, 1, W), jnp.int32),
        vmem((ITERS, COLS, 1, W), F32),
        vmem((ITERS, ROWS, 1, W), F32),
        vmem((X, 128, W), BF16),
        vmem((X - 1, 128, W), BF16),
        vmem((2 * X, 128, W), BF16),
        vmem((Y - 1, 128, 256), BF16),
        vmem((Y - 1, 128, 256), BF16),
        vmem((128, 256), F32),
        vmem((Z - 1, 16, 256), BF16),
        vmem((Z - 1, 16, 256), BF16),
        vmem((128, D), BF16),
        vmem((Y, 4, 256), F32),
        vmem((ROWS * Y, 4, 256), F32),
        vmem((32, D), F32),
        vmem((ROWS, 4, D + 128), F32),
        vmem((ROWS, 4, D + 128), F32),
        pltpu.SemaphoreType.DMA((5,)),
        pltpu.SemaphoreType.DMA((40,)),
        pltpu.SemaphoreType.DMA((8,)),
        pltpu.SemaphoreType.DMA((18,)),
        pltpu.SemaphoreType.DMA((18,)),
    ]
    hbm = pl.BlockSpec(memory_space=pltpu.HBM)
    here = pl.BlockSpec(memory_space=pltpu.VMEM)
    return pl.pallas_call(
        body,
        out_shape=jax.ShapeDtypeStruct((4, D), F32),
        in_specs=[hbm] * 5,
        out_specs=here,
        scratch_shapes=scratch,
        compiler_params=pltpu.CompilerParams(
            collective_id=0, has_side_effects=True, vmem_limit_bytes=63 * 2**20
        ),
        name="procrustes",
    )(src_emb.T, tgt_emb, rotation, src_ids.reshape(1, W), tgt_ids.reshape(1, W))


def solution(mesh):
    return jax.shard_map(
        shards,
        mesh=mesh,
        in_specs=(P("row", "col"), P("col", "row"), P(), P("row"), P("col")),
        out_specs=P(("row", "col"), None),
        check_vma=False,
    )
```

```python
import math

import jax
import jax.numpy as jnp
from jax import lax
from jax.experimental import pallas as pl
from jax.experimental.pallas import tpu as pltpu
from jax.sharding import PartitionSpec as P

MESH = pl.DeviceIdType.MESH
F32 = jnp.float32
BF16 = jnp.bfloat16
D = 1024
W = 512
ITERS = 3
X, Y, Z = 4, 4, 8
ROWS, COLS = 2 * X, Y * Z


def hops(step, size):
    return min(step, size - step)


COL_ORDER = sorted(
    ((dy, dz) for dy in range(Y) for dz in range(Z) if dy or dz),
    key=lambda d: -hops(d[0], Y) - hops(d[1], Z))
PLANE_ORDER = sorted(
    ((dx, dk, dy) for dx in range(X) for dk in range(2) for dy in range(Y) if dx or dk or dy),
    key=lambda d: -2 * hops(d[0], X) - 3 * d[1] - 2 * hops(d[2], Y))
ROW_ORDER = [d[:2] for d in PLANE_ORDER if d[2] == 0]
Z_ORDER = (4, 3, 5, 2, 6, 1, 7)
Z_NEAR = (0, 1, 7, 2, 6, 3, 5, 4)
PARTS = 2
ROWS_IN = 128 // PARTS
CHUNKS = Z // PARTS
XY_ORDER = (2, 1, 3)
NN = (((1,), (0,)), ((), ()))
NT = (((1,), (1,)), ((), ()))


def dot(a, b, dims):
    return lax.dot_general(a, b, dims, preferred_element_type=F32)


def send(src, dst, send_sem, recv_sem, device):
    pltpu.make_async_remote_copy(
        src_ref=src, dst_ref=dst, send_sem=send_sem, recv_sem=recv_sem,
        device_id=device, device_id_type=MESH,
    ).start()


def wait(ref, sem):
    pltpu.make_async_copy(ref, ref, sem).wait()


def block(i, size):
    return pl.ds(pl.multiple_of(i * size, size), size)


def body(src_hbm, tgt_hbm, rot_hbm, src_ids, tgt_ids, out_ref,
         src_t, ordered, tgt, rot, u, kt, ids, colbuf, rowbuf,
         a_mate, a_out, a_x, x_out, yb, y_out, y_mine, zb, z_out, xr, own4, req, rows, c_out, c_in,
         local, zs, xs, ss, rs):
    sent = []

    def finish():
        for ref, sem in sent:
            wait(ref, sem)

    r, c = lax.axis_index("row"), lax.axis_index("col")
    x, core = r // 2, r % 2
    y, z = c // Z, c % Z
    mate = (2 * x + (1 - core), c)

    def xpeer(k):
        return (2 * ((x + k) % X) + core, c)

    def ypeer(k):
        return (r, Z * ((y + k) % Y) + z)

    def zpeer(k):
        return (r, Z * y + (z + k) % Z)

    def colpeer(d):
        return (r, Z * ((y + d[0]) % Y) + (z + d[1]) % Z)

    def rowpeer(d):
        return (2 * ((x + d[0]) % X) + (core + d[1]) % 2, c)

    def planepeer(d):
        return (rowpeer(d)[0], Z * ((y + d[2]) % Y) + z)

    def feature(i, j):
        return pl.ds(pl.multiple_of(128 * i + 32 * j, 32), 32)

    mine = src_t.at[feature(z, y)]
    load_src = pltpu.make_async_copy(src_hbm, mine, local.at[0])
    load_src.start()
    my_tgt = tgt.at[:, block(r, 128)]
    load_tgt = pltpu.make_async_copy(tgt_hbm, my_tgt, local.at[1])
    load_tgt.start()
    for i in range(Z):
        for j in range(Y):
            pltpu.make_async_copy(
                rot_hbm.at[pl.ds(32 * (Z * j + i), 32)], rot.at[pl.ds(128 * i + 32 * j, 32)], local.at[2]).start()
    load_ids = [pltpu.make_async_copy(ref, ids.at[i], local.at[3 + i]) for i, ref in enumerate((src_ids, tgt_ids))]
    for load in load_ids:
        load.start()
    bar = pltpu.get_barrier_semaphore()

    near = [zpeer(k) for k in Z_ORDER] + [xpeer(k) for k in XY_ORDER] + [ypeer(k) for k in XY_ORDER] + [mate]
    for device in near:
        pl.semaphore_signal(bar, inc=1, device_id=device, device_id_type=MESH)
    load_src.wait()
    load_tgt.wait()
    pl.semaphore_wait(bar, len(near))

    def over_y(k):
        got = src_t.at[feature((z + Z - k) % Z, y)]
        wait(mine, zs.at[k])
        for j in (1, 3, 2):
            send(got, got, ss.at[2], zs.at[32 + k], ypeer(j))

    def over_z(j):
        got = src_t.at[feature(z, (y + Y - j) % Y)]
        wait(got, zs.at[24 + j])
        for k in (1, 7):
            send(got, got, ss.at[0], zs.at[32 + k], zpeer(k))

    for j in (1, 3, 2):
        send(mine, mine, ss.at[2], zs.at[24 + j], ypeer(j))
    for k in (2, 6, 3, 5, 4, 1, 7):
        send(mine, mine, ss.at[0], zs.at[k], zpeer(k))
    for k in (1, 3, 2):
        send(my_tgt, my_tgt, ss.at[1], xs.at[k], xpeer(k))
    send(my_tgt, my_tgt, ss.at[3], rs.at[3], mate)
    sent.append((src_t.at[pl.ds(0, 13 * 32), :], ss.at[0]))
    sent.append((tgt.at[:, pl.ds(0, 384)], ss.at[1]))
    sent.append((src_t.at[pl.ds(0, 18 * 32), :], ss.at[2]))
    sent.append((tgt.at[:, pl.ds(0, 512)], ss.at[3]))

    def forward_tgt(k):
        got = tgt.at[:, block(2 * ((x + X - k) % X) + core, 128)]
        wait(got, xs.at[k])
        send(got, got, ss.at[3], rs.at[3], mate)

    over_z(1)
    over_z(3)
    over_y(2)
    over_y(6)
    over_z(2)
    forward_tgt(1)
    forward_tgt(3)
    over_y(3)
    over_y(5)
    forward_tgt(2)
    over_y(4)

    wait(tgt.at[:, pl.ds(0, 512)], rs.at[3])
    wait(rot, local.at[2])
    tv = tgt[...].astype(F32)
    tsum = jnp.sum(tv * tv, axis=1, keepdims=True)
    tscale = lax.rsqrt(tsum * (1.0 / D) + 1e-06) * (1.0 / math.sqrt(D))
    u[...] = (dot(tgt[...], rot[...], NT) * tscale).astype(BF16)
    for load in load_ids:
        load.wait()
    logits = jnp.zeros((W, W), F32)
    square = jnp.zeros((1, W), F32)
    for k in Z_NEAR:
        i = (z + Z - k) % Z
        here = src_t.at[block(i, 128)]
        if k in (1, 7):
            wait(mine, zs.at[k])
        if k:
            wait(src_t.at[pl.ds(0, 96)], zs.at[32 + k])
        part = here[...]
        logits = logits + dot(u[:, block(i, 128)], part, NN)
        part = part.astype(F32)
        square = square + jnp.sum(part * part, axis=0, keepdims=True)
    sscale = lax.rsqrt(square * (1.0 / D) + 1e-06) * (1.0 / math.sqrt(D))
    kt[...] = jnp.exp(logits * (sscale * (1.0 / 0.03))).astype(BF16)

    row8 = lax.broadcasted_iota(jnp.int32, (8, W), 0)

    def matvec(v, dims):
        high = v.astype(BF16).astype(F32)
        both = jnp.where(row8 == 0, high, jnp.where(row8 == 1, v - high, 0.0)).astype(BF16)
        return jnp.sum(dot(both, kt[...], dims), axis=0, keepdims=True)

    def meanwhile():
        at = lax.broadcasted_iota(jnp.int32, (128, 128), 0)
        step = jnp.zeros((128, 128), jnp.int32)
        for i, k in enumerate(Z_ORDER):
            step = jnp.where(at // 16 == i, k, step)
        to = 32 * (at // 4 % 4) + 4 * ((z + step) % Z) + at % 4
        order = (lax.broadcasted_iota(jnp.int32, (128, 128), 1) == to).astype(BF16)
        for i in range(ROWS):
            natural = [src_t[128 * j + 32 * (i // 2):128 * j + 32 * (i // 2) + 32]
                       for j in range(4 * (i % 2), 4 * (i % 2) + 4)]
            ordered[i] = dot(order, jnp.concatenate(natural, axis=0), NN).astype(BF16)

    def sum_col(part, it):
        colbuf[it, c] = part

        for d in COL_ORDER:
            send(colbuf.at[it, c], colbuf.at[it, c], ss.at[4 + it], rs.at[4 + it], colpeer(d))
        sent.append((colbuf.at[it, pl.ds(0, COLS - 1)], ss.at[4 + it]))
        if it == 0:
            meanwhile()
        wait(colbuf.at[it, pl.ds(0, COLS - 1)], rs.at[4 + it])
        return jnp.sum(colbuf[it], axis=0)

    def start_row(part, it):
        rowbuf[it, r] = part
        for d in ROW_ORDER:
            send(rowbuf.at[it, r], rowbuf.at[it, r], ss.at[7 + it], rs.at[7 + it], rowpeer(d))
        sent.append((rowbuf.at[it, pl.ds(0, ROWS - 1)], ss.at[7 + it]))

    def end_row(it):
        wait(rowbuf.at[it, pl.ds(0, ROWS - 1)], rs.at[7 + it])
        return jnp.sum(rowbuf[it], axis=0)

    src_mass = lax.rsqrt(1000.0 + ids[0].astype(F32))
    tgt_mass = lax.rsqrt(1000.0 + ids[1].astype(F32))
    tgt_scale = jnp.ones((1, W), F32)
    for it in range(ITERS):
        src_scale = src_mass / sum_col(matvec(tgt_scale, NN), it)
        if it < ITERS - 1:
            start_row(matvec(src_scale, NT), it)
            tgt_scale = tgt_mass / end_row(it)

    plan = (kt[...].astype(F32) * (src_scale * sscale)).astype(BF16)
    def some_rows(k, h):
        first = pl.ds(ROWS_IN * h, ROWS_IN)
        return jnp.concatenate([ordered[2 * ((x + j) % X) + k, first] for j in range(X)], axis=0)

    for h in range(PARTS):
        a_out[h] = dot(some_rows(1 - core, h), plan, NT).astype(BF16)
        send(a_out.at[h], a_mate.at[h], ss.at[10], xs.at[4 + h], mate)
    sent.append((a_mate, ss.at[10]))
    start_row(matvec(src_scale, NT), ITERS - 1)
    tscale_l = jnp.transpose(jnp.broadcast_to(tscale, (W, 128)))[0:1, :]
    kept = []
    for h in range(PARTS):
        half = dot(some_rows(core, h), plan, NT)
        wait(a_mate.at[h], xs.at[4 + h])
        half = half + a_mate[h].astype(F32)
        kept.append(half[0:ROWS_IN])
        for k in (2, 1, 3):
            x_out[h, k - 1] = half[ROWS_IN * k:ROWS_IN * (k + 1)].astype(BF16)
            send(x_out.at[h, k - 1], a_x.at[h, k - 1], ss.at[11], xs.at[8 + h], xpeer(k))
    sent.append((a_x, ss.at[11]))
    factor = (tgt_mass / end_row(ITERS - 1)) * tscale_l

    for h in range(PARTS):
        wait(a_x.at[h], xs.at[8 + h])
        total = kept[h] + ((a_x[h, 0].astype(F32) + a_x[h, 1].astype(F32)) + a_x[h, 2].astype(F32))
        total = (total * factor).astype(BF16)
        for j in XY_ORDER:
            y_out[h, j - 1] = dot(total, tgt[:, block((y + j) % Y, 256)], NN).astype(BF16)
            send(y_out.at[h, j - 1], yb.at[h, j - 1], ss.at[12], xs.at[12 + h], ypeer(j))
        y_mine[h] = dot(total, tgt[:, block(y, 256)], NN)
    sent.append((yb, ss.at[12]))
    for h in range(PARTS):
        wait(yb.at[h], xs.at[12 + h])
        part = (y_mine[h] + yb[h, 0].astype(F32)) + (yb[h, 1].astype(F32) + yb[h, 2].astype(F32))
        for i in range(CHUNKS):
            own = part[16 * i:16 * (i + 1)]
            k = (Z_ORDER + (0,))[CHUNKS * h + i]
            if k:
                z_out[k - 1] = own.astype(BF16)
                send(z_out.at[k - 1], zb.at[k - 1], ss.at[13], rs.at[13], zpeer(k))
    sent.append((zb, ss.at[13]))
    wait(zb, rs.at[13])
    own = own + jnp.sum(zb[...].astype(F32), axis=0)

    def cell(i, j):
        return xr.at[block(i, 16), block(j, 256)]

    xr[block(z, 16), block(y, 256)] = own.astype(BF16)
    for k in Z_ORDER:
        send(cell(z, y), cell(z, y), ss.at[14], zs.at[16 + k], zpeer(k))
    sent.append((xr.at[pl.ds(0, 112), pl.ds(0, 256)], ss.at[14]))
    for j in range(Y):
        own4[j] = own[4 * j:4 * (j + 1)]
    for d in PLANE_ORDER:
        send(own4.at[(y + d[2]) % Y], req.at[Y * r + y], ss.at[15], rs.at[15], planepeer(d))
    sent.append((req.at[pl.ds(0, ROWS * Y - 1)], ss.at[15]))
    req[Y * r + y] = own4[y]
    for j in XY_ORDER:
        send(cell(z, y), cell(z, y), ss.at[16], rs.at[16], ypeer(j))
    for k in (1, 7, 2, 6, 3, 5, 4):
        got = cell((z + Z - k) % Z, y)
        wait(got, zs.at[16 + k])
        for j in XY_ORDER:
            send(got, got, ss.at[16], rs.at[16], ypeer(j))
    sent.append((xr.at[pl.ds(0, 96), :], ss.at[16]))
    wait(req.at[pl.ds(0, ROWS * Y - 1)], rs.at[15])
    for i in range(ROWS):
        for j in range(Y):
            rows[4 * i:4 * (i + 1), 256 * j:256 * (j + 1)] = req[Y * i + j]
    wait(xr.at[pl.ds(0, 96), :], rs.at[16])

    xv = xr[...].astype(F32)
    square = jnp.sum(jnp.sum(xv * xv, axis=0, keepdims=True), axis=1, keepdims=True)
    gram = dot(rows[...].astype(BF16), xr[...], NT) * (1.0 / (square * (1.0 / (128 * D)) + 1e-30))
    cubic = dot(gram.astype(BF16), xr[...], NN)
    for i in range(ROWS):
        c_out[i, :, 0:D] = cubic[4 * i:4 * (i + 1)]
        c_out[i, :, D:] = jnp.broadcast_to(square, (4, 128))
    for d in ROW_ORDER:
        peer = rowpeer(d)
        send(c_out.at[peer[0]], c_in.at[r], ss.at[17], rs.at[17], peer)
    sent.append((c_in.at[pl.ds(0, ROWS - 1)], ss.at[17]))
    c_in[r] = c_out[r]
    linear = jnp.concatenate([req[Y * r + j] for j in range(Y)], axis=1)
    wait(c_in.at[pl.ds(0, ROWS - 1)], rs.at[17])
    squares = [c_in[i, 0:1, D:D + 1] for i in range(ROWS)]
    mean = sum(squares) * (1.0 / (D * D)) + 1e-30
    inverse = 1.0 / (mean * (4.0 * D))
    cubic = sum(
        c_in[i, :, 0:D] * ((squares[i] * (1.0 / (128 * D)) + 1e-30) * inverse) for i in range(ROWS))
    scale = lax.rsqrt(mean) * (1.0 / (2.0 * math.sqrt(D)))
    out_ref[...] = (math.sqrt(D) * scale) * (1.5 * linear - 0.5 * cubic)
    finish()


def shards(src_emb, tgt_emb, rotation, src_ids, tgt_ids):
    vmem = pltpu.VMEM
    scratch = [
        vmem((D, W), BF16),
        vmem((ROWS, 128, W), BF16),
        vmem((W, D), BF16),
        vmem((D, D), BF16),
        vmem((W, D), BF16),
        vmem((W, W), BF16),
        vmem((2, 1, W), jnp.int32),
        vmem((ITERS, COLS, 1, W), F32),
        vmem((ITERS, ROWS, 1, W), F32),
        vmem((PARTS, X * ROWS_IN, W), BF16),
        vmem((PARTS, X * ROWS_IN, W), BF16),
        vmem((PARTS, X - 1, ROWS_IN, W), BF16),
        vmem((PARTS, X - 1, ROWS_IN, W), BF16),
        vmem((PARTS, Y - 1, ROWS_IN, 256), BF16),
        vmem((PARTS, Y - 1, ROWS_IN, 256), BF16),
        vmem((PARTS, ROWS_IN, 256), F32),
        vmem((Z - 1, 16, 256), BF16),
        vmem((Z - 1, 16, 256), BF16),
        vmem((128, D), BF16),
        vmem((Y, 4, 256), F32),
        vmem((ROWS * Y, 4, 256), F32),
        vmem((32, D), F32),
        vmem((ROWS, 4, D + 128), F32),
        vmem((ROWS, 4, D + 128), F32),
        pltpu.SemaphoreType.DMA((5,)),
        pltpu.SemaphoreType.DMA((40,)),
        pltpu.SemaphoreType.DMA((16,)),
        pltpu.SemaphoreType.DMA((18,)),
        pltpu.SemaphoreType.DMA((18,)),
    ]
    hbm = pl.BlockSpec(memory_space=pltpu.HBM)
    here = pl.BlockSpec(memory_space=pltpu.VMEM)
    return pl.pallas_call(
        body,
        out_shape=jax.ShapeDtypeStruct((4, D), F32),
        in_specs=[hbm] * 5,
        out_specs=here,
        scratch_shapes=scratch,
        compiler_params=pltpu.CompilerParams(
            collective_id=0, has_side_effects=True, vmem_limit_bytes=63 * 2**20
        ),
        name="procrustes",
    )(src_emb.T, tgt_emb, rotation, src_ids.reshape(1, W), tgt_ids.reshape(1, W))


def solution(mesh):
    return jax.shard_map(
        shards,
        mesh=mesh,
        in_specs=(P("row", "col"), P("col", "row"), P(), P("row"), P("col")),
        out_specs=P(("row", "col"), None),
        check_vma=False,
    )
```

```python
import math

import jax
import jax.numpy as jnp
from jax import lax
from jax.experimental import pallas as pl
from jax.experimental.pallas import tpu as pltpu
from jax.sharding import PartitionSpec as P

MESH = pl.DeviceIdType.MESH
F32 = jnp.float32
BF16 = jnp.bfloat16
D = 1024
W = 512
ITERS = 3
X, Y, Z = 4, 4, 8
ROWS, COLS = 2 * X, Y * Z


def hops(step, size):
    return min(step, size - step)


COL_ORDER = sorted(
    ((dy, dz) for dy in range(Y) for dz in range(Z) if dy or dz),
    key=lambda d: -hops(d[0], Y) - hops(d[1], Z))
PLANE_ORDER = sorted(
    ((dx, dk, dy) for dx in range(X) for dk in range(2) for dy in range(Y) if dx or dk or dy),
    key=lambda d: -2 * hops(d[0], X) - 3 * d[1] - 2 * hops(d[2], Y))
ROW_ORDER = [d[:2] for d in PLANE_ORDER if d[2] == 0]
Z_ORDER = (4, 3, 5, 2, 6, 1, 7)
Z_NEAR = (0, 1, 7, 2, 6, 3, 5, 4)
PARTS = 4
ROWS_IN = 128 // PARTS
CHUNKS = Z // PARTS
XY_ORDER = (2, 1, 3)
NN = (((1,), (0,)), ((), ()))
NT = (((1,), (1,)), ((), ()))


def dot(a, b, dims):
    return lax.dot_general(a, b, dims, preferred_element_type=F32)


def send(src, dst, send_sem, recv_sem, device):
    pltpu.make_async_remote_copy(
        src_ref=src, dst_ref=dst, send_sem=send_sem, recv_sem=recv_sem,
        device_id=device, device_id_type=MESH,
    ).start()


def wait(ref, sem):
    pltpu.make_async_copy(ref, ref, sem).wait()


def add_up(parts):
    while len(parts) > 1:
        parts = [a + b for a, b in zip(parts[::2], parts[1::2])]
    return parts[0]


def block(i, size):
    return pl.ds(pl.multiple_of(i * size, size), size)


def body(src_hbm, tgt_hbm, rot_hbm, src_ids, tgt_ids, out_ref,
         src_t, ordered, tgt, rot, u, kt, kst, ids, colbuf, rowbuf,
         a_mate, a_out, a_x, x_out, yb, y_out, y_mine, zb, z_out, xr, own4, req, rows, stack, squares, c_out, c_in,
         local, zs, xs, ss, rs):
    sent = []

    def finish():
        for ref, sem in sent:
            wait(ref, sem)

    r, c = lax.axis_index("row"), lax.axis_index("col")
    x, core = r // 2, r % 2
    y, z = c // Z, c % Z
    mate = (2 * x + (1 - core), c)

    def xpeer(k):
        return (2 * ((x + k) % X) + core, c)

    def ypeer(k):
        return (r, Z * ((y + k) % Y) + z)

    def zpeer(k):
        return (r, Z * y + (z + k) % Z)

    def colpeer(d):
        return (r, Z * ((y + d[0]) % Y) + (z + d[1]) % Z)

    def rowpeer(d):
        return (2 * ((x + d[0]) % X) + (core + d[1]) % 2, c)

    def planepeer(d):
        return (rowpeer(d)[0], Z * ((y + d[2]) % Y) + z)

    def feature(i, j):
        return pl.ds(pl.multiple_of(128 * i + 32 * j, 32), 32)

    mine = src_t.at[feature(z, y)]
    load_src = pltpu.make_async_copy(src_hbm, mine, local.at[0])
    load_src.start()
    my_tgt = tgt.at[:, block(r, 128)]
    load_tgt = pltpu.make_async_copy(tgt_hbm, my_tgt, local.at[1])
    load_tgt.start()
    for i in range(Z):
        for j in range(Y):
            pltpu.make_async_copy(
                rot_hbm.at[pl.ds(32 * (Z * j + i), 32)], rot.at[pl.ds(128 * i + 32 * j, 32)], local.at[2]).start()
    load_ids = [pltpu.make_async_copy(ref, ids.at[i], local.at[3 + i]) for i, ref in enumerate((src_ids, tgt_ids))]
    for load in load_ids:
        load.start()
    bar = pltpu.get_barrier_semaphore()

    near = [zpeer(k) for k in Z_ORDER] + [xpeer(k) for k in XY_ORDER] + [ypeer(k) for k in XY_ORDER] + [mate]
    for device in near:
        pl.semaphore_signal(bar, inc=1, device_id=device, device_id_type=MESH)
    load_src.wait()
    load_tgt.wait()
    pl.semaphore_wait(bar, len(near))

    def over_y(k):
        got = src_t.at[feature((z + Z - k) % Z, y)]
        wait(mine, zs.at[k])
        for j in (1, 3, 2):
            send(got, got, ss.at[2], zs.at[32 + k], ypeer(j))

    def over_z(j):
        got = src_t.at[feature(z, (y + Y - j) % Y)]
        wait(got, zs.at[24 + j])
        for k in (1, 7):
            send(got, got, ss.at[0], zs.at[32 + k], zpeer(k))

    for j in (1, 3, 2):
        send(mine, mine, ss.at[2], zs.at[24 + j], ypeer(j))
    for k in (2, 6, 3, 5, 4, 1, 7):
        send(mine, mine, ss.at[0], zs.at[k], zpeer(k))
    for k in (1, 3, 2):
        send(my_tgt, my_tgt, ss.at[1], xs.at[k], xpeer(k))
    send(my_tgt, my_tgt, ss.at[3], rs.at[3], mate)
    sent.append((src_t.at[pl.ds(0, 13 * 32), :], ss.at[0]))
    sent.append((tgt.at[:, pl.ds(0, 384)], ss.at[1]))
    sent.append((src_t.at[pl.ds(0, 18 * 32), :], ss.at[2]))
    sent.append((tgt.at[:, pl.ds(0, 512)], ss.at[3]))

    def forward_tgt(k):
        got = tgt.at[:, block(2 * ((x + X - k) % X) + core, 128)]
        wait(got, xs.at[k])
        send(got, got, ss.at[3], rs.at[3], mate)

    over_z(1)
    over_z(3)
    over_y(2)
    over_y(6)
    over_z(2)
    forward_tgt(1)
    forward_tgt(3)
    over_y(3)
    over_y(5)
    forward_tgt(2)
    over_y(4)

    wait(tgt.at[:, pl.ds(0, 512)], rs.at[3])
    wait(rot, local.at[2])
    tv = tgt[...].astype(F32)
    tsum = jnp.sum(tv * tv, axis=1, keepdims=True)
    tscale = lax.rsqrt(tsum * (1.0 / D) + 1e-06) * (1.0 / math.sqrt(D))
    u[...] = (dot(tgt[...], rot[...], NT) * tscale).astype(BF16)
    for load in load_ids:
        load.wait()
    logits = jnp.zeros((W, W), F32)
    square = jnp.zeros((1, W), F32)
    for k in Z_NEAR:
        i = (z + Z - k) % Z
        here = src_t.at[block(i, 128)]
        if k in (1, 7):
            wait(mine, zs.at[k])
        if k:
            wait(src_t.at[pl.ds(0, 96)], zs.at[32 + k])
        part = here[...]
        logits = logits + dot(u[:, block(i, 128)], part, NN)
        part = part.astype(F32)
        square = square + jnp.sum(part * part, axis=0, keepdims=True)
    sscale = lax.rsqrt(square * (1.0 / D) + 1e-06) * (1.0 / math.sqrt(D))
    kt[...] = jnp.exp(logits * (sscale * (1.0 / 0.03))).astype(BF16)

    row8 = lax.broadcasted_iota(jnp.int32, (8, W), 0)

    def matvec(v, matrix):
        high = v.astype(BF16).astype(F32)
        both = jnp.where(row8 == 0, high, jnp.where(row8 == 1, v - high, 0.0)).astype(BF16)
        return jnp.sum(dot(both, matrix[...], NN), axis=0, keepdims=True)

    def meanwhile():
        at = lax.broadcasted_iota(jnp.int32, (128, 128), 0)
        step = jnp.zeros((128, 128), jnp.int32)
        for i, k in enumerate(Z_ORDER):
            step = jnp.where(at // 16 == i, k, step)
        to = 32 * (at // 4 % 4) + 4 * ((z + step) % Z) + at % 4
        order = (lax.broadcasted_iota(jnp.int32, (128, 128), 1) == to).astype(BF16)
        kst[...] = jnp.transpose(kt[...])
        for i in range(ROWS):
            natural = [src_t[128 * j + 32 * (i // 2):128 * j + 32 * (i // 2) + 32]
                       for j in range(4 * (i % 2), 4 * (i % 2) + 4)]
            ordered[i] = dot(order, jnp.concatenate(natural, axis=0), NN).astype(BF16)

    def sum_col(part, it):
        colbuf[it, c] = part

        for d in COL_ORDER:
            send(colbuf.at[it, c], colbuf.at[it, c], ss.at[4 + it], rs.at[4 + it], colpeer(d))
        sent.append((colbuf.at[it, pl.ds(0, COLS - 1)], ss.at[4 + it]))
        if it == 0:
            meanwhile()
        wait(colbuf.at[it, pl.ds(0, COLS - 1)], rs.at[4 + it])
        return add_up([colbuf[it, i] for i in range(COLS)])

    def start_row(part, it):
        rowbuf[it, r] = part
        for d in ROW_ORDER:
            send(rowbuf.at[it, r], rowbuf.at[it, r], ss.at[7 + it], rs.at[7 + it], rowpeer(d))
        sent.append((rowbuf.at[it, pl.ds(0, ROWS - 1)], ss.at[7 + it]))

    def end_row(it):
        wait(rowbuf.at[it, pl.ds(0, ROWS - 1)], rs.at[7 + it])
        return add_up([rowbuf[it, i] for i in range(ROWS)])

    src_mass = lax.rsqrt(1000.0 + ids[0].astype(F32))
    tgt_mass = lax.rsqrt(1000.0 + ids[1].astype(F32))
    tgt_scale = jnp.ones((1, W), F32)
    for it in range(ITERS):
        src_scale = src_mass / sum_col(matvec(tgt_scale, kt), it)
        if it < ITERS - 1:
            start_row(matvec(src_scale, kst), it)
            tgt_scale = tgt_mass / end_row(it)

    plan = (kt[...].astype(F32) * (src_scale * sscale)).astype(BF16)
    def some_rows(k, h):
        first = pl.ds(ROWS_IN * h, ROWS_IN)
        return jnp.concatenate([ordered[2 * ((x + j) % X) + k, first] for j in range(X)], axis=0)

    for h in range(PARTS):
        a_out[h] = dot(some_rows(1 - core, h), plan, NT).astype(BF16)
        send(a_out.at[h], a_mate.at[h], ss.at[10], xs.at[4 + h], mate)
    sent.append((a_mate, ss.at[10]))
    start_row(matvec(src_scale, kst), ITERS - 1)
    tscale_l = jnp.transpose(jnp.broadcast_to(tscale, (W, 128)))[0:1, :]
    kept = []
    for h in range(PARTS):
        half = dot(some_rows(core, h), plan, NT)
        wait(a_mate.at[h], xs.at[4 + h])
        half = half + a_mate[h].astype(F32)
        kept.append(half[0:ROWS_IN])
        for k in (2, 1, 3):
            x_out[h, k - 1] = half[ROWS_IN * k:ROWS_IN * (k + 1)].astype(BF16)
            send(x_out.at[h, k - 1], a_x.at[h, k - 1], ss.at[11], xs.at[8 + h], xpeer(k))
    sent.append((a_x, ss.at[11]))
    factor = (tgt_mass / end_row(ITERS - 1)) * tscale_l

    for h in range(PARTS):
        wait(a_x.at[h], xs.at[8 + h])
        total = kept[h] + ((a_x[h, 0].astype(F32) + a_x[h, 1].astype(F32)) + a_x[h, 2].astype(F32))
        total = (total * factor).astype(BF16)
        for j in XY_ORDER:
            y_out[h, j - 1] = dot(total, tgt[:, block((y + j) % Y, 256)], NN).astype(BF16)
            send(y_out.at[h, j - 1], yb.at[h, j - 1], ss.at[12], xs.at[12 + h], ypeer(j))
        y_mine[h] = dot(total, tgt[:, block(y, 256)], NN)
    sent.append((yb, ss.at[12]))
    for h in range(PARTS):
        wait(yb.at[h], xs.at[12 + h])
        part = (y_mine[h] + yb[h, 0].astype(F32)) + (yb[h, 1].astype(F32) + yb[h, 2].astype(F32))
        for i in range(CHUNKS):
            own = part[16 * i:16 * (i + 1)]
            k = (Z_ORDER + (0,))[CHUNKS * h + i]
            if k:
                z_out[k - 1] = own.astype(BF16)
                send(z_out.at[k - 1], zb.at[k - 1], ss.at[13], rs.at[13], zpeer(k))
    sent.append((zb, ss.at[13]))
    wait(zb, rs.at[13])
    own = own + jnp.sum(zb[...].astype(F32), axis=0)

    def cell(i, j):
        return xr.at[block(i, 16), block(j, 256)]

    xr[block(z, 16), block(y, 256)] = own.astype(BF16)
    for k in Z_ORDER:
        send(cell(z, y), cell(z, y), ss.at[14], zs.at[16 + k], zpeer(k))
    sent.append((xr.at[pl.ds(0, 112), pl.ds(0, 256)], ss.at[14]))
    for j in XY_ORDER:
        send(cell(z, y), cell(z, y), ss.at[16], rs.at[16], ypeer(j))
    for j in range(Y):
        own4[j] = own[4 * j:4 * (j + 1)]
    for d in PLANE_ORDER:
        send(own4.at[(y + d[2]) % Y], req.at[Y * r + y], ss.at[15], rs.at[15], planepeer(d))
    sent.append((req.at[pl.ds(0, ROWS * Y - 1)], ss.at[15]))
    req[Y * r + y] = own4[y]
    for k in (1, 7, 2, 6, 3, 5, 4):
        got = cell((z + Z - k) % Z, y)
        wait(got, zs.at[16 + k])
        for j in XY_ORDER:
            send(got, got, ss.at[16], rs.at[16], ypeer(j))
    sent.append((xr.at[pl.ds(0, 96), :], ss.at[16]))
    wait(req.at[pl.ds(0, ROWS * Y - 1)], rs.at[15])
    for i in range(ROWS):
        for j in range(Y):
            rows[4 * i:4 * (i + 1), 256 * j:256 * (j + 1)] = req[Y * i + j]
    wait(xr.at[pl.ds(0, 96), :], rs.at[16])

    xv = xr[...].astype(F32)
    square = jnp.sum(jnp.sum(xv * xv, axis=0, keepdims=True), axis=1, keepdims=True)
    squares[r] = jnp.broadcast_to(square, (1, 128))
    for d in ROW_ORDER:
        send(squares.at[r], squares.at[r], ss.at[18], rs.at[18], rowpeer(d))
    sent.append((squares.at[pl.ds(0, ROWS - 1)], ss.at[18]))
    gram = dot(rows[...].astype(BF16), xr[...], NT) * (1.0 / (square * (1.0 / (128 * D)) + 1e-30))
    cubic = dot(gram.astype(BF16), xr[...], NN)
    for i in range(ROWS):
        for j in range(Y):
            stack[i, 4 * j:4 * (j + 1)] = cubic[4 * i:4 * (i + 1), 256 * j:256 * (j + 1)]
    c_out[...] = stack[...].astype(BF16)
    for d in ROW_ORDER:
        peer = rowpeer(d)
        send(c_out.at[peer[0]], c_in.at[r], ss.at[17], rs.at[17], peer)
    sent.append((c_in.at[pl.ds(0, ROWS - 1)], ss.at[17]))
    c_in[r] = c_out[r]
    linear = jnp.concatenate([req[Y * r + j] for j in range(Y)], axis=1)
    wait(squares.at[pl.ds(0, ROWS - 1)], rs.at[18])
    each = [squares[i][:, 0:1] for i in range(ROWS)]
    mean = add_up(each) * (1.0 / (D * D)) + 1e-30
    inverse = 1.0 / (mean * (4.0 * D))
    scale = lax.rsqrt(mean) * (1.0 / (2.0 * math.sqrt(D)))
    wait(c_in.at[pl.ds(0, ROWS - 1)], rs.at[17])
    cubic = add_up([
        c_in[i].astype(F32) * ((each[i] * (1.0 / (128 * D)) + 1e-30) * inverse) for i in range(ROWS)])
    cubic = jnp.concatenate([cubic[4 * j:4 * (j + 1)] for j in range(Y)], axis=1)
    out_ref[...] = (math.sqrt(D) * scale) * (1.5 * linear - 0.5 * cubic)
    finish()


def shards(src_emb, tgt_emb, rotation, src_ids, tgt_ids):
    vmem = pltpu.VMEM
    scratch = [
        vmem((D, W), BF16),
        vmem((ROWS, 128, W), BF16),
        vmem((W, D), BF16),
        vmem((D, D), BF16),
        vmem((W, D), BF16),
        vmem((W, W), BF16),
        vmem((W, W), BF16),
        vmem((2, 1, W), jnp.int32),
        vmem((ITERS, COLS, 1, W), F32),
        vmem((ITERS, ROWS, 1, W), F32),
        vmem((PARTS, X * ROWS_IN, W), BF16),
        vmem((PARTS, X * ROWS_IN, W), BF16),
        vmem((PARTS, X - 1, ROWS_IN, W), BF16),
        vmem((PARTS, X - 1, ROWS_IN, W), BF16),
        vmem((PARTS, Y - 1, ROWS_IN, 256), BF16),
        vmem((PARTS, Y - 1, ROWS_IN, 256), BF16),
        vmem((PARTS, ROWS_IN, 256), F32),
        vmem((Z - 1, 16, 256), BF16),
        vmem((Z - 1, 16, 256), BF16),
        vmem((128, D), BF16),
        vmem((Y, 4, 256), F32),
        vmem((ROWS * Y, 4, 256), F32),
        vmem((32, D), F32),
        vmem((ROWS, 16, 256), F32),
        vmem((ROWS, 1, 128), F32),
        vmem((ROWS, 16, 256), BF16),
        vmem((ROWS, 16, 256), BF16),
        pltpu.SemaphoreType.DMA((5,)),
        pltpu.SemaphoreType.DMA((40,)),
        pltpu.SemaphoreType.DMA((16,)),
        pltpu.SemaphoreType.DMA((19,)),
        pltpu.SemaphoreType.DMA((19,)),
    ]
    hbm = pl.BlockSpec(memory_space=pltpu.HBM)
    here = pl.BlockSpec(memory_space=pltpu.VMEM)
    return pl.pallas_call(
        body,
        out_shape=pltpu.VMEM((4, D), F32),
        in_specs=[hbm] * 5,
        out_specs=here,
        scratch_shapes=scratch,
        compiler_params=pltpu.CompilerParams(
            collective_id=0, has_side_effects=True, vmem_limit_bytes=60 * 2**20
        ),
        name="procrustes",
    )(src_emb.T, tgt_emb, rotation, src_ids.reshape(1, W), tgt_ids.reshape(1, W))


def solution(mesh):
    return jax.shard_map(
        shards,
        mesh=mesh,
        in_specs=(P("row", "col"), P("col", "row"), P(), P("row"), P("col")),
        out_specs=P(("row", "col"), None),
        check_vma=False,
    )
```

```python
import math

import jax
import jax.numpy as jnp
from jax import lax
from jax.experimental import pallas as pl
from jax.experimental.pallas import tpu as pltpu
from jax.sharding import PartitionSpec as P

MESH = pl.DeviceIdType.MESH
F32 = jnp.float32
BF16 = jnp.bfloat16
D = 1024
W = 512
ITERS = 3
X, Y, Z = 4, 4, 8
ROWS, COLS = 2 * X, Y * Z


def hops(step, size):
    return min(step, size - step)


COL_ORDER = sorted(
    ((dy, dz) for dy in range(Y) for dz in range(Z) if dy or dz),
    key=lambda d: -hops(d[0], Y) - hops(d[1], Z))
PLANE_ORDER = sorted(
    ((dx, dk, dy) for dx in range(X) for dk in range(2) for dy in range(Y) if dx or dk or dy),
    key=lambda d: -2 * hops(d[0], X) - 3 * d[1] - 2 * hops(d[2], Y))
ROW_ORDER = [d[:2] for d in PLANE_ORDER if d[2] == 0]
Z_ORDER = (4, 3, 5, 2, 6, 1, 7)
Z_NEAR = (0, 2, 6, 1, 7, 3, 5, 4)
PARTS = 4
ROWS_IN = 128 // PARTS
CHUNKS = Z // PARTS
XY_ORDER = (2, 1, 3)
NN = (((1,), (0,)), ((), ()))
NT = (((1,), (1,)), ((), ()))


def dot(a, b, dims):
    return lax.dot_general(a, b, dims, preferred_element_type=F32)


def send(src, dst, send_sem, recv_sem, device):
    pltpu.make_async_remote_copy(
        src_ref=src, dst_ref=dst, send_sem=send_sem, recv_sem=recv_sem,
        device_id=device, device_id_type=MESH,
    ).start()


def wait(ref, sem):
    pltpu.make_async_copy(ref, ref, sem).wait()


def add_up(parts):
    while len(parts) > 1:
        parts = [a + b for a, b in zip(parts[::2], parts[1::2])]
    return parts[0]


def block(i, size):
    return pl.ds(pl.multiple_of(i * size, size), size)


def body(src_hbm, tgt_hbm, rot_hbm, src_ids, tgt_ids, out_ref,
         src_t, ordered, tgt, rot, u, kt, kst, ids, colbuf, rowbuf,
         kt_mate, ord_mate, src_factor, plan, a_x, x_out, yb, y_out, y_mine, zb, z_out, xr, own4, req, rows, stack, squares, c_out, c_in,
         local, zs, xs, ss, rs):
    sent = []

    def finish():
        for ref, sem in sent:
            wait(ref, sem)

    r, c = lax.axis_index("row"), lax.axis_index("col")
    x, core = r // 2, r % 2
    y, z = c // Z, c % Z
    mate = (2 * x + (1 - core), c)

    def xpeer(k):
        return (2 * ((x + k) % X) + core, c)

    def ypeer(k):
        return (r, Z * ((y + k) % Y) + z)

    def zpeer(k):
        return (r, Z * y + (z + k) % Z)

    def colpeer(d):
        return (r, Z * ((y + d[0]) % Y) + (z + d[1]) % Z)

    def rowpeer(d):
        return (2 * ((x + d[0]) % X) + (core + d[1]) % 2, c)

    def planepeer(d):
        return (rowpeer(d)[0], Z * ((y + d[2]) % Y) + z)

    def feature(i, j):
        return pl.ds(pl.multiple_of(128 * i + 32 * j, 32), 32)

    mine = src_t.at[feature(z, y)]
    load_src = pltpu.make_async_copy(src_hbm, mine, local.at[0])
    load_src.start()
    my_tgt = tgt.at[:, block(r, 128)]
    load_tgt = pltpu.make_async_copy(tgt_hbm, my_tgt, local.at[1])
    load_tgt.start()
    for i in range(Z):
        for j in range(Y):
            pltpu.make_async_copy(
                rot_hbm.at[pl.ds(32 * (Z * j + i), 32)], rot.at[pl.ds(128 * i + 32 * j, 32)], local.at[2]).start()
    load_ids = [pltpu.make_async_copy(ref, ids.at[i], local.at[3 + i]) for i, ref in enumerate((src_ids, tgt_ids))]
    for load in load_ids:
        load.start()
    bar = pltpu.get_barrier_semaphore()

    near = [zpeer(k) for k in (2, 6, 1, 7)] + [xpeer(k) for k in XY_ORDER] + [ypeer(k) for k in XY_ORDER] + [mate]
    for device in near:
        pl.semaphore_signal(bar, inc=1, device_id=device, device_id_type=MESH)
    load_src.wait()
    load_tgt.wait()
    pl.semaphore_wait(bar, len(near))

    def over_y(k):
        got = src_t.at[feature((z + Z - k) % Z, y)]
        wait(mine, zs.at[k])
        if k in (2, 6):
            send(got, got, ss.at[0], zs.at[3 if k == 2 else 5], zpeer(1 if k == 2 else 7))
            half = src_t.at[feature((z + Z - k) % Z, y), pl.ds(0 if k == 2 else W // 2, W // 2)]
            send(half, half, ss.at[0], zs.at[4], zpeer(k))
        for j in (1, 3, 2):
            send(got, got, ss.at[2], zs.at[32 + k], ypeer(j))

    def over_z(j):
        got = src_t.at[feature(z, (y + Y - j) % Y)]
        wait(got, zs.at[24 + j])
        for k in (1, 7):
            send(got, got, ss.at[0], zs.at[32 + k], zpeer(k))

    for j in (1, 3, 2):
        send(mine, mine, ss.at[2], zs.at[24 + j], ypeer(j))
    for k in (2, 6, 1, 7):
        send(mine, mine, ss.at[0], zs.at[k], zpeer(k))
    for k in (1, 3, 2):
        send(my_tgt, my_tgt, ss.at[1], xs.at[k], xpeer(k))
    send(my_tgt, my_tgt, ss.at[3], rs.at[3], mate)
    sent.append((src_t.at[pl.ds(0, 13 * 32), :], ss.at[0]))
    sent.append((tgt.at[:, pl.ds(0, 384)], ss.at[1]))
    sent.append((src_t.at[pl.ds(0, 18 * 32), :], ss.at[2]))
    sent.append((tgt.at[:, pl.ds(0, 512)], ss.at[3]))

    def forward_tgt(k):
        got = tgt.at[:, block(2 * ((x + X - k) % X) + core, 128)]
        wait(got, xs.at[k])
        send(got, got, ss.at[3], rs.at[3], mate)

    over_y(2)
    over_y(6)
    over_z(1)
    over_z(3)
    over_z(2)
    over_y(3)
    over_y(5)
    forward_tgt(1)
    forward_tgt(3)
    over_y(4)
    forward_tgt(2)

    wait(tgt.at[:, pl.ds(0, 512)], rs.at[3])
    wait(rot, local.at[2])
    tv = tgt[...].astype(F32)
    tsum = jnp.sum(tv * tv, axis=1, keepdims=True)
    tscale = lax.rsqrt(tsum * (1.0 / D) + 1e-06) * (1.0 / math.sqrt(D))
    u[...] = (dot(tgt[...], rot[...], NT) * tscale).astype(BF16)
    for load in load_ids:
        load.wait()
    logits = jnp.zeros((W, W), F32)
    square = jnp.zeros((1, W), F32)
    for k in Z_NEAR:
        i = (z + Z - k) % Z
        here = src_t.at[block(i, 128)]
        if k in (1, 7):
            wait(mine, zs.at[k])
        if k:
            wait(src_t.at[pl.ds(0, 96)], zs.at[32 + k])
        part = here[...]
        logits = logits + dot(u[:, block(i, 128)], part, NN)
        part = part.astype(F32)
        square = square + jnp.sum(part * part, axis=0, keepdims=True)
    sscale = lax.rsqrt(square * (1.0 / D) + 1e-06) * (1.0 / math.sqrt(D))
    kt[...] = jnp.exp(logits * (sscale * (1.0 / 0.03))).astype(BF16)

    row8 = lax.broadcasted_iota(jnp.int32, (8, W), 0)

    def matvec(v, matrix):
        high = v.astype(BF16).astype(F32)
        both = jnp.where(row8 == 0, high, jnp.where(row8 == 1, v - high, 0.0)).astype(BF16)
        return jnp.sum(dot(both, matrix[...], NN), axis=0, keepdims=True)

    def meanwhile():
        at = lax.broadcasted_iota(jnp.int32, (128, 128), 0)
        step = jnp.zeros((128, 128), jnp.int32)
        for i, k in enumerate(Z_ORDER):
            step = jnp.where(at // 16 == i, k, step)
        to = 32 * (at // 4 % 4) + 4 * ((z + step) % Z) + at % 4
        order = (lax.broadcasted_iota(jnp.int32, (128, 128), 1) == to).astype(BF16)
        kst[...] = jnp.transpose(kt[...])
        for i in range(ROWS):
            natural = [src_t[128 * j + 32 * (i // 2):128 * j + 32 * (i // 2) + 32]
                       for j in range(4 * (i % 2), 4 * (i % 2) + 4)]
            ordered[i] = dot(order, jnp.concatenate(natural, axis=0), NN).astype(BF16)
        for j in range(X):
            send(ordered.at[2 * j + (1 - core)], ord_mate.at[j], ss.at[19], xs.at[5], mate)
        sent.append((ord_mate, ss.at[19]))

    def sum_col(part, it):
        colbuf[it, c] = part

        for d in COL_ORDER:
            send(colbuf.at[it, c], colbuf.at[it, c], ss.at[4 + it], rs.at[4 + it], colpeer(d))
        sent.append((colbuf.at[it, pl.ds(0, COLS - 1)], ss.at[4 + it]))
        if it == 0:
            send(kt, kt_mate, ss.at[10], xs.at[4], mate)
            sent.append((kt_mate, ss.at[10]))
            meanwhile()
        wait(colbuf.at[it, pl.ds(0, COLS - 1)], rs.at[4 + it])
        if it == 0:
            wait(kt_mate, xs.at[4])
            wait(ord_mate, xs.at[5])
        return add_up([colbuf[it, i] for i in range(COLS)])

    def start_row(part, it):
        rowbuf[it, r] = part
        for d in ROW_ORDER:
            send(rowbuf.at[it, r], rowbuf.at[it, r], ss.at[7 + it], rs.at[7 + it], rowpeer(d))
        sent.append((rowbuf.at[it, pl.ds(0, ROWS - 1)], ss.at[7 + it]))

    def end_row(it):
        wait(rowbuf.at[it, pl.ds(0, ROWS - 1)], rs.at[7 + it])
        return add_up([rowbuf[it, i] for i in range(ROWS)])

    src_mass = lax.rsqrt(1000.0 + ids[0].astype(F32))
    tgt_mass = lax.rsqrt(1000.0 + ids[1].astype(F32))
    tgt_scale = jnp.ones((1, W), F32)
    for it in range(ITERS):
        src_scale = src_mass / sum_col(matvec(tgt_scale, kt), it)
        if it < ITERS - 1:
            start_row(matvec(src_scale, kst), it)
            tgt_scale = tgt_mass / end_row(it)

    src_factor[0] = src_scale * sscale
    send(src_factor.at[0], src_factor.at[1], ss.at[20], xs.at[6], mate)
    sent.append((src_factor.at[0], ss.at[20]))
    plan[0] = (kt[...].astype(F32) * src_factor[0]).astype(BF16)

    def some_rows(h, i):
        first = pl.ds(ROWS_IN * h, ROWS_IN)
        rows_of = [ordered[2 * ((x + j) % X) + core, first] if i == 0 else ord_mate[(x + j) % X, first] for j in range(X)]
        return dot(jnp.concatenate(rows_of, axis=0), plan[i], NT)

    first_part = some_rows(0, 0)
    start_row(matvec(src_scale, kst), ITERS - 1)
    tscale_l = jnp.transpose(jnp.broadcast_to(tscale, (W, 128)))[0:1, :]
    wait(src_factor.at[1], xs.at[6])
    plan[1] = (kt_mate[...].astype(F32) * src_factor[1]).astype(BF16)
    kept = []
    for h in range(PARTS):
        part = (some_rows(h, 0) if h else first_part) + some_rows(h, 1)
        kept.append(part[0:ROWS_IN])
        for k in (2, 1, 3):
            x_out[h, k - 1] = part[ROWS_IN * k:ROWS_IN * (k + 1)].astype(BF16)
            send(x_out.at[h, k - 1], a_x.at[h, k - 1], ss.at[11], xs.at[12 + h], xpeer(k))
    sent.append((a_x, ss.at[11]))
    factor = (tgt_mass / end_row(ITERS - 1)) * tscale_l

    for h in range(PARTS):
        wait(a_x.at[h], xs.at[12 + h])
        total = kept[h] + ((a_x[h, 0].astype(F32) + a_x[h, 1].astype(F32)) + a_x[h, 2].astype(F32))
        total = (total * factor).astype(BF16)
        for j in XY_ORDER:
            y_out[h, j - 1] = dot(total, tgt[:, block((y + j) % Y, 256)], NN).astype(BF16)
            send(y_out.at[h, j - 1], yb.at[h, j - 1], ss.at[12], xs.at[20 + h], ypeer(j))
        y_mine[h] = dot(total, tgt[:, block(y, 256)], NN)
    sent.append((yb, ss.at[12]))
    for h in range(PARTS):
        wait(yb.at[h], xs.at[20 + h])
        part = (y_mine[h] + yb[h, 0].astype(F32)) + (yb[h, 1].astype(F32) + yb[h, 2].astype(F32))
        for i in range(CHUNKS):
            own = part[16 * i:16 * (i + 1)]
            k = (Z_ORDER + (0,))[CHUNKS * h + i]
            if k:
                z_out[k - 1] = own.astype(BF16)
                send(z_out.at[k - 1], zb.at[k - 1], ss.at[13], rs.at[13], zpeer(k))
    sent.append((zb, ss.at[13]))
    wait(zb, rs.at[13])
    own = own + jnp.sum(zb[...].astype(F32), axis=0)

    def cell(i, j):
        return xr.at[block(i, 16), block(j, 256)]

    xr[block(z, 16), block(y, 256)] = own.astype(BF16)
    for k in Z_ORDER:
        send(cell(z, y), cell(z, y), ss.at[14], zs.at[16 + k], zpeer(k))
    sent.append((xr.at[pl.ds(0, 112), pl.ds(0, 256)], ss.at[14]))
    for j in XY_ORDER:
        send(cell(z, y), cell(z, y), ss.at[16], rs.at[16], ypeer(j))
    for j in range(Y):
        own4[j] = own[4 * j:4 * (j + 1)]
    for d in PLANE_ORDER:
        send(own4.at[(y + d[2]) % Y], req.at[Y * r + y], ss.at[15], rs.at[15], planepeer(d))
    sent.append((req.at[pl.ds(0, ROWS * Y - 1)], ss.at[15]))
    req[Y * r + y] = own4[y]
    for k in (1, 7, 2, 6, 3, 5, 4):
        got = cell((z + Z - k) % Z, y)
        wait(got, zs.at[16 + k])
        for j in XY_ORDER:
            send(got, got, ss.at[16], rs.at[16], ypeer(j))
    sent.append((xr.at[pl.ds(0, 96), :], ss.at[16]))
    wait(req.at[pl.ds(0, ROWS * Y - 1)], rs.at[15])
    for i in range(ROWS):
        for j in range(Y):
            rows[4 * i:4 * (i + 1), 256 * j:256 * (j + 1)] = req[Y * i + j]
    wait(xr.at[pl.ds(0, 96), :], rs.at[16])

    xv = xr[...].astype(F32)
    square = jnp.sum(jnp.sum(xv * xv, axis=0, keepdims=True), axis=1, keepdims=True)
    squares[r] = jnp.broadcast_to(square, (1, 128))
    for d in ROW_ORDER:
        send(squares.at[r], squares.at[r], ss.at[18], rs.at[18], rowpeer(d))
    sent.append((squares.at[pl.ds(0, ROWS - 1)], ss.at[18]))
    gram = dot(rows[...].astype(BF16), xr[...], NT) * (1.0 / (square * (1.0 / (128 * D)) + 1e-30))
    cubic = dot(gram.astype(BF16), xr[...], NN)
    for i in range(ROWS):
        for j in range(Y):
            stack[i, 4 * j:4 * (j + 1)] = cubic[4 * i:4 * (i + 1), 256 * j:256 * (j + 1)]
    c_out[...] = stack[...].astype(BF16)
    for d in ROW_ORDER:
        peer = rowpeer(d)
        send(c_out.at[peer[0]], c_in.at[r], ss.at[17], rs.at[17], peer)
    sent.append((c_in.at[pl.ds(0, ROWS - 1)], ss.at[17]))
    c_in[r] = c_out[r]
    linear = jnp.concatenate([req[Y * r + j] for j in range(Y)], axis=1)
    wait(squares.at[pl.ds(0, ROWS - 1)], rs.at[18])
    each = [squares[i][:, 0:1] for i in range(ROWS)]
    mean = add_up(each) * (1.0 / (D * D)) + 1e-30
    inverse = 1.0 / (mean * (4.0 * D))
    scale = lax.rsqrt(mean) * (1.0 / (2.0 * math.sqrt(D)))
    wait(c_in.at[pl.ds(0, ROWS - 1)], rs.at[17])
    cubic = add_up([
        c_in[i].astype(F32) * ((each[i] * (1.0 / (128 * D)) + 1e-30) * inverse) for i in range(ROWS)])
    cubic = jnp.concatenate([cubic[4 * j:4 * (j + 1)] for j in range(Y)], axis=1)
    out_ref[...] = (math.sqrt(D) * scale) * (1.5 * linear - 0.5 * cubic)
    finish()


def shards(src_emb, tgt_emb, rotation, src_ids, tgt_ids):
    vmem = pltpu.VMEM
    scratch = [
        vmem((D, W), BF16),
        vmem((ROWS, 128, W), BF16),
        vmem((W, D), BF16),
        vmem((D, D), BF16),
        vmem((W, D), BF16),
        vmem((W, W), BF16),
        vmem((W, W), BF16),
        vmem((2, 1, W), jnp.int32),
        vmem((ITERS, COLS, 1, W), F32),
        vmem((ITERS, ROWS, 1, W), F32),
        vmem((W, W), BF16),
        vmem((X, 128, W), BF16),
        vmem((2, 1, W), F32),
        vmem((2, W, W), BF16),
        vmem((PARTS, X - 1, ROWS_IN, W), BF16),
        vmem((PARTS, X - 1, ROWS_IN, W), BF16),
        vmem((PARTS, Y - 1, ROWS_IN, 256), BF16),
        vmem((PARTS, Y - 1, ROWS_IN, 256), BF16),
        vmem((PARTS, ROWS_IN, 256), F32),
        vmem((Z - 1, 16, 256), BF16),
        vmem((Z - 1, 16, 256), BF16),
        vmem((128, D), BF16),
        vmem((Y, 4, 256), F32),
        vmem((ROWS * Y, 4, 256), F32),
        vmem((32, D), F32),
        vmem((ROWS, 16, 256), F32),
        vmem((ROWS, 1, 128), F32),
        vmem((ROWS, 16, 256), BF16),
        vmem((ROWS, 16, 256), BF16),
        pltpu.SemaphoreType.DMA((5,)),
        pltpu.SemaphoreType.DMA((40,)),
        pltpu.SemaphoreType.DMA((28,)),
        pltpu.SemaphoreType.DMA((21,)),
        pltpu.SemaphoreType.DMA((21,)),
    ]
    hbm = pl.BlockSpec(memory_space=pltpu.HBM)
    here = pl.BlockSpec(memory_space=pltpu.VMEM)
    return pl.pallas_call(
        body,
        out_shape=pltpu.VMEM((4, D), F32),
        in_specs=[hbm] * 5,
        out_specs=here,
        scratch_shapes=scratch,
        compiler_params=pltpu.CompilerParams(
            collective_id=0, has_side_effects=True, vmem_limit_bytes=60 * 2**20
        ),
        name="procrustes",
    )(src_emb.T, tgt_emb, rotation, src_ids.reshape(1, W), tgt_ids.reshape(1, W))


def solution(mesh):
    return jax.shard_map(
        shards,
        mesh=mesh,
        in_specs=(P("row", "col"), P("col", "row"), P(), P("row"), P("col")),
        out_specs=P(("row", "col"), None),
        check_vma=False,
    )
```

```python
import math

import jax
import jax.numpy as jnp
from jax import lax
from jax.experimental import pallas as pl
from jax.experimental.pallas import tpu as pltpu
from jax.sharding import PartitionSpec as P

MESH = pl.DeviceIdType.MESH
F32 = jnp.float32
BF16 = jnp.bfloat16
D = 1024
W = 512
ITERS = 3
X, Y, Z = 4, 4, 8
ROWS, COLS = 2 * X, Y * Z


def hops(step, size):
    return min(step, size - step)


COL_ORDER = sorted(
    ((dy, dz) for dy in range(Y) for dz in range(Z) if dy or dz),
    key=lambda d: -hops(d[0], Y) - hops(d[1], Z))
PLANE_ORDER = sorted(
    ((dx, dk, dy) for dx in range(X) for dk in range(2) for dy in range(Y) if dx or dk or dy),
    key=lambda d: -2 * hops(d[0], X) - 3 * d[1] - 2 * hops(d[2], Y))
ROW_ORDER = [d[:2] for d in PLANE_ORDER if d[2] == 0]
Z_ORDER = (4, 3, 5, 2, 6, 1, 7)
Z_NEAR = (0, 2, 6, 1, 7, 3, 5, 4)
PARTS = 4
ROWS_IN = 128 // PARTS
CHUNKS = Z // PARTS
XY_ORDER = (2, 1, 3)
NN = (((1,), (0,)), ((), ()))
NT = (((1,), (1,)), ((), ()))


def dot(a, b, dims):
    return lax.dot_general(a, b, dims, preferred_element_type=F32)


def send(src, dst, send_sem, recv_sem, device):
    pltpu.make_async_remote_copy(
        src_ref=src, dst_ref=dst, send_sem=send_sem, recv_sem=recv_sem,
        device_id=device, device_id_type=MESH,
    ).start()


def wait(ref, sem):
    pltpu.make_async_copy(ref, ref, sem).wait()


def add_up(parts):
    while len(parts) > 1:
        parts = [a + b for a, b in zip(parts[::2], parts[1::2])]
    return parts[0]


def block(i, size):
    return pl.ds(pl.multiple_of(i * size, size), size)


def body(src_hbm, tgt_hbm, rot_hbm, src_ids, tgt_ids, out_ref,
         src_t, ordered, tgt, rot, u, kt, kst, ids, colbuf, rowbuf,
         kt_mate, ord_mate, src_factor, tscale_row, plan, a_x, x_out, yb, y_out, y_mine, zb, z_out, xr, own4, req, rows, stack, squares, c_out, c_in,
         local, zs, xs, ss, rs):
    sent = []

    def finish():
        for ref, sem in sent:
            wait(ref, sem)

    r, c = lax.axis_index("row"), lax.axis_index("col")
    x, core = r // 2, r % 2
    y, z = c // Z, c % Z
    mate = (2 * x + (1 - core), c)

    def xpeer(k):
        return (2 * ((x + k) % X) + core, c)

    def ypeer(k):
        return (r, Z * ((y + k) % Y) + z)

    def zpeer(k):
        return (r, Z * y + (z + k) % Z)

    def colpeer(d):
        return (r, Z * ((y + d[0]) % Y) + (z + d[1]) % Z)

    def rowpeer(d):
        return (2 * ((x + d[0]) % X) + (core + d[1]) % 2, c)

    def planepeer(d):
        return (rowpeer(d)[0], Z * ((y + d[2]) % Y) + z)

    def feature(i, j):
        return pl.ds(pl.multiple_of(128 * i + 32 * j, 32), 32)

    mine = src_t.at[feature(z, y)]
    load_src = pltpu.make_async_copy(src_hbm, mine, local.at[0])
    load_src.start()
    my_tgt = tgt.at[:, block(r, 128)]
    load_tgt = pltpu.make_async_copy(tgt_hbm, my_tgt, local.at[1])
    load_tgt.start()
    for i in range(Z):
        for j in range(Y):
            pltpu.make_async_copy(
                rot_hbm.at[pl.ds(32 * (Z * j + i), 32)], rot.at[pl.ds(128 * i + 32 * j, 32)], local.at[2]).start()
    load_ids = [pltpu.make_async_copy(ref, ids.at[i], local.at[3 + i]) for i, ref in enumerate((src_ids, tgt_ids))]
    for load in load_ids:
        load.start()
    bar = pltpu.get_barrier_semaphore()

    near = [zpeer(k) for k in (2, 6, 1, 7)] + [xpeer(k) for k in XY_ORDER] + [ypeer(k) for k in XY_ORDER] + [mate]
    for device in near:
        pl.semaphore_signal(bar, inc=1, device_id=device, device_id_type=MESH)
    load_src.wait()
    load_tgt.wait()
    pl.semaphore_wait(bar, len(near))

    def over_y(k):
        got = src_t.at[feature((z + Z - k) % Z, y)]
        wait(mine, zs.at[k])
        if k in (2, 6):
            send(got, got, ss.at[0], zs.at[3 if k == 2 else 5], zpeer(1 if k == 2 else 7))
            half = src_t.at[feature((z + Z - k) % Z, y), pl.ds(0 if k == 2 else W // 2, W // 2)]
            send(half, half, ss.at[0], zs.at[4], zpeer(k))
        for j in (1, 3, 2):
            send(got, got, ss.at[2], zs.at[32 + k], ypeer(j))

    def over_z(j):
        got = src_t.at[feature(z, (y + Y - j) % Y)]
        wait(got, zs.at[24 + j])
        for k in (1, 7):
            send(got, got, ss.at[0], zs.at[32 + k], zpeer(k))

    for j in (1, 3, 2):
        send(mine, mine, ss.at[2], zs.at[24 + j], ypeer(j))
    for k in (2, 6, 1, 7):
        send(mine, mine, ss.at[0], zs.at[k], zpeer(k))
    for k in (1, 3, 2):
        send(my_tgt, my_tgt, ss.at[1], xs.at[k], xpeer(k))
    send(my_tgt, my_tgt, ss.at[3], rs.at[3], mate)
    sent.append((src_t.at[pl.ds(0, 13 * 32), :], ss.at[0]))
    sent.append((tgt.at[:, pl.ds(0, 384)], ss.at[1]))
    sent.append((src_t.at[pl.ds(0, 18 * 32), :], ss.at[2]))
    sent.append((tgt.at[:, pl.ds(0, 512)], ss.at[3]))

    def forward_tgt(k):
        got = tgt.at[:, block(2 * ((x + X - k) % X) + core, 128)]
        wait(got, xs.at[k])
        send(got, got, ss.at[3], rs.at[3], mate)

    over_y(2)
    over_y(6)
    over_z(1)
    over_z(3)
    over_z(2)
    over_y(3)
    over_y(5)
    forward_tgt(1)
    forward_tgt(3)
    over_y(4)
    forward_tgt(2)

    wait(tgt.at[:, pl.ds(0, 512)], rs.at[3])
    wait(rot, local.at[2])
    tv = tgt[...].astype(F32)
    tsum = jnp.sum(tv * tv, axis=1, keepdims=True)
    tscale = lax.rsqrt(tsum * (1.0 / D) + 1e-06) * (1.0 / math.sqrt(D))
    u[...] = (dot(tgt[...], rot[...], NT) * tscale).astype(BF16)
    for load in load_ids:
        load.wait()
    logits = jnp.zeros((W, W), F32)
    square = jnp.zeros((1, W), F32)
    for k in Z_NEAR:
        i = (z + Z - k) % Z
        here = src_t.at[block(i, 128)]
        if k in (1, 7):
            wait(mine, zs.at[k])
        if k:
            wait(src_t.at[pl.ds(0, 96)], zs.at[32 + k])
        part = here[...]
        logits = logits + dot(u[:, block(i, 128)], part, NN)
        part = part.astype(F32)
        square = square + jnp.sum(part * part, axis=0, keepdims=True)
    sscale = lax.rsqrt(square * (1.0 / D) + 1e-06) * (1.0 / math.sqrt(D))
    kt[...] = jnp.exp(logits * (sscale * (1.0 / 0.03))).astype(BF16)

    row8 = lax.broadcasted_iota(jnp.int32, (8, W), 0)

    def matvec(v, matrix):
        high = v.astype(BF16).astype(F32)
        both = jnp.where(row8 == 0, high, jnp.where(row8 == 1, v - high, 0.0)).astype(BF16)
        return jnp.sum(dot(both, matrix[...], NN), axis=0, keepdims=True)

    def meanwhile():
        at = lax.broadcasted_iota(jnp.int32, (128, 128), 0)
        step = jnp.zeros((128, 128), jnp.int32)
        for i, k in enumerate(Z_ORDER):
            step = jnp.where(at // 16 == i, k, step)
        to = 32 * (at // 4 % 4) + 4 * ((z + step) % Z) + at % 4
        order = (lax.broadcasted_iota(jnp.int32, (128, 128), 1) == to).astype(BF16)
        for i in range(ROWS):
            natural = [src_t[128 * j + 32 * (i // 2):128 * j + 32 * (i // 2) + 32]
                       for j in range(4 * (i % 2), 4 * (i % 2) + 4)]
            ordered[i] = dot(order, jnp.concatenate(natural, axis=0), NN).astype(BF16)
        for j in range(X):
            send(ordered.at[2 * j + (1 - core)], ord_mate.at[j], ss.at[19], xs.at[5], mate)
        sent.append((ord_mate, ss.at[19]))

    def sum_col(part, it):
        colbuf[it, c] = part

        for d in COL_ORDER:
            send(colbuf.at[it, c], colbuf.at[it, c], ss.at[4 + it], rs.at[4 + it], colpeer(d))
        sent.append((colbuf.at[it, pl.ds(0, COLS - 1)], ss.at[4 + it]))
        if it == 0:
            send(kt, kt_mate, ss.at[10], xs.at[4], mate)
            sent.append((kt_mate, ss.at[10]))
            kst[...] = jnp.transpose(kt[...])
            tscale_row[...] = jnp.transpose(jnp.broadcast_to(tscale, (W, 128)))[0:1, :]
        elif it == 1:
            meanwhile()
        wait(colbuf.at[it, pl.ds(0, COLS - 1)], rs.at[4 + it])
        return add_up([colbuf[it, i] for i in range(COLS)])

    def start_row(part, it):
        rowbuf[it, r] = part
        for d in ROW_ORDER:
            send(rowbuf.at[it, r], rowbuf.at[it, r], ss.at[7 + it], rs.at[7 + it], rowpeer(d))
        sent.append((rowbuf.at[it, pl.ds(0, ROWS - 1)], ss.at[7 + it]))

    def end_row(it):
        wait(rowbuf.at[it, pl.ds(0, ROWS - 1)], rs.at[7 + it])
        return add_up([rowbuf[it, i] for i in range(ROWS)])

    src_mass = lax.rsqrt(1000.0 + ids[0].astype(F32))
    tgt_mass = lax.rsqrt(1000.0 + ids[1].astype(F32))
    tgt_scale = jnp.ones((1, W), F32)
    for it in range(ITERS):
        src_scale = src_mass / sum_col(matvec(tgt_scale, kt), it)
        if it < ITERS - 1:
            start_row(matvec(src_scale, kst), it)
            tgt_scale = tgt_mass / end_row(it)

    wait(kt_mate, xs.at[4])
    wait(ord_mate, xs.at[5])
    src_factor[0] = src_scale * sscale
    send(src_factor.at[0], src_factor.at[1], ss.at[20], xs.at[6], mate)
    sent.append((src_factor.at[0], ss.at[20]))
    plan[0] = (kt[...].astype(F32) * src_factor[0]).astype(BF16)

    def some_rows(h, i):
        first = pl.ds(ROWS_IN * h, ROWS_IN)
        rows_of = [ordered[2 * ((x + j) % X) + core, first] if i == 0 else ord_mate[(x + j) % X, first] for j in range(X)]
        return dot(jnp.concatenate(rows_of, axis=0), plan[i], NT)

    first_part = some_rows(0, 0)
    wait(src_factor.at[1], xs.at[6])
    plan[1] = (kt_mate[...].astype(F32) * src_factor[1]).astype(BF16)
    kept = []
    for h in range(PARTS):
        part = (some_rows(h, 0) if h else first_part) + some_rows(h, 1)
        kept.append(part[0:ROWS_IN])
        for k in (2, 1, 3):
            x_out[h, k - 1] = part[ROWS_IN * k:ROWS_IN * (k + 1)].astype(BF16)
            send(x_out.at[h, k - 1], a_x.at[h, k - 1], ss.at[11], xs.at[12 + h], xpeer(k))
        if h == 0:
            start_row(matvec(src_scale, kst), ITERS - 1)
    sent.append((a_x, ss.at[11]))
    factor = (tgt_mass / end_row(ITERS - 1)) * tscale_row[...]

    for h in range(PARTS):
        wait(a_x.at[h], xs.at[12 + h])
        total = kept[h] + ((a_x[h, 0].astype(F32) + a_x[h, 1].astype(F32)) + a_x[h, 2].astype(F32))
        total = (total * factor).astype(BF16)
        for j in XY_ORDER:
            y_out[h, j - 1] = dot(total, tgt[:, block((y + j) % Y, 256)], NN).astype(BF16)
            send(y_out.at[h, j - 1], yb.at[h, j - 1], ss.at[12], xs.at[20 + h], ypeer(j))
        y_mine[h] = dot(total, tgt[:, block(y, 256)], NN)
    sent.append((yb, ss.at[12]))
    for h in range(PARTS):
        wait(yb.at[h], xs.at[20 + h])
        part = (y_mine[h] + yb[h, 0].astype(F32)) + (yb[h, 1].astype(F32) + yb[h, 2].astype(F32))
        for i in range(CHUNKS):
            own = part[16 * i:16 * (i + 1)]
            k = (Z_ORDER + (0,))[CHUNKS * h + i]
            if k:
                z_out[k - 1] = own.astype(BF16)
                send(z_out.at[k - 1], zb.at[k - 1], ss.at[13], rs.at[13], zpeer(k))
    sent.append((zb, ss.at[13]))
    wait(zb, rs.at[13])
    own = own + jnp.sum(zb[...].astype(F32), axis=0)

    def cell(i, j):
        return xr.at[block(i, 16), block(j, 256)]

    xr[block(z, 16), block(y, 256)] = own.astype(BF16)
    for k in Z_ORDER:
        send(cell(z, y), cell(z, y), ss.at[14], zs.at[16 + k], zpeer(k))
    sent.append((xr.at[pl.ds(0, 112), pl.ds(0, 256)], ss.at[14]))
    for j in XY_ORDER:
        send(cell(z, y), cell(z, y), ss.at[16], rs.at[16], ypeer(j))
    for j in range(Y):
        own4[j] = own[4 * j:4 * (j + 1)]
    for d in PLANE_ORDER:
        send(own4.at[(y + d[2]) % Y], req.at[Y * r + y], ss.at[15], rs.at[15], planepeer(d))
    sent.append((req.at[pl.ds(0, ROWS * Y - 1)], ss.at[15]))
    req[Y * r + y] = own4[y]
    for k in (1, 7, 2, 6, 3, 5, 4):
        got = cell((z + Z - k) % Z, y)
        wait(got, zs.at[16 + k])
        for j in XY_ORDER:
            send(got, got, ss.at[16], rs.at[16], ypeer(j))
    sent.append((xr.at[pl.ds(0, 96), :], ss.at[16]))
    wait(req.at[pl.ds(0, ROWS * Y - 1)], rs.at[15])
    for i in range(ROWS):
        for j in range(Y):
            rows[4 * i:4 * (i + 1), 256 * j:256 * (j + 1)] = req[Y * i + j]
    wait(xr.at[pl.ds(0, 96), :], rs.at[16])

    xv = xr[...].astype(F32)
    square = jnp.sum(jnp.sum(xv * xv, axis=0, keepdims=True), axis=1, keepdims=True)
    squares[r] = jnp.broadcast_to(square, (1, 128))
    earlier = list(sent)
    sent.clear()
    for d in ROW_ORDER:
        send(squares.at[r], squares.at[r], ss.at[18], rs.at[18], rowpeer(d))
    sent.append((squares.at[pl.ds(0, ROWS - 1)], ss.at[18]))
    gram = dot(rows[...].astype(BF16), xr[...], NT) * (1.0 / (square * (1.0 / (128 * D)) + 1e-30))
    cubic = dot(gram.astype(BF16), xr[...], NN)
    for i in range(ROWS):
        for j in range(Y):
            stack[i, 4 * j:4 * (j + 1)] = cubic[4 * i:4 * (i + 1), 256 * j:256 * (j + 1)]
    c_out[...] = stack[...].astype(BF16)
    for d in ROW_ORDER:
        peer = rowpeer(d)
        send(c_out.at[peer[0]], c_in.at[r], ss.at[17], rs.at[17], peer)
    sent.append((c_in.at[pl.ds(0, ROWS - 1)], ss.at[17]))
    c_in[r] = c_out[r]
    for ref, sem in earlier:
        wait(ref, sem)
    linear = jnp.concatenate([req[Y * r + j] for j in range(Y)], axis=1)
    wait(squares.at[pl.ds(0, ROWS - 1)], rs.at[18])
    each = [squares[i][:, 0:1] for i in range(ROWS)]
    mean = add_up(each) * (1.0 / (D * D)) + 1e-30
    inverse = 1.0 / (mean * (4.0 * D))
    scale = lax.rsqrt(mean) * (1.0 / (2.0 * math.sqrt(D)))
    wait(c_in.at[pl.ds(0, ROWS - 1)], rs.at[17])
    cubic = add_up([
        c_in[i].astype(F32) * ((each[i] * (1.0 / (128 * D)) + 1e-30) * inverse) for i in range(ROWS)])
    cubic = jnp.concatenate([cubic[4 * j:4 * (j + 1)] for j in range(Y)], axis=1)
    out_ref[...] = (math.sqrt(D) * scale) * (1.5 * linear - 0.5 * cubic)
    finish()


def shards(src_emb, tgt_emb, rotation, src_ids, tgt_ids):
    vmem = pltpu.VMEM
    scratch = [
        vmem((D, W), BF16),
        vmem((ROWS, 128, W), BF16),
        vmem((W, D), BF16),
        vmem((D, D), BF16),
        vmem((W, D), BF16),
        vmem((W, W), BF16),
        vmem((W, W), BF16),
        vmem((2, 1, W), jnp.int32),
        vmem((ITERS, COLS, 1, W), F32),
        vmem((ITERS, ROWS, 1, W), F32),
        vmem((W, W), BF16),
        vmem((X, 128, W), BF16),
        vmem((2, 1, W), F32),
        vmem((1, W), F32),
        vmem((2, W, W), BF16),
        vmem((PARTS, X - 1, ROWS_IN, W), BF16),
        vmem((PARTS, X - 1, ROWS_IN, W), BF16),
        vmem((PARTS, Y - 1, ROWS_IN, 256), BF16),
        vmem((PARTS, Y - 1, ROWS_IN, 256), BF16),
        vmem((PARTS, ROWS_IN, 256), F32),
        vmem((Z - 1, 16, 256), BF16),
        vmem((Z - 1, 16, 256), BF16),
        vmem((128, D), BF16),
        vmem((Y, 4, 256), F32),
        vmem((ROWS * Y, 4, 256), F32),
        vmem((32, D), F32),
        vmem((ROWS, 16, 256), F32),
        vmem((ROWS, 1, 128), F32),
        vmem((ROWS, 16, 256), BF16),
        vmem((ROWS, 16, 256), BF16),
        pltpu.SemaphoreType.DMA((5,)),
        pltpu.SemaphoreType.DMA((40,)),
        pltpu.SemaphoreType.DMA((28,)),
        pltpu.SemaphoreType.DMA((21,)),
        pltpu.SemaphoreType.DMA((21,)),
    ]
    hbm = pl.BlockSpec(memory_space=pltpu.HBM)
    here = pl.BlockSpec(memory_space=pltpu.VMEM)
    return pl.pallas_call(
        body,
        out_shape=pltpu.VMEM((4, D), F32),
        in_specs=[hbm] * 5,
        out_specs=here,
        scratch_shapes=scratch,
        compiler_params=pltpu.CompilerParams(
            collective_id=0, has_side_effects=True, vmem_limit_bytes=60 * 2**20
        ),
        name="procrustes",
    )(src_emb.T, tgt_emb, rotation, src_ids.reshape(1, W), tgt_ids.reshape(1, W))


def solution(mesh):
    return jax.shard_map(
        shards,
        mesh=mesh,
        in_specs=(P("row", "col"), P("col", "row"), P(), P("row"), P("col")),
        out_specs=P(("row", "col"), None),
        check_vma=False,
    )
```

```python
import math

import jax
import jax.numpy as jnp
from jax import lax
from jax.experimental import pallas as pl
from jax.experimental.pallas import tpu as pltpu
from jax.sharding import PartitionSpec as P

MESH = pl.DeviceIdType.MESH
F32 = jnp.float32
BF16 = jnp.bfloat16
D = 1024
W = 512
ITERS = 3
X, Y, Z = 4, 4, 8
ROWS, COLS = 2 * X, Y * Z


def hops(step, size):
    return min(step, size - step)


COL_ORDER = sorted(
    ((dy, dz) for dy in range(Y) for dz in range(Z) if dy or dz),
    key=lambda d: -hops(d[0], Y) - hops(d[1], Z))
PLANE_ORDER = sorted(
    ((dx, dk, dy) for dx in range(X) for dk in range(2) for dy in range(Y) if dx or dk or dy),
    key=lambda d: -2 * hops(d[0], X) - 3 * d[1] - 2 * hops(d[2], Y))
ROW_ORDER = [d[:2] for d in PLANE_ORDER if d[2] == 0]
Z_ORDER = (4, 3, 5, 2, 6, 1, 7)
Z_NEAR = (0, 2, 6, 1, 7, 3, 5, 4)
PARTS = 4
ROWS_IN = 128 // PARTS
CHUNKS = Z // PARTS
XY_ORDER = (2, 1, 3)
NN = (((1,), (0,)), ((), ()))
NT = (((1,), (1,)), ((), ()))


def dot(a, b, dims):
    return lax.dot_general(a, b, dims, preferred_element_type=F32)


def send(src, dst, send_sem, recv_sem, device):
    pltpu.make_async_remote_copy(
        src_ref=src, dst_ref=dst, send_sem=send_sem, recv_sem=recv_sem,
        device_id=device, device_id_type=MESH,
    ).start()


def wait(ref, sem):
    pltpu.make_async_copy(ref, ref, sem).wait()


def add_up(parts):
    while len(parts) > 1:
        parts = [a + b for a, b in zip(parts[::2], parts[1::2])]
    return parts[0]


def block(i, size):
    return pl.ds(pl.multiple_of(i * size, size), size)


def body(src_hbm, tgt_hbm, rot_hbm, src_ids, tgt_ids, out_ref,
         src_t, ordered, tgt, rot, u, kt, kst, ids, colbuf, rowbuf,
         kt_mate, ord_mate, src_factor, tscale_row, plan, a_x, x_out, yb, y_out, y_mine, zb, z_out, xr, own4, req, rows, stack, squares, c_out, c_in,
         local, zs, xs, ss, rs):
    sent = []

    def finish():
        for ref, sem in sent:
            wait(ref, sem)

    r, c = lax.axis_index("row"), lax.axis_index("col")
    x, core = r // 2, r % 2
    y, z = c // Z, c % Z
    mate = (2 * x + (1 - core), c)

    def xpeer(k):
        return (2 * ((x + k) % X) + core, c)

    def ypeer(k):
        return (r, Z * ((y + k) % Y) + z)

    def zpeer(k):
        return (r, Z * y + (z + k) % Z)

    def colpeer(d):
        return (r, Z * ((y + d[0]) % Y) + (z + d[1]) % Z)

    def rowpeer(d):
        return (2 * ((x + d[0]) % X) + (core + d[1]) % 2, c)

    def planepeer(d):
        return (rowpeer(d)[0], Z * ((y + d[2]) % Y) + z)

    def feature(i, j):
        return pl.ds(pl.multiple_of(128 * i + 32 * j, 32), 32)

    mine = src_t.at[feature(z, y)]
    load_src = pltpu.make_async_copy(src_hbm, mine, local.at[0])
    load_src.start()
    my_tgt = tgt.at[:, block(r, 128)]
    load_tgt = pltpu.make_async_copy(tgt_hbm, my_tgt, local.at[1])
    load_tgt.start()
    for i in range(Z):
        for j in range(Y):
            pltpu.make_async_copy(
                rot_hbm.at[pl.ds(32 * (Z * j + i), 32)], rot.at[pl.ds(128 * i + 32 * j, 32)], local.at[2]).start()
    load_ids = [pltpu.make_async_copy(ref, ids.at[i], local.at[3 + i]) for i, ref in enumerate((src_ids, tgt_ids))]
    for load in load_ids:
        load.start()
    bar = pltpu.get_barrier_semaphore()

    near = [zpeer(k) for k in (2, 6, 1, 7)] + [xpeer(k) for k in XY_ORDER] + [ypeer(k) for k in XY_ORDER] + [mate]
    for device in near:
        pl.semaphore_signal(bar, inc=1, device_id=device, device_id_type=MESH)
    load_src.wait()
    load_tgt.wait()
    pl.semaphore_wait(bar, len(near))

    def over_y(k):
        got = src_t.at[feature((z + Z - k) % Z, y)]
        wait(mine, zs.at[k])
        if k in (2, 6):
            send(got, got, ss.at[0], zs.at[3 if k == 2 else 5], zpeer(1 if k == 2 else 7))
            half = src_t.at[feature((z + Z - k) % Z, y), pl.ds(0 if k == 2 else W // 2, W // 2)]
            send(half, half, ss.at[0], zs.at[4], zpeer(k))
        for j in (1, 3, 2):
            send(got, got, ss.at[2], zs.at[32 + k], ypeer(j))

    def over_z(j):
        got = src_t.at[feature(z, (y + Y - j) % Y)]
        wait(got, zs.at[24 + j])
        for k in (1, 7):
            send(got, got, ss.at[0], zs.at[32 + k], zpeer(k))

    for j in (1, 3, 2):
        send(mine, mine, ss.at[2], zs.at[24 + j], ypeer(j))
    for k in (2, 6, 1, 7):
        send(mine, mine, ss.at[0], zs.at[k], zpeer(k))
    for k in (1, 3, 2):
        send(my_tgt, my_tgt, ss.at[1], xs.at[k], xpeer(k))
    send(my_tgt, my_tgt, ss.at[3], rs.at[3], mate)
    sent.append((src_t.at[pl.ds(0, 13 * 32), :], ss.at[0]))
    sent.append((tgt.at[:, pl.ds(0, 384)], ss.at[1]))
    sent.append((src_t.at[pl.ds(0, 18 * 32), :], ss.at[2]))
    sent.append((tgt.at[:, pl.ds(0, 512)], ss.at[3]))

    def forward_tgt(k):
        got = tgt.at[:, block(2 * ((x + X - k) % X) + core, 128)]
        wait(got, xs.at[k])
        send(got, got, ss.at[3], rs.at[3], mate)

    over_y(2)
    over_y(6)
    over_z(1)
    over_z(3)
    over_z(2)
    over_y(3)
    over_y(5)
    forward_tgt(1)
    forward_tgt(3)
    over_y(4)
    forward_tgt(2)

    wait(tgt.at[:, pl.ds(0, 512)], rs.at[3])
    wait(rot, local.at[2])
    tv = tgt[...].astype(F32)
    tsum = jnp.sum(tv * tv, axis=1, keepdims=True)
    tscale = lax.rsqrt(tsum * (1.0 / D) + 1e-06) * (1.0 / math.sqrt(D))
    u[...] = (dot(tgt[...], rot[...], NT) * tscale).astype(BF16)
    for load in load_ids:
        load.wait()
    logits = jnp.zeros((W, W), F32)
    square = jnp.zeros((1, W), F32)
    for k in Z_NEAR:
        i = (z + Z - k) % Z
        here = src_t.at[block(i, 128)]
        if k in (1, 7):
            wait(mine, zs.at[k])
        if k:
            wait(src_t.at[pl.ds(0, 96)], zs.at[32 + k])
        part = here[...]
        logits = logits + dot(u[:, block(i, 128)], part, NN)
        part = part.astype(F32)
        square = square + jnp.sum(part * part, axis=0, keepdims=True)
    sscale = lax.rsqrt(square * (1.0 / D) + 1e-06) * (1.0 / math.sqrt(D))
    kt[...] = jnp.exp(logits * (sscale * (1.0 / 0.03))).astype(BF16)

    row8 = lax.broadcasted_iota(jnp.int32, (8, W), 0)

    def matvec(v, matrix):
        high = v.astype(BF16).astype(F32)
        both = jnp.where(row8 == 0, high, jnp.where(row8 == 1, v - high, 0.0)).astype(BF16)
        return jnp.sum(dot(both, matrix[...], NN), axis=0, keepdims=True)

    def meanwhile():
        at = lax.broadcasted_iota(jnp.int32, (128, 128), 0)
        step = jnp.zeros((128, 128), jnp.int32)
        for i, k in enumerate(Z_ORDER):
            step = jnp.where(at // 16 == i, k, step)
        to = 32 * (at // 4 % 4) + 4 * ((z + step) % Z) + at % 4
        order = (lax.broadcasted_iota(jnp.int32, (128, 128), 1) == to).astype(BF16)
        for i in range(ROWS):
            natural = [src_t[128 * j + 32 * (i // 2):128 * j + 32 * (i // 2) + 32]
                       for j in range(4 * (i % 2), 4 * (i % 2) + 4)]
            ordered[i] = dot(order, jnp.concatenate(natural, axis=0), NN).astype(BF16)
        for j in range(X):
            send(ordered.at[2 * j + (1 - core)], ord_mate.at[j], ss.at[19], xs.at[5], mate)
        sent.append((ord_mate, ss.at[19]))

    def sum_col(part, it):
        colbuf[it, c] = part

        for d in COL_ORDER:
            send(colbuf.at[it, c], colbuf.at[it, c], ss.at[4 + it], rs.at[4 + it], colpeer(d))
        sent.append((colbuf.at[it, pl.ds(0, COLS - 1)], ss.at[4 + it]))
        if it == 0:
            send(kt, kt_mate, ss.at[10], xs.at[4], mate)
            sent.append((kt_mate, ss.at[10]))
            kst[...] = jnp.transpose(kt[...])
            tscale_row[...] = jnp.transpose(jnp.broadcast_to(tscale, (W, 128)))[0:1, :]
        elif it == 1:
            meanwhile()
        wait(colbuf.at[it, pl.ds(0, COLS - 1)], rs.at[4 + it])
        return add_up([colbuf[it, i] for i in range(COLS)])

    def start_row(part, it):
        rowbuf[it, r] = part
        for d in ROW_ORDER:
            send(rowbuf.at[it, r], rowbuf.at[it, r], ss.at[7 + it], rs.at[7 + it], rowpeer(d))
        sent.append((rowbuf.at[it, pl.ds(0, ROWS - 1)], ss.at[7 + it]))

    def end_row(it):
        wait(rowbuf.at[it, pl.ds(0, ROWS - 1)], rs.at[7 + it])
        return add_up([rowbuf[it, i] for i in range(ROWS)])

    src_mass = lax.rsqrt(1000.0 + ids[0].astype(F32))
    tgt_mass = lax.rsqrt(1000.0 + ids[1].astype(F32))
    tgt_scale = jnp.ones((1, W), F32)
    for it in range(ITERS):
        src_scale = src_mass / sum_col(matvec(tgt_scale, kt), it)
        if it < ITERS - 1:
            start_row(matvec(src_scale, kst), it)
            tgt_scale = tgt_mass / end_row(it)

    wait(kt_mate, xs.at[4])
    wait(ord_mate, xs.at[5])
    src_factor[0] = src_scale * sscale
    send(src_factor.at[0], src_factor.at[1], ss.at[20], xs.at[6], mate)
    sent.append((src_factor.at[0], ss.at[20]))
    plan[0] = (kt[...].astype(F32) * src_factor[0]).astype(BF16)

    def some_rows(h, i):
        first = pl.ds(ROWS_IN * h, ROWS_IN)
        rows_of = [ordered[2 * ((x + j) % X) + core, first] if i == 0 else ord_mate[(x + j) % X, first] for j in range(X)]
        return dot(jnp.concatenate(rows_of, axis=0), plan[i], NT)

    first_part = some_rows(0, 0)
    wait(src_factor.at[1], xs.at[6])
    plan[1] = (kt_mate[...].astype(F32) * src_factor[1]).astype(BF16)
    kept = []
    for h in range(PARTS):
        part = (some_rows(h, 0) if h else first_part) + some_rows(h, 1)
        kept.append(part[0:ROWS_IN])
        for k in (2, 1, 3):
            x_out[h, k - 1] = part[ROWS_IN * k:ROWS_IN * (k + 1)].astype(BF16)
            send(x_out.at[h, k - 1], a_x.at[h, k - 1], ss.at[11], xs.at[12 + h], xpeer(k))
        if h == 0:
            start_row(matvec(src_scale, kst), ITERS - 1)
    sent.append((a_x, ss.at[11]))
    factor = (tgt_mass / end_row(ITERS - 1)) * tscale_row[...]

    for h in range(PARTS):
        wait(a_x.at[h], xs.at[12 + h])
        total = kept[h] + ((a_x[h, 0].astype(F32) + a_x[h, 1].astype(F32)) + a_x[h, 2].astype(F32))
        total = (total * factor).astype(BF16)
        for j in XY_ORDER:
            y_out[h, j - 1] = dot(total, tgt[:, block((y + j) % Y, 256)], NN).astype(BF16)
            send(y_out.at[h, j - 1], yb.at[h, j - 1], ss.at[12], xs.at[20 + h], ypeer(j))
        y_mine[h] = dot(total, tgt[:, block(y, 256)], NN)
    sent.append((yb, ss.at[12]))
    for h in range(PARTS):
        wait(yb.at[h], xs.at[20 + h])
        part = (y_mine[h] + yb[h, 0].astype(F32)) + (yb[h, 1].astype(F32) + yb[h, 2].astype(F32))
        for i in range(CHUNKS):
            own = part[16 * i:16 * (i + 1)]
            k = (Z_ORDER + (0,))[CHUNKS * h + i]
            if k:
                z_out[k - 1] = own.astype(BF16)
                send(z_out.at[k - 1], zb.at[k - 1], ss.at[13], rs.at[13], zpeer(k))
    sent.append((zb, ss.at[13]))
    wait(zb, rs.at[13])
    own = own + jnp.sum(zb[...].astype(F32), axis=0)

    xr[c] = own.astype(BF16)
    for d in COL_ORDER:
        send(xr.at[c], xr.at[c], ss.at[14], rs.at[14], colpeer(d))
    sent.append((xr.at[pl.ds(0, COLS - 1)], ss.at[14]))
    for j in range(Y):
        own4[j] = own[4 * j:4 * (j + 1)]
    for d in PLANE_ORDER:
        send(own4.at[(y + d[2]) % Y], req.at[Y * r + y], ss.at[15], rs.at[15], planepeer(d))
    sent.append((req.at[pl.ds(0, ROWS * Y - 1)], ss.at[15]))
    req[Y * r + y] = own4[y]
    wait(req.at[pl.ds(0, ROWS * Y - 1)], rs.at[15])
    for i in range(ROWS):
        for j in range(Y):
            rows[4 * i:4 * (i + 1), 256 * j:256 * (j + 1)] = req[Y * i + j]
    wait(xr.at[pl.ds(0, COLS - 1)], rs.at[14])

    lanes = [xr[Z * j:Z * (j + 1)].reshape(128, 256) for j in range(Y)]
    square = add_up([jnp.sum(v.astype(F32) * v.astype(F32), axis=0, keepdims=True) for v in lanes])
    square = jnp.sum(square, axis=1, keepdims=True)
    squares[r] = jnp.broadcast_to(square, (1, 128))
    earlier = list(sent)
    sent.clear()
    for d in ROW_ORDER:
        send(squares.at[r], squares.at[r], ss.at[18], rs.at[18], rowpeer(d))
    sent.append((squares.at[pl.ds(0, ROWS - 1)], ss.at[18]))
    gram = add_up([dot(rows[:, 256 * j:256 * (j + 1)].astype(BF16), lanes[j], NT) for j in range(Y)])
    gram = (gram * (1.0 / (square * (1.0 / (128 * D)) + 1e-30))).astype(BF16)
    for j in range(Y):
        cubic = dot(gram, lanes[j], NN)
        for i in range(ROWS):
            stack[i, 4 * j:4 * (j + 1)] = cubic[4 * i:4 * (i + 1)]
    c_out[...] = stack[...].astype(BF16)
    for d in ROW_ORDER:
        peer = rowpeer(d)
        send(c_out.at[peer[0]], c_in.at[r], ss.at[17], rs.at[17], peer)
    sent.append((c_in.at[pl.ds(0, ROWS - 1)], ss.at[17]))
    c_in[r] = c_out[r]
    for ref, sem in earlier:
        wait(ref, sem)
    linear = jnp.concatenate([req[Y * r + j] for j in range(Y)], axis=1)
    wait(squares.at[pl.ds(0, ROWS - 1)], rs.at[18])
    each = [squares[i][:, 0:1] for i in range(ROWS)]
    mean = add_up(each) * (1.0 / (D * D)) + 1e-30
    inverse = 1.0 / (mean * (4.0 * D))
    scale = lax.rsqrt(mean) * (1.0 / (2.0 * math.sqrt(D)))
    wait(c_in.at[pl.ds(0, ROWS - 1)], rs.at[17])
    cubic = add_up([
        c_in[i].astype(F32) * ((each[i] * (1.0 / (128 * D)) + 1e-30) * inverse) for i in range(ROWS)])
    cubic = jnp.concatenate([cubic[4 * j:4 * (j + 1)] for j in range(Y)], axis=1)
    out_ref[...] = (math.sqrt(D) * scale) * (1.5 * linear - 0.5 * cubic)
    finish()


def shards(src_emb, tgt_emb, rotation, src_ids, tgt_ids):
    vmem = pltpu.VMEM
    scratch = [
        vmem((D, W), BF16),
        vmem((ROWS, 128, W), BF16),
        vmem((W, D), BF16),
        vmem((D, D), BF16),
        vmem((W, D), BF16),
        vmem((W, W), BF16),
        vmem((W, W), BF16),
        vmem((2, 1, W), jnp.int32),
        vmem((ITERS, COLS, 1, W), F32),
        vmem((ITERS, ROWS, 1, W), F32),
        vmem((W, W), BF16),
        vmem((X, 128, W), BF16),
        vmem((2, 1, W), F32),
        vmem((1, W), F32),
        vmem((2, W, W), BF16),
        vmem((PARTS, X - 1, ROWS_IN, W), BF16),
        vmem((PARTS, X - 1, ROWS_IN, W), BF16),
        vmem((PARTS, Y - 1, ROWS_IN, 256), BF16),
        vmem((PARTS, Y - 1, ROWS_IN, 256), BF16),
        vmem((PARTS, ROWS_IN, 256), F32),
        vmem((Z - 1, 16, 256), BF16),
        vmem((Z - 1, 16, 256), BF16),
        vmem((COLS, 16, 256), BF16),
        vmem((Y, 4, 256), F32),
        vmem((ROWS * Y, 4, 256), F32),
        vmem((32, D), F32),
        vmem((ROWS, 16, 256), F32),
        vmem((ROWS, 1, 128), F32),
        vmem((ROWS, 16, 256), BF16),
        vmem((ROWS, 16, 256), BF16),
        pltpu.SemaphoreType.DMA((5,)),
        pltpu.SemaphoreType.DMA((40,)),
        pltpu.SemaphoreType.DMA((28,)),
        pltpu.SemaphoreType.DMA((21,)),
        pltpu.SemaphoreType.DMA((21,)),
    ]
    hbm = pl.BlockSpec(memory_space=pltpu.HBM)
    here = pl.BlockSpec(memory_space=pltpu.VMEM)
    return pl.pallas_call(
        body,
        out_shape=pltpu.VMEM((4, D), F32),
        in_specs=[hbm] * 5,
        out_specs=here,
        scratch_shapes=scratch,
        compiler_params=pltpu.CompilerParams(
            collective_id=0, has_side_effects=True, vmem_limit_bytes=60 * 2**20
        ),
        name="procrustes",
    )(src_emb.T, tgt_emb, rotation, src_ids.reshape(1, W), tgt_ids.reshape(1, W))


def solution(mesh):
    return jax.shard_map(
        shards,
        mesh=mesh,
        in_specs=(P("row", "col"), P("col", "row"), P(), P("row"), P("col")),
        out_specs=P(("row", "col"), None),
        check_vma=False,
    )
```

```python
import math

import jax
import jax.numpy as jnp
from jax import lax
from jax.experimental import pallas as pl
from jax.experimental.pallas import tpu as pltpu
from jax.sharding import PartitionSpec as P

MESH = pl.DeviceIdType.MESH
F32 = jnp.float32
BF16 = jnp.bfloat16
D = 1024
W = 512
ITERS = 3
X, Y, Z = 4, 4, 8
ROWS, COLS = 2 * X, Y * Z


def hops(step, size):
    return min(step, size - step)


COL_ORDER = sorted(
    ((dy, dz) for dy in range(Y) for dz in range(Z) if dy or dz),
    key=lambda d: -hops(d[0], Y) - hops(d[1], Z))
PLANE_ORDER = sorted(
    ((dx, dk, dy) for dx in range(X) for dk in range(2) for dy in range(Y) if dx or dk or dy),
    key=lambda d: -2 * hops(d[0], X) - 3 * d[1] - 2 * hops(d[2], Y))
ROW_ORDER = [d[:2] for d in PLANE_ORDER if d[2] == 0]
Z_ORDER = (4, 3, 5, 2, 6, 1, 7)
Z_NEAR = (0, 2, 6, 1, 7, 3, 5, 4)
PARTS = 4
ROWS_IN = 128 // PARTS
CHUNKS = Z // PARTS
XY_ORDER = (2, 1, 3)
NN = (((1,), (0,)), ((), ()))
NT = (((1,), (1,)), ((), ()))


def dot(a, b, dims):
    return lax.dot_general(a, b, dims, preferred_element_type=F32)


def send(src, dst, send_sem, recv_sem, device):
    pltpu.make_async_remote_copy(
        src_ref=src, dst_ref=dst, send_sem=send_sem, recv_sem=recv_sem,
        device_id=device, device_id_type=MESH,
    ).start()


def wait(ref, sem):
    pltpu.make_async_copy(ref, ref, sem).wait()


def add_up(parts):
    while len(parts) > 1:
        parts = [a + b for a, b in zip(parts[::2], parts[1::2])]
    return parts[0]


def block(i, size):
    return pl.ds(pl.multiple_of(i * size, size), size)


def body(src_hbm, tgt_hbm, rot_hbm, src_ids, tgt_ids, out_ref,
         src_t, ordered, tgt, rot, u, kt, kst, ids, colbuf, rowbuf,
         kt_mate, ord_mate, src_factor, plan, a_x, x_out, yb, y_out, y_mine, zb, z_out, xr, own4, req, rows, stack, squares, c_out, c_in,
         local, zs, xs, ss, rs):
    sent = []

    def finish():
        for ref, sem in sent:
            wait(ref, sem)

    r, c = lax.axis_index("row"), lax.axis_index("col")
    x, core = r // 2, r % 2
    y, z = c // Z, c % Z
    mate = (2 * x + (1 - core), c)

    def xpeer(k):
        return (2 * ((x + k) % X) + core, c)

    def ypeer(k):
        return (r, Z * ((y + k) % Y) + z)

    def zpeer(k):
        return (r, Z * y + (z + k) % Z)

    def colpeer(d):
        return (r, Z * ((y + d[0]) % Y) + (z + d[1]) % Z)

    def rowpeer(d):
        return (2 * ((x + d[0]) % X) + (core + d[1]) % 2, c)

    def planepeer(d):
        return (rowpeer(d)[0], Z * ((y + d[2]) % Y) + z)

    def feature(i, j):
        return pl.ds(pl.multiple_of(128 * i + 32 * j, 32), 32)

    mine = src_t.at[feature(z, y)]
    load_src = pltpu.make_async_copy(src_hbm, mine, local.at[0])
    load_src.start()
    my_tgt = tgt.at[:, block(r, 128)]
    load_tgt = pltpu.make_async_copy(tgt_hbm, my_tgt, local.at[1])
    load_tgt.start()
    for i in range(Z):
        for j in range(Y):
            pltpu.make_async_copy(
                rot_hbm.at[pl.ds(32 * (Z * j + i), 32)], rot.at[pl.ds(128 * i + 32 * j, 32)], local.at[2]).start()
    load_ids = [pltpu.make_async_copy(ref, ids.at[i], local.at[3 + i]) for i, ref in enumerate((src_ids, tgt_ids))]
    for load in load_ids:
        load.start()
    bar = pltpu.get_barrier_semaphore()

    near = [zpeer(k) for k in (2, 6, 1, 7)] + [xpeer(k) for k in XY_ORDER] + [ypeer(k) for k in XY_ORDER] + [mate]
    for device in near:
        pl.semaphore_signal(bar, inc=1, device_id=device, device_id_type=MESH)
    load_src.wait()
    load_tgt.wait()
    pl.semaphore_wait(bar, len(near))

    def over_y(k):
        got = src_t.at[feature((z + Z - k) % Z, y)]
        wait(mine, zs.at[k])
        if k in (2, 6):
            send(got, got, ss.at[0], zs.at[3 if k == 2 else 5], zpeer(1 if k == 2 else 7))
            half = src_t.at[feature((z + Z - k) % Z, y), pl.ds(0 if k == 2 else W // 2, W // 2)]
            send(half, half, ss.at[0], zs.at[4], zpeer(k))
        for j in (1, 3, 2):
            send(got, got, ss.at[2], zs.at[32 + k], ypeer(j))

    def over_z(j):
        got = src_t.at[feature(z, (y + Y - j) % Y)]
        wait(got, zs.at[24 + j])
        for k in (1, 7):
            send(got, got, ss.at[0], zs.at[32 + k], zpeer(k))

    for j in (1, 3, 2):
        send(mine, mine, ss.at[2], zs.at[24 + j], ypeer(j))
    for k in (2, 6, 1, 7):
        send(mine, mine, ss.at[0], zs.at[k], zpeer(k))
    for k in (1, 3, 2):
        send(my_tgt, my_tgt, ss.at[1], xs.at[k], xpeer(k))
    send(my_tgt, my_tgt, ss.at[3], rs.at[3], mate)
    sent.append((src_t.at[pl.ds(0, 13 * 32), :], ss.at[0]))
    sent.append((tgt.at[:, pl.ds(0, 384)], ss.at[1]))
    sent.append((src_t.at[pl.ds(0, 18 * 32), :], ss.at[2]))
    sent.append((tgt.at[:, pl.ds(0, 512)], ss.at[3]))

    def forward_tgt(k):
        got = tgt.at[:, block(2 * ((x + X - k) % X) + core, 128)]
        wait(got, xs.at[k])
        send(got, got, ss.at[3], rs.at[3], mate)

    over_y(2)
    over_y(6)
    over_z(1)
    over_z(3)
    over_z(2)
    over_y(3)
    over_y(5)
    forward_tgt(1)
    forward_tgt(3)
    over_y(4)
    forward_tgt(2)

    wait(tgt.at[:, pl.ds(0, 512)], rs.at[3])
    wait(rot, local.at[2])
    tv = tgt[...].astype(F32)
    tsum = jnp.sum(tv * tv, axis=1, keepdims=True)
    tscale = lax.rsqrt(tsum * (1.0 / D) + 1e-06) * (1.0 / math.sqrt(D))
    u[...] = (dot(tgt[...], rot[...], NT) * tscale).astype(BF16)
    for load in load_ids:
        load.wait()
    logits = jnp.zeros((W, W), F32)
    square = jnp.zeros((1, W), F32)
    for k in Z_NEAR:
        i = (z + Z - k) % Z
        here = src_t.at[block(i, 128)]
        if k in (1, 7):
            wait(mine, zs.at[k])
        if k:
            wait(src_t.at[pl.ds(0, 96)], zs.at[32 + k])
        part = here[...]
        logits = logits + dot(u[:, block(i, 128)], part, NN)
        part = part.astype(F32)
        square = square + jnp.sum(part * part, axis=0, keepdims=True)
    sscale = lax.rsqrt(square * (1.0 / D) + 1e-06) * (1.0 / math.sqrt(D))
    kt[...] = jnp.exp(logits * (sscale * (1.0 / 0.03))).astype(BF16)

    row8 = lax.broadcasted_iota(jnp.int32, (8, W), 0)

    def matvec(v, matrix):
        high = v.astype(BF16).astype(F32)
        both = jnp.where(row8 == 0, high, jnp.where(row8 == 1, v - high, 0.0)).astype(BF16)
        return jnp.sum(dot(both, matrix[...], NN), axis=0, keepdims=True)

    def meanwhile():
        at = lax.broadcasted_iota(jnp.int32, (128, 128), 0)
        step = jnp.zeros((128, 128), jnp.int32)
        for i, k in enumerate(Z_ORDER):
            step = jnp.where(at // 16 == i, k, step)
        to = 32 * (at // 4 % 4) + 4 * ((z + step) % Z) + at % 4
        order = (lax.broadcasted_iota(jnp.int32, (128, 128), 1) == to).astype(BF16)
        kst[...] = jnp.transpose(kt[...])
        for i in range(ROWS):
            natural = [src_t[128 * j + 32 * (i // 2):128 * j + 32 * (i // 2) + 32]
                       for j in range(4 * (i % 2), 4 * (i % 2) + 4)]
            ordered[i] = dot(order, jnp.concatenate(natural, axis=0), NN).astype(BF16)
        for j in range(X):
            send(ordered.at[2 * j + (1 - core)], ord_mate.at[j], ss.at[19], xs.at[5], mate)
        sent.append((ord_mate, ss.at[19]))

    def sum_col(part, it):
        colbuf[it, c] = part

        for d in COL_ORDER:
            send(colbuf.at[it, c], colbuf.at[it, c], ss.at[4 + it], rs.at[4 + it], colpeer(d))
        sent.append((colbuf.at[it, pl.ds(0, COLS - 1)], ss.at[4 + it]))
        if it == 0:
            send(kt, kt_mate, ss.at[10], xs.at[4], mate)
            sent.append((kt_mate, ss.at[10]))
            meanwhile()
        wait(colbuf.at[it, pl.ds(0, COLS - 1)], rs.at[4 + it])
        if it == 0:
            wait(kt_mate, xs.at[4])
            wait(ord_mate, xs.at[5])
        return add_up([colbuf[it, i] for i in range(COLS)])

    def start_row(part, it):
        rowbuf[it, r] = part
        for d in ROW_ORDER:
            send(rowbuf.at[it, r], rowbuf.at[it, r], ss.at[7 + it], rs.at[7 + it], rowpeer(d))
        sent.append((rowbuf.at[it, pl.ds(0, ROWS - 1)], ss.at[7 + it]))

    def end_row(it):
        wait(rowbuf.at[it, pl.ds(0, ROWS - 1)], rs.at[7 + it])
        return add_up([rowbuf[it, i] for i in range(ROWS)])

    src_mass = lax.rsqrt(1000.0 + ids[0].astype(F32))
    tgt_mass = lax.rsqrt(1000.0 + ids[1].astype(F32))
    tgt_scale = jnp.ones((1, W), F32)
    for it in range(ITERS):
        src_scale = src_mass / sum_col(matvec(tgt_scale, kt), it)
        if it < ITERS - 1:
            start_row(matvec(src_scale, kst), it)
            tgt_scale = tgt_mass / end_row(it)

    src_factor[0] = src_scale * sscale
    send(src_factor.at[0], src_factor.at[1], ss.at[20], xs.at[6], mate)
    sent.append((src_factor.at[0], ss.at[20]))
    plan[0] = (kt[...].astype(F32) * src_factor[0]).astype(BF16)

    def some_rows(h, i):
        first = pl.ds(ROWS_IN * h, ROWS_IN)
        rows_of = [ordered[2 * ((x + j) % X) + core, first] if i == 0 else ord_mate[(x + j) % X, first] for j in range(X)]
        return dot(jnp.concatenate(rows_of, axis=0), plan[i], NT)

    first_part = some_rows(0, 0)
    start_row(matvec(src_scale, kst), ITERS - 1)
    tscale_l = jnp.transpose(jnp.broadcast_to(tscale, (W, 128)))[0:1, :]
    wait(src_factor.at[1], xs.at[6])
    plan[1] = (kt_mate[...].astype(F32) * src_factor[1]).astype(BF16)
    kept = []
    for h in range(PARTS):
        part = (some_rows(h, 0) if h else first_part) + some_rows(h, 1)
        kept.append(part[0:ROWS_IN])
        for k in (2, 1, 3):
            x_out[h, k - 1] = part[ROWS_IN * k:ROWS_IN * (k + 1)].astype(BF16)
            send(x_out.at[h, k - 1], a_x.at[h, k - 1], ss.at[11], xs.at[12 + h], xpeer(k))
    sent.append((a_x, ss.at[11]))
    factor = (tgt_mass / end_row(ITERS - 1)) * tscale_l

    for h in range(PARTS):
        wait(a_x.at[h], xs.at[12 + h])
        total = kept[h] + ((a_x[h, 0].astype(F32) + a_x[h, 1].astype(F32)) + a_x[h, 2].astype(F32))
        total = (total * factor).astype(BF16)
        for j in XY_ORDER:
            y_out[h, j - 1] = dot(total, tgt[:, block((y + j) % Y, 256)], NN).astype(BF16)
            send(y_out.at[h, j - 1], yb.at[h, j - 1], ss.at[12], xs.at[20 + h], ypeer(j))
        y_mine[h] = dot(total, tgt[:, block(y, 256)], NN)
    sent.append((yb, ss.at[12]))
    for h in range(PARTS):
        wait(yb.at[h], xs.at[20 + h])
        part = (y_mine[h] + yb[h, 0].astype(F32)) + (yb[h, 1].astype(F32) + yb[h, 2].astype(F32))
        for i in range(CHUNKS):
            own = part[16 * i:16 * (i + 1)]
            k = (Z_ORDER + (0,))[CHUNKS * h + i]
            if k:
                z_out[k - 1] = own.astype(BF16)
                send(z_out.at[k - 1], zb.at[k - 1], ss.at[13], rs.at[13], zpeer(k))
    sent.append((zb, ss.at[13]))
    wait(zb, rs.at[13])
    own = own + jnp.sum(zb[...].astype(F32), axis=0)

    xr[c] = own.astype(BF16)
    for d in COL_ORDER:
        send(xr.at[c], xr.at[c], ss.at[14], rs.at[14], colpeer(d))
    sent.append((xr.at[pl.ds(0, COLS - 1)], ss.at[14]))
    for j in range(Y):
        own4[j] = own[4 * j:4 * (j + 1)]
    for d in PLANE_ORDER:
        send(own4.at[(y + d[2]) % Y], req.at[Y * r + y], ss.at[15], rs.at[15], planepeer(d))
    sent.append((req.at[pl.ds(0, ROWS * Y - 1)], ss.at[15]))
    req[Y * r + y] = own4[y]
    wait(req.at[pl.ds(0, ROWS * Y - 1)], rs.at[15])
    for i in range(ROWS):
        for j in range(Y):
            rows[4 * i:4 * (i + 1), 256 * j:256 * (j + 1)] = req[Y * i + j]
    wait(xr.at[pl.ds(0, COLS - 1)], rs.at[14])

    lanes = [xr[Z * j:Z * (j + 1)].reshape(128, 256) for j in range(Y)]
    square = add_up([jnp.sum(v.astype(F32) * v.astype(F32), axis=0, keepdims=True) for v in lanes])
    square = jnp.sum(square, axis=1, keepdims=True)
    squares[r] = jnp.broadcast_to(square, (1, 128))
    earlier = list(sent)
    sent.clear()
    for d in ROW_ORDER:
        send(squares.at[r], squares.at[r], ss.at[18], rs.at[18], rowpeer(d))
    sent.append((squares.at[pl.ds(0, ROWS - 1)], ss.at[18]))
    gram = add_up([dot(rows[:, 256 * j:256 * (j + 1)].astype(BF16), lanes[j], NT) for j in range(Y)])
    gram = (gram * (1.0 / (square * (1.0 / (128 * D)) + 1e-30))).astype(BF16)
    for j in range(Y):
        cubic = dot(gram, lanes[j], NN)
        for i in range(ROWS):
            stack[i, 4 * j:4 * (j + 1)] = cubic[4 * i:4 * (i + 1)]
    c_out[...] = stack[...].astype(BF16)
    for d in ROW_ORDER:
        peer = rowpeer(d)
        send(c_out.at[peer[0]], c_in.at[r], ss.at[17], rs.at[17], peer)
    sent.append((c_in.at[pl.ds(0, ROWS - 1)], ss.at[17]))
    c_in[r] = c_out[r]
    for ref, sem in earlier:
        wait(ref, sem)
    linear = jnp.concatenate([req[Y * r + j] for j in range(Y)], axis=1)
    wait(squares.at[pl.ds(0, ROWS - 1)], rs.at[18])
    each = [squares[i][:, 0:1] for i in range(ROWS)]
    mean = add_up(each) * (1.0 / (D * D)) + 1e-30
    inverse = 1.0 / (mean * (4.0 * D))
    scale = lax.rsqrt(mean) * (1.0 / (2.0 * math.sqrt(D)))
    wait(c_in.at[pl.ds(0, ROWS - 1)], rs.at[17])
    cubic = add_up([
        c_in[i].astype(F32) * ((each[i] * (1.0 / (128 * D)) + 1e-30) * inverse) for i in range(ROWS)])
    cubic = jnp.concatenate([cubic[4 * j:4 * (j + 1)] for j in range(Y)], axis=1)
    out_ref[...] = (math.sqrt(D) * scale) * (1.5 * linear - 0.5 * cubic)
    finish()


def shards(src_emb, tgt_emb, rotation, src_ids, tgt_ids):
    vmem = pltpu.VMEM
    scratch = [
        vmem((D, W), BF16),
        vmem((ROWS, 128, W), BF16),
        vmem((W, D), BF16),
        vmem((D, D), BF16),
        vmem((W, D), BF16),
        vmem((W, W), BF16),
        vmem((W, W), BF16),
        vmem((2, 1, W), jnp.int32),
        vmem((ITERS, COLS, 1, W), F32),
        vmem((ITERS, ROWS, 1, W), F32),
        vmem((W, W), BF16),
        vmem((X, 128, W), BF16),
        vmem((2, 1, W), F32),
        vmem((2, W, W), BF16),
        vmem((PARTS, X - 1, ROWS_IN, W), BF16),
        vmem((PARTS, X - 1, ROWS_IN, W), BF16),
        vmem((PARTS, Y - 1, ROWS_IN, 256), BF16),
        vmem((PARTS, Y - 1, ROWS_IN, 256), BF16),
        vmem((PARTS, ROWS_IN, 256), F32),
        vmem((Z - 1, 16, 256), BF16),
        vmem((Z - 1, 16, 256), BF16),
        vmem((COLS, 16, 256), BF16),
        vmem((Y, 4, 256), F32),
        vmem((ROWS * Y, 4, 256), F32),
        vmem((32, D), F32),
        vmem((ROWS, 16, 256), F32),
        vmem((ROWS, 1, 128), F32),
        vmem((ROWS, 16, 256), BF16),
        vmem((ROWS, 16, 256), BF16),
        pltpu.SemaphoreType.DMA((5,)),
        pltpu.SemaphoreType.DMA((40,)),
        pltpu.SemaphoreType.DMA((28,)),
        pltpu.SemaphoreType.DMA((21,)),
        pltpu.SemaphoreType.DMA((21,)),
    ]
    hbm = pl.BlockSpec(memory_space=pltpu.HBM)
    here = pl.BlockSpec(memory_space=pltpu.VMEM)
    return pl.pallas_call(
        body,
        out_shape=pltpu.VMEM((4, D), F32),
        in_specs=[hbm] * 5,
        out_specs=here,
        scratch_shapes=scratch,
        compiler_params=pltpu.CompilerParams(
            collective_id=0, has_side_effects=True, vmem_limit_bytes=60 * 2**20
        ),
        name="procrustes",
    )(src_emb.T, tgt_emb, rotation, src_ids.reshape(1, W), tgt_ids.reshape(1, W))


def solution(mesh):
    return jax.shard_map(
        shards,
        mesh=mesh,
        in_specs=(P("row", "col"), P("col", "row"), P(), P("row"), P("col")),
        out_specs=P(("row", "col"), None),
        check_vma=False,
    )
```

```python
import math

import jax
import jax.numpy as jnp
from jax import lax
from jax.experimental import pallas as pl
from jax.experimental.pallas import tpu as pltpu
from jax.sharding import PartitionSpec as P

MESH = pl.DeviceIdType.MESH
F32 = jnp.float32
BF16 = jnp.bfloat16
D = 1024
W = 512
ITERS = 3
X, Y, Z = 4, 4, 8
ROWS, COLS = 2 * X, Y * Z


def hops(step, size):
    return min(step, size - step)


COL_ORDER = sorted(
    ((dy, dz) for dy in range(Y) for dz in range(Z) if dy or dz),
    key=lambda d: -hops(d[0], Y) - hops(d[1], Z))
PLANE_ORDER = sorted(
    ((dx, dk, dy) for dx in range(X) for dk in range(2) for dy in range(Y) if dx or dk or dy),
    key=lambda d: -2 * hops(d[0], X) - 3 * d[1] - 2 * hops(d[2], Y))
ROW_ORDER = [d[:2] for d in PLANE_ORDER if d[2] == 0]
Z_ORDER = (4, 3, 5, 2, 6, 1, 7)
Z_NEAR = (0, 2, 6, 1, 7, 3, 5, 4)
PARTS = 4
ROWS_IN = 128 // PARTS
CHUNKS = Z // PARTS
XY_ORDER = (2, 1, 3)
NN = (((1,), (0,)), ((), ()))
NT = (((1,), (1,)), ((), ()))


def dot(a, b, dims):
    return lax.dot_general(a, b, dims, preferred_element_type=F32)


def send(src, dst, send_sem, recv_sem, device):
    pltpu.make_async_remote_copy(
        src_ref=src, dst_ref=dst, send_sem=send_sem, recv_sem=recv_sem,
        device_id=device, device_id_type=MESH,
    ).start()


def wait(ref, sem):
    pltpu.make_async_copy(ref, ref, sem).wait()


def add_up(parts):
    while len(parts) > 1:
        parts = [a + b for a, b in zip(parts[::2], parts[1::2])]
    return parts[0]


def block(i, size):
    return pl.ds(pl.multiple_of(i * size, size), size)


def body(src_hbm, tgt_hbm, rot_hbm, src_ids, tgt_ids, out_ref,
         src_t, ordered, tgt, rot, u, kt, kst, ids, colbuf, rowbuf,
         kt_mate, ord_mate, src_factor, plan, a_x, x_out, yb, y_out, y_mine, zb, z_out, xr, own4, req, rows, stack, squares, c_out, c_in,
         local, zs, xs, ss, rs):
    sent = []

    def finish():
        for ref, sem in sent:
            wait(ref, sem)

    r, c = lax.axis_index("row"), lax.axis_index("col")
    x, core = r // 2, r % 2
    y, z = c // Z, c % Z
    mate = (2 * x + (1 - core), c)

    def xpeer(k):
        return (2 * ((x + k) % X) + core, c)

    def ypeer(k):
        return (r, Z * ((y + k) % Y) + z)

    def zpeer(k):
        return (r, Z * y + (z + k) % Z)

    def colpeer(d):
        return (r, Z * ((y + d[0]) % Y) + (z + d[1]) % Z)

    def rowpeer(d):
        return (2 * ((x + d[0]) % X) + (core + d[1]) % 2, c)

    def planepeer(d):
        return (rowpeer(d)[0], Z * ((y + d[2]) % Y) + z)

    def feature(i, j):
        return pl.ds(pl.multiple_of(128 * i + 32 * j, 32), 32)

    mine = src_t.at[feature(z, y)]
    bar = pltpu.get_barrier_semaphore()

    near = [zpeer(k) for k in (2, 6, 1, 7)] + [xpeer(k) for k in XY_ORDER] + [ypeer(k) for k in XY_ORDER] + [mate]
    for device in near:
        pl.semaphore_signal(bar, inc=1, device_id=device, device_id_type=MESH)
    load_src = pltpu.make_async_copy(src_hbm, mine, local.at[0])
    load_src.start()
    my_tgt = tgt.at[:, block(r, 128)]
    load_tgt = pltpu.make_async_copy(tgt_hbm, my_tgt, local.at[1])
    load_tgt.start()
    load_src.wait()
    load_tgt.wait()
    pl.semaphore_wait(bar, len(near))

    def over_y(k):
        got = src_t.at[feature((z + Z - k) % Z, y)]
        wait(mine, zs.at[k])
        if k in (2, 6):
            send(got, got, ss.at[0], zs.at[3 if k == 2 else 5], zpeer(1 if k == 2 else 7))
            half = src_t.at[feature((z + Z - k) % Z, y), pl.ds(0 if k == 2 else W // 2, W // 2)]
            send(half, half, ss.at[0], zs.at[4], zpeer(k))
        for j in (1, 3, 2):
            send(got, got, ss.at[2], zs.at[32 + k], ypeer(j))

    def over_z(j):
        got = src_t.at[feature(z, (y + Y - j) % Y)]
        wait(got, zs.at[24 + j])
        for k in (1, 7):
            send(got, got, ss.at[0], zs.at[32 + k], zpeer(k))

    for j in (1, 3, 2):
        send(mine, mine, ss.at[2], zs.at[24 + j], ypeer(j))
    for k in (2, 6, 1, 7):
        send(mine, mine, ss.at[0], zs.at[k], zpeer(k))
    for k in (1, 3, 2):
        send(my_tgt, my_tgt, ss.at[1], xs.at[k], xpeer(k))
    send(my_tgt, my_tgt, ss.at[3], rs.at[3], mate)
    for i in range(Z):
        for j in range(Y):
            pltpu.make_async_copy(
                rot_hbm.at[pl.ds(32 * (Z * j + i), 32)], rot.at[pl.ds(128 * i + 32 * j, 32)], local.at[2]).start()
    load_ids = [pltpu.make_async_copy(ref, ids.at[i], local.at[3 + i]) for i, ref in enumerate((src_ids, tgt_ids))]
    for load in load_ids:
        load.start()
    sent.append((src_t.at[pl.ds(0, 13 * 32), :], ss.at[0]))
    sent.append((tgt.at[:, pl.ds(0, 384)], ss.at[1]))
    sent.append((src_t.at[pl.ds(0, 18 * 32), :], ss.at[2]))
    sent.append((tgt.at[:, pl.ds(0, 512)], ss.at[3]))

    def forward_tgt(k):
        got = tgt.at[:, block(2 * ((x + X - k) % X) + core, 128)]
        wait(got, xs.at[k])
        send(got, got, ss.at[3], rs.at[3], mate)

    over_y(2)
    over_y(6)
    over_z(1)
    over_z(3)
    over_z(2)
    over_y(3)
    over_y(5)
    forward_tgt(1)
    forward_tgt(3)
    over_y(4)
    forward_tgt(2)

    wait(tgt.at[:, pl.ds(0, 512)], rs.at[3])
    wait(rot, local.at[2])
    tv = tgt[...].astype(F32)
    tsum = jnp.sum(tv * tv, axis=1, keepdims=True)
    tscale = lax.rsqrt(tsum * (1.0 / D) + 1e-06) * (1.0 / math.sqrt(D))
    u[...] = (dot(tgt[...], rot[...], NT) * tscale).astype(BF16)
    for load in load_ids:
        load.wait()
    logits = jnp.zeros((W, W), F32)
    square = jnp.zeros((1, W), F32)
    for k in Z_NEAR:
        i = (z + Z - k) % Z
        here = src_t.at[block(i, 128)]
        if k in (1, 7):
            wait(mine, zs.at[k])
        if k:
            wait(src_t.at[pl.ds(0, 96)], zs.at[32 + k])
        part = here[...]
        logits = logits + dot(u[:, block(i, 128)], part, NN)
        part = part.astype(F32)
        square = square + jnp.sum(part * part, axis=0, keepdims=True)
    sscale = lax.rsqrt(square * (1.0 / D) + 1e-06) * (1.0 / math.sqrt(D))
    kt[...] = jnp.exp(logits * (sscale * (1.0 / 0.03))).astype(BF16)

    row8 = lax.broadcasted_iota(jnp.int32, (8, W), 0)

    def matvec(v, matrix):
        high = v.astype(BF16).astype(F32)
        both = jnp.where(row8 == 0, high, jnp.where(row8 == 1, v - high, 0.0)).astype(BF16)
        return jnp.sum(dot(both, matrix[...], NN), axis=0, keepdims=True)

    def meanwhile():
        at = lax.broadcasted_iota(jnp.int32, (128, 128), 0)
        step = jnp.zeros((128, 128), jnp.int32)
        for i, k in enumerate(Z_ORDER):
            step = jnp.where(at // 16 == i, k, step)
        to = 32 * (at // 4 % 4) + 4 * ((z + step) % Z) + at % 4
        order = (lax.broadcasted_iota(jnp.int32, (128, 128), 1) == to).astype(BF16)
        kst[...] = jnp.transpose(kt[...])
        for i in range(ROWS):
            natural = [src_t[128 * j + 32 * (i // 2):128 * j + 32 * (i // 2) + 32]
                       for j in range(4 * (i % 2), 4 * (i % 2) + 4)]
            ordered[i] = dot(order, jnp.concatenate(natural, axis=0), NN).astype(BF16)
        for j in range(X):
            send(ordered.at[2 * j + (1 - core)], ord_mate.at[j], ss.at[19], xs.at[5], mate)
        sent.append((ord_mate, ss.at[19]))

    def sum_col(part, it):
        colbuf[it, c] = part

        for d in COL_ORDER:
            send(colbuf.at[it, c], colbuf.at[it, c], ss.at[4 + it], rs.at[4 + it], colpeer(d))
        sent.append((colbuf.at[it, pl.ds(0, COLS - 1)], ss.at[4 + it]))
        if it == 0:
            send(kt, kt_mate, ss.at[10], xs.at[4], mate)
            sent.append((kt_mate, ss.at[10]))
            meanwhile()
        wait(colbuf.at[it, pl.ds(0, COLS - 1)], rs.at[4 + it])
        if it == 0:
            wait(kt_mate, xs.at[4])
            wait(ord_mate, xs.at[5])
        return add_up([colbuf[it, i] for i in range(COLS)])

    def start_row(part, it):
        rowbuf[it, r] = part
        for d in ROW_ORDER:
            send(rowbuf.at[it, r], rowbuf.at[it, r], ss.at[7 + it], rs.at[7 + it], rowpeer(d))
        sent.append((rowbuf.at[it, pl.ds(0, ROWS - 1)], ss.at[7 + it]))

    def end_row(it):
        wait(rowbuf.at[it, pl.ds(0, ROWS - 1)], rs.at[7 + it])
        return add_up([rowbuf[it, i] for i in range(ROWS)])

    src_mass = lax.rsqrt(1000.0 + ids[0].astype(F32))
    tgt_mass = lax.rsqrt(1000.0 + ids[1].astype(F32))
    tgt_scale = jnp.ones((1, W), F32)
    for it in range(ITERS):
        src_scale = src_mass / sum_col(matvec(tgt_scale, kt), it)
        if it < ITERS - 1:
            start_row(matvec(src_scale, kst), it)
            tgt_scale = tgt_mass / end_row(it)

    src_factor[0] = src_scale * sscale
    send(src_factor.at[0], src_factor.at[1], ss.at[20], xs.at[6], mate)
    sent.append((src_factor.at[0], ss.at[20]))
    plan[0] = (kt[...].astype(F32) * src_factor[0]).astype(BF16)

    def some_rows(h, i):
        first = pl.ds(ROWS_IN * h, ROWS_IN)
        rows_of = [ordered[2 * ((x + j) % X) + core, first] if i == 0 else ord_mate[(x + j) % X, first] for j in range(X)]
        return dot(jnp.concatenate(rows_of, axis=0), plan[i], NT)

    first_part = some_rows(0, 0)
    start_row(matvec(src_scale, kst), ITERS - 1)
    tscale_l = jnp.transpose(jnp.broadcast_to(tscale, (W, 128)))[0:1, :]
    wait(src_factor.at[1], xs.at[6])
    plan[1] = (kt_mate[...].astype(F32) * src_factor[1]).astype(BF16)
    kept = []
    for h in range(PARTS):
        part = (some_rows(h, 0) if h else first_part) + some_rows(h, 1)
        kept.append(part[0:ROWS_IN])
        for k in (2, 1, 3):
            x_out[h, k - 1] = part[ROWS_IN * k:ROWS_IN * (k + 1)].astype(BF16)
            send(x_out.at[h, k - 1], a_x.at[h, k - 1], ss.at[11], xs.at[12 + h], xpeer(k))
    sent.append((a_x, ss.at[11]))
    factor = (tgt_mass / end_row(ITERS - 1)) * tscale_l

    for h in range(PARTS):
        wait(a_x.at[h], xs.at[12 + h])
        total = kept[h] + ((a_x[h, 0].astype(F32) + a_x[h, 1].astype(F32)) + a_x[h, 2].astype(F32))
        total = (total * factor).astype(BF16)
        for j in XY_ORDER:
            y_out[h, j - 1] = dot(total, tgt[:, block((y + j) % Y, 256)], NN).astype(BF16)
            send(y_out.at[h, j - 1], yb.at[h, j - 1], ss.at[12], xs.at[20 + h], ypeer(j))
        y_mine[h] = dot(total, tgt[:, block(y, 256)], NN)
    sent.append((yb, ss.at[12]))
    for h in range(PARTS):
        wait(yb.at[h], xs.at[20 + h])
        part = (y_mine[h] + yb[h, 0].astype(F32)) + (yb[h, 1].astype(F32) + yb[h, 2].astype(F32))
        for i in range(CHUNKS):
            own = part[16 * i:16 * (i + 1)]
            k = (Z_ORDER + (0,))[CHUNKS * h + i]
            if k:
                z_out[k - 1] = own.astype(BF16)
                send(z_out.at[k - 1], zb.at[k - 1], ss.at[13], rs.at[13], zpeer(k))
    sent.append((zb, ss.at[13]))
    wait(zb, rs.at[13])
    own = own + jnp.sum(zb[...].astype(F32), axis=0)

    def cell(i, j):
        return xr.at[block(i, 16), block(j, 256)]

    xr[block(z, 16), block(y, 256)] = own.astype(BF16)
    for k in Z_ORDER:
        send(cell(z, y), cell(z, y), ss.at[14], zs.at[16 + k], zpeer(k))
    sent.append((xr.at[pl.ds(0, 112), pl.ds(0, 256)], ss.at[14]))
    for j in XY_ORDER:
        send(cell(z, y), cell(z, y), ss.at[16], rs.at[16], ypeer(j))
    for j in range(Y):
        own4[j] = own[4 * j:4 * (j + 1)]
    for d in PLANE_ORDER:
        send(own4.at[(y + d[2]) % Y], req.at[Y * r + y], ss.at[15], rs.at[15], planepeer(d))
    sent.append((req.at[pl.ds(0, ROWS * Y - 1)], ss.at[15]))
    req[Y * r + y] = own4[y]
    for k in (1, 7, 2, 6, 3, 5, 4):
        got = cell((z + Z - k) % Z, y)
        wait(got, zs.at[16 + k])
        for j in XY_ORDER:
            send(got, got, ss.at[16], rs.at[16], ypeer(j))
    sent.append((xr.at[pl.ds(0, 96), :], ss.at[16]))
    wait(req.at[pl.ds(0, ROWS * Y - 1)], rs.at[15])
    for i in range(ROWS):
        for j in range(Y):
            rows[4 * i:4 * (i + 1), 256 * j:256 * (j + 1)] = req[Y * i + j]
    wait(xr.at[pl.ds(0, 96), :], rs.at[16])

    xv = xr[...].astype(F32)
    square = jnp.sum(jnp.sum(xv * xv, axis=0, keepdims=True), axis=1, keepdims=True)
    squares[r] = jnp.broadcast_to(square, (1, 128))
    for d in ROW_ORDER:
        send(squares.at[r], squares.at[r], ss.at[18], rs.at[18], rowpeer(d))
    sent.append((squares.at[pl.ds(0, ROWS - 1)], ss.at[18]))
    gram = dot(rows[...].astype(BF16), xr[...], NT) * (1.0 / (square * (1.0 / (128 * D)) + 1e-30))
    cubic = dot(gram.astype(BF16), xr[...], NN)
    for i in range(ROWS):
        for j in range(Y):
            stack[i, 4 * j:4 * (j + 1)] = cubic[4 * i:4 * (i + 1), 256 * j:256 * (j + 1)]
    c_out[...] = stack[...].astype(BF16)
    for d in ROW_ORDER:
        peer = rowpeer(d)
        send(c_out.at[peer[0]], c_in.at[r], ss.at[17], rs.at[17], peer)
    sent.append((c_in.at[pl.ds(0, ROWS - 1)], ss.at[17]))
    c_in[r] = c_out[r]
    linear = jnp.concatenate([req[Y * r + j] for j in range(Y)], axis=1)
    wait(squares.at[pl.ds(0, ROWS - 1)], rs.at[18])
    each = [squares[i][:, 0:1] for i in range(ROWS)]
    mean = add_up(each) * (1.0 / (D * D)) + 1e-30
    inverse = 1.0 / (mean * (4.0 * D))
    scale = lax.rsqrt(mean) * (1.0 / (2.0 * math.sqrt(D)))
    wait(c_in.at[pl.ds(0, ROWS - 1)], rs.at[17])
    cubic = add_up([
        c_in[i].astype(F32) * ((each[i] * (1.0 / (128 * D)) + 1e-30) * inverse) for i in range(ROWS)])
    cubic = jnp.concatenate([cubic[4 * j:4 * (j + 1)] for j in range(Y)], axis=1)
    out_ref[...] = (math.sqrt(D) * scale) * (1.5 * linear - 0.5 * cubic)
    finish()


def shards(src_emb, tgt_emb, rotation, src_ids, tgt_ids):
    vmem = pltpu.VMEM
    scratch = [
        vmem((D, W), BF16),
        vmem((ROWS, 128, W), BF16),
        vmem((W, D), BF16),
        vmem((D, D), BF16),
        vmem((W, D), BF16),
        vmem((W, W), BF16),
        vmem((W, W), BF16),
        vmem((2, 1, W), jnp.int32),
        vmem((ITERS, COLS, 1, W), F32),
        vmem((ITERS, ROWS, 1, W), F32),
        vmem((W, W), BF16),
        vmem((X, 128, W), BF16),
        vmem((2, 1, W), F32),
        vmem((2, W, W), BF16),
        vmem((PARTS, X - 1, ROWS_IN, W), BF16),
        vmem((PARTS, X - 1, ROWS_IN, W), BF16),
        vmem((PARTS, Y - 1, ROWS_IN, 256), BF16),
        vmem((PARTS, Y - 1, ROWS_IN, 256), BF16),
        vmem((PARTS, ROWS_IN, 256), F32),
        vmem((Z - 1, 16, 256), BF16),
        vmem((Z - 1, 16, 256), BF16),
        vmem((128, D), BF16),
        vmem((Y, 4, 256), F32),
        vmem((ROWS * Y, 4, 256), F32),
        vmem((32, D), F32),
        vmem((ROWS, 16, 256), F32),
        vmem((ROWS, 1, 128), F32),
        vmem((ROWS, 16, 256), BF16),
        vmem((ROWS, 16, 256), BF16),
        pltpu.SemaphoreType.DMA((5,)),
        pltpu.SemaphoreType.DMA((40,)),
        pltpu.SemaphoreType.DMA((28,)),
        pltpu.SemaphoreType.DMA((21,)),
        pltpu.SemaphoreType.DMA((21,)),
    ]
    hbm = pl.BlockSpec(memory_space=pltpu.HBM)
    here = pl.BlockSpec(memory_space=pltpu.VMEM)
    return pl.pallas_call(
        body,
        out_shape=pltpu.VMEM((4, D), F32),
        in_specs=[hbm] * 5,
        out_specs=here,
        scratch_shapes=scratch,
        compiler_params=pltpu.CompilerParams(
            collective_id=0, has_side_effects=True, vmem_limit_bytes=60 * 2**20
        ),
        name="procrustes",
    )(src_emb.T, tgt_emb, rotation, src_ids.reshape(1, W), tgt_ids.reshape(1, W))


def solution(mesh):
    return jax.shard_map(
        shards,
        mesh=mesh,
        in_specs=(P("row", "col"), P("col", "row"), P(), P("row"), P("col")),
        out_specs=P(("row", "col"), None),
        check_vma=False,
    )
```

```python
import math

import jax
import jax.numpy as jnp
from jax import lax
from jax.experimental import pallas as pl
from jax.experimental.pallas import tpu as pltpu
from jax.sharding import PartitionSpec as P

MESH = pl.DeviceIdType.MESH
F32 = jnp.float32
BF16 = jnp.bfloat16
D = 1024
W = 512
ITERS = 3
X, Y, Z = 4, 4, 8
ROWS, COLS = 2 * X, Y * Z


def hops(step, size):
    return min(step, size - step)


COL_ORDER = sorted(
    ((dy, dz) for dy in range(Y) for dz in range(Z) if dy or dz),
    key=lambda d: -hops(d[0], Y) - hops(d[1], Z))
PLANE_ORDER = sorted(
    ((dx, dk, dy) for dx in range(X) for dk in range(2) for dy in range(Y) if dx or dk or dy),
    key=lambda d: -2 * hops(d[0], X) - 3 * d[1] - 2 * hops(d[2], Y))
ROW_ORDER = [d[:2] for d in PLANE_ORDER if d[2] == 0]
Z_ORDER = (4, 3, 5, 2, 6, 1, 7)
Z_NEAR = (0, 2, 6, 1, 7, 3, 5, 4)
PARTS = 4
ROWS_IN = 128 // PARTS
CHUNKS = Z // PARTS
XY_ORDER = (2, 1, 3)
NN = (((1,), (0,)), ((), ()))
NT = (((1,), (1,)), ((), ()))


def dot(a, b, dims):
    return lax.dot_general(a, b, dims, preferred_element_type=F32)


def send(src, dst, send_sem, recv_sem, device):
    pltpu.make_async_remote_copy(
        src_ref=src, dst_ref=dst, send_sem=send_sem, recv_sem=recv_sem,
        device_id=device, device_id_type=MESH,
    ).start()


def wait(ref, sem):
    pltpu.make_async_copy(ref, ref, sem).wait()


def add_up(parts):
    while len(parts) > 1:
        parts = [a + b for a, b in zip(parts[::2], parts[1::2])]
    return parts[0]


def block(i, size):
    return pl.ds(pl.multiple_of(i * size, size), size)


def body(src_hbm, tgt_hbm, rot_hbm, src_ids, tgt_ids, out_ref,
         src_t, ordered, tgt, rot, u, kt, kst, ids, colbuf, rowbuf,
         kt_mate, ord_mate, src_factor, plan, a_x, x_out, yb, y_out, y_mine, zb, z_out, xr, own4, req, rows, stack, squares, c_out, c_in,
         local, zs, xs, ss, rs):
    sent = []

    def finish():
        for ref, sem in sent:
            wait(ref, sem)

    r, c = lax.axis_index("row"), lax.axis_index("col")
    x, core = r // 2, r % 2
    y, z = c // Z, c % Z
    mate = (2 * x + (1 - core), c)

    def xpeer(k):
        return (2 * ((x + k) % X) + core, c)

    def ypeer(k):
        return (r, Z * ((y + k) % Y) + z)

    def zpeer(k):
        return (r, Z * y + (z + k) % Z)

    def colpeer(d):
        return (r, Z * ((y + d[0]) % Y) + (z + d[1]) % Z)

    def rowpeer(d):
        return (2 * ((x + d[0]) % X) + (core + d[1]) % 2, c)

    def planepeer(d):
        return (rowpeer(d)[0], Z * ((y + d[2]) % Y) + z)

    def feature(i, j):
        return pl.ds(pl.multiple_of(128 * i + 32 * j, 32), 32)

    mine = src_t.at[feature(z, y)]
    load_src = pltpu.make_async_copy(src_hbm, mine, local.at[0])
    load_src.start()
    my_tgt = tgt.at[:, block(r, 128)]
    load_tgt = pltpu.make_async_copy(tgt_hbm, my_tgt, local.at[1])
    load_tgt.start()
    for i in range(Z):
        for j in range(Y):
            pltpu.make_async_copy(
                rot_hbm.at[pl.ds(32 * (Z * j + i), 32)], rot.at[pl.ds(128 * i + 32 * j, 32)], local.at[2]).start()
    load_ids = [pltpu.make_async_copy(ref, ids.at[i], local.at[3 + i]) for i, ref in enumerate((src_ids, tgt_ids))]
    for load in load_ids:
        load.start()
    bar = pltpu.get_barrier_semaphore()

    near = [zpeer(k) for k in (2, 6, 1, 7)] + [xpeer(k) for k in XY_ORDER] + [ypeer(k) for k in XY_ORDER] + [mate]
    for device in near:
        pl.semaphore_signal(bar, inc=1, device_id=device, device_id_type=MESH)
    load_src.wait()
    load_tgt.wait()
    pl.semaphore_wait(bar, len(near))

    def over_y(k):
        got = src_t.at[feature((z + Z - k) % Z, y)]
        wait(mine, zs.at[k])
        if k in (2, 6):
            send(got, got, ss.at[0], zs.at[3 if k == 2 else 5], zpeer(1 if k == 2 else 7))
            half = src_t.at[feature((z + Z - k) % Z, y), pl.ds(0 if k == 2 else W // 2, W // 2)]
            send(half, half, ss.at[0], zs.at[4], zpeer(k))
        for j in (1, 3, 2):
            send(got, got, ss.at[2], zs.at[32 + k], ypeer(j))

    def over_z(j):
        got = src_t.at[feature(z, (y + Y - j) % Y)]
        wait(got, zs.at[24 + j])
        for k in (1, 7):
            send(got, got, ss.at[0], zs.at[32 + k], zpeer(k))

    for j in (1, 3, 2):
        send(mine, mine, ss.at[2], zs.at[24 + j], ypeer(j))
    for k in (2, 6, 1, 7):
        send(mine, mine, ss.at[0], zs.at[k], zpeer(k))
    for k in (1, 3, 2):
        send(my_tgt, my_tgt, ss.at[1], xs.at[k], xpeer(k))
    send(my_tgt, my_tgt, ss.at[3], rs.at[3], mate)
    sent.append((src_t.at[pl.ds(0, 13 * 32), :], ss.at[0]))
    sent.append((tgt.at[:, pl.ds(0, 384)], ss.at[1]))
    sent.append((src_t.at[pl.ds(0, 18 * 32), :], ss.at[2]))
    sent.append((tgt.at[:, pl.ds(0, 512)], ss.at[3]))

    def forward_tgt(k):
        got = tgt.at[:, block(2 * ((x + X - k) % X) + core, 128)]
        wait(got, xs.at[k])
        send(got, got, ss.at[3], rs.at[3], mate)

    over_y(2)
    over_y(6)
    over_z(1)
    over_z(3)
    over_z(2)
    over_y(3)
    over_y(5)
    forward_tgt(1)
    forward_tgt(3)
    over_y(4)
    forward_tgt(2)

    wait(tgt.at[:, pl.ds(0, 512)], rs.at[3])
    wait(rot, local.at[2])
    tv = tgt[...].astype(F32)
    tsum = jnp.sum(tv * tv, axis=1, keepdims=True)
    tscale = lax.rsqrt(tsum * (1.0 / D) + 1e-06) * (1.0 / math.sqrt(D))
    u[...] = (dot(tgt[...], rot[...], NT) * tscale).astype(BF16)
    for load in load_ids:
        load.wait()
    logits = jnp.zeros((W, W), F32)
    square = jnp.zeros((1, W), F32)
    for k in Z_NEAR:
        i = (z + Z - k) % Z
        here = src_t.at[block(i, 128)]
        if k in (1, 7):
            wait(mine, zs.at[k])
        if k:
            wait(src_t.at[pl.ds(0, 96)], zs.at[32 + k])
        part = here[...]
        logits = logits + dot(u[:, block(i, 128)], part, NN)
        part = part.astype(F32)
        square = square + jnp.sum(part * part, axis=0, keepdims=True)
    sscale = lax.rsqrt(square * (1.0 / D) + 1e-06) * (1.0 / math.sqrt(D))
    kt[...] = jnp.exp(logits * (sscale * (1.0 / 0.03))).astype(BF16)

    row8 = lax.broadcasted_iota(jnp.int32, (8, W), 0)

    def matvec(v, matrix):
        high = v.astype(BF16).astype(F32)
        both = jnp.where(row8 == 0, high, jnp.where(row8 == 1, v - high, 0.0)).astype(BF16)
        return jnp.sum(dot(both, matrix[...], NN), axis=0, keepdims=True)

    def meanwhile():
        at = lax.broadcasted_iota(jnp.int32, (128, 128), 0)
        step = jnp.zeros((128, 128), jnp.int32)
        for i, k in enumerate(Z_ORDER):
            step = jnp.where(at // 16 == i, k, step)
        to = 32 * (at // 4 % 4) + 4 * ((z + step) % Z) + at % 4
        order = (lax.broadcasted_iota(jnp.int32, (128, 128), 1) == to).astype(BF16)
        kst[...] = jnp.transpose(kt[...])
        for i in range(ROWS):
            natural = [src_t[128 * j + 32 * (i // 2):128 * j + 32 * (i // 2) + 32]
                       for j in range(4 * (i % 2), 4 * (i % 2) + 4)]
            ordered[i] = dot(order, jnp.concatenate(natural, axis=0), NN).astype(BF16)
        for j in range(X):
            send(ordered.at[2 * j + (1 - core)], ord_mate.at[j], ss.at[19], xs.at[5], mate)
        sent.append((ord_mate, ss.at[19]))

    def sum_col(part, it):
        colbuf[it, c] = part

        for d in COL_ORDER:
            send(colbuf.at[it, c], colbuf.at[it, c], ss.at[4 + it], rs.at[4 + it], colpeer(d))
        sent.append((colbuf.at[it, pl.ds(0, COLS - 1)], ss.at[4 + it]))
        if it == 0:
            send(kt, kt_mate, ss.at[10], xs.at[4], mate)
            sent.append((kt_mate, ss.at[10]))
            meanwhile()
        wait(colbuf.at[it, pl.ds(0, COLS - 1)], rs.at[4 + it])
        if it == 0:
            wait(kt_mate, xs.at[4])
            wait(ord_mate, xs.at[5])
        return add_up([colbuf[it, i] for i in range(COLS)])

    def start_row(part, it):
        rowbuf[it, r] = part
        for d in ROW_ORDER:
            send(rowbuf.at[it, r], rowbuf.at[it, r], ss.at[7 + it], rs.at[7 + it], rowpeer(d))
        sent.append((rowbuf.at[it, pl.ds(0, ROWS - 1)], ss.at[7 + it]))

    def end_row(it):
        wait(rowbuf.at[it, pl.ds(0, ROWS - 1)], rs.at[7 + it])
        return add_up([rowbuf[it, i] for i in range(ROWS)])

    src_mass = lax.rsqrt(1000.0 + ids[0].astype(F32))
    tgt_mass = lax.rsqrt(1000.0 + ids[1].astype(F32))
    tgt_scale = jnp.ones((1, W), F32)
    for it in range(ITERS):
        src_scale = src_mass / sum_col(matvec(tgt_scale, kt), it)
        if it < ITERS - 1:
            start_row(matvec(src_scale, kst), it)
            tgt_scale = tgt_mass / end_row(it)

    src_factor[0] = src_scale * sscale
    send(src_factor.at[0], src_factor.at[1], ss.at[20], xs.at[6], mate)
    sent.append((src_factor.at[0], ss.at[20]))
    plan[0] = (kt[...].astype(F32) * src_factor[0]).astype(BF16)

    def some_rows(h, i):
        first = pl.ds(ROWS_IN * h, ROWS_IN)
        rows_of = [ordered[2 * ((x + j) % X) + core, first] if i == 0 else ord_mate[(x + j) % X, first] for j in range(X)]
        return dot(jnp.concatenate(rows_of, axis=0), plan[i], NT)

    first_part = some_rows(0, 0)
    tscale_l = jnp.transpose(jnp.broadcast_to(tscale, (W, 128)))[0:1, :]
    wait(src_factor.at[1], xs.at[6])
    plan[1] = (kt_mate[...].astype(F32) * src_factor[1]).astype(BF16)
    kept = []
    for h in range(PARTS):
        part = (some_rows(h, 0) if h else first_part) + some_rows(h, 1)
        kept.append(part[0:ROWS_IN])
        for k in (2, 1, 3):
            x_out[h, k - 1] = part[ROWS_IN * k:ROWS_IN * (k + 1)].astype(BF16)
            send(x_out.at[h, k - 1], a_x.at[h, k - 1], ss.at[11], xs.at[12 + h], xpeer(k))
        if h == 0:
            start_row(matvec(src_scale, kst), ITERS - 1)
    sent.append((a_x, ss.at[11]))
    factor = (tgt_mass / end_row(ITERS - 1)) * tscale_l

    for h in range(PARTS):
        wait(a_x.at[h], xs.at[12 + h])
        total = kept[h] + ((a_x[h, 0].astype(F32) + a_x[h, 1].astype(F32)) + a_x[h, 2].astype(F32))
        total = (total * factor).astype(BF16)
        for j in XY_ORDER:
            y_out[h, j - 1] = dot(total, tgt[:, block((y + j) % Y, 256)], NN).astype(BF16)
            send(y_out.at[h, j - 1], yb.at[h, j - 1], ss.at[12], xs.at[20 + h], ypeer(j))
        y_mine[h] = dot(total, tgt[:, block(y, 256)], NN)
    sent.append((yb, ss.at[12]))
    for h in range(PARTS):
        wait(yb.at[h], xs.at[20 + h])
        part = (y_mine[h] + yb[h, 0].astype(F32)) + (yb[h, 1].astype(F32) + yb[h, 2].astype(F32))
        for i in range(CHUNKS):
            own = part[16 * i:16 * (i + 1)]
            k = (Z_ORDER + (0,))[CHUNKS * h + i]
            if k:
                z_out[k - 1] = own.astype(BF16)
                send(z_out.at[k - 1], zb.at[k - 1], ss.at[13], rs.at[13], zpeer(k))
    sent.append((zb, ss.at[13]))
    wait(zb, rs.at[13])
    own = own + jnp.sum(zb[...].astype(F32), axis=0)

    def cell(i, j):
        return xr.at[block(i, 16), block(j, 256)]

    xr[block(z, 16), block(y, 256)] = own.astype(BF16)
    for k in Z_ORDER:
        send(cell(z, y), cell(z, y), ss.at[14], zs.at[16 + k], zpeer(k))
    sent.append((xr.at[pl.ds(0, 112), pl.ds(0, 256)], ss.at[14]))
    for j in XY_ORDER:
        send(cell(z, y), cell(z, y), ss.at[16], rs.at[16], ypeer(j))
    for j in range(Y):
        own4[j] = own[4 * j:4 * (j + 1)]
    for d in PLANE_ORDER:
        send(own4.at[(y + d[2]) % Y], req.at[Y * r + y], ss.at[15], rs.at[15], planepeer(d))
    sent.append((req.at[pl.ds(0, ROWS * Y - 1)], ss.at[15]))
    req[Y * r + y] = own4[y]
    for k in (1, 7, 2, 6, 3, 5, 4):
        got = cell((z + Z - k) % Z, y)
        wait(got, zs.at[16 + k])
        for j in XY_ORDER:
            send(got, got, ss.at[16], rs.at[16], ypeer(j))
    sent.append((xr.at[pl.ds(0, 96), :], ss.at[16]))
    wait(req.at[pl.ds(0, ROWS * Y - 1)], rs.at[15])
    for i in range(ROWS):
        for j in range(Y):
            rows[4 * i:4 * (i + 1), 256 * j:256 * (j + 1)] = req[Y * i + j]
    wait(xr.at[pl.ds(0, 96), :], rs.at[16])

    xv = xr[...].astype(F32)
    square = jnp.sum(jnp.sum(xv * xv, axis=0, keepdims=True), axis=1, keepdims=True)
    squares[r] = jnp.broadcast_to(square, (1, 128))
    for d in ROW_ORDER:
        send(squares.at[r], squares.at[r], ss.at[18], rs.at[18], rowpeer(d))
    sent.append((squares.at[pl.ds(0, ROWS - 1)], ss.at[18]))
    gram = dot(rows[...].astype(BF16), xr[...], NT) * (1.0 / (square * (1.0 / (128 * D)) + 1e-30))
    cubic = dot(gram.astype(BF16), xr[...], NN)
    for i in range(ROWS):
        for j in range(Y):
            stack[i, 4 * j:4 * (j + 1)] = cubic[4 * i:4 * (i + 1), 256 * j:256 * (j + 1)]
    c_out[...] = stack[...].astype(BF16)
    for d in ROW_ORDER:
        peer = rowpeer(d)
        send(c_out.at[peer[0]], c_in.at[r], ss.at[17], rs.at[17], peer)
    sent.append((c_in.at[pl.ds(0, ROWS - 1)], ss.at[17]))
    c_in[r] = c_out[r]
    linear = jnp.concatenate([req[Y * r + j] for j in range(Y)], axis=1)
    wait(squares.at[pl.ds(0, ROWS - 1)], rs.at[18])
    each = [squares[i][:, 0:1] for i in range(ROWS)]
    mean = add_up(each) * (1.0 / (D * D)) + 1e-30
    inverse = 1.0 / (mean * (4.0 * D))
    scale = lax.rsqrt(mean) * (1.0 / (2.0 * math.sqrt(D)))
    wait(c_in.at[pl.ds(0, ROWS - 1)], rs.at[17])
    cubic = add_up([
        c_in[i].astype(F32) * ((each[i] * (1.0 / (128 * D)) + 1e-30) * inverse) for i in range(ROWS)])
    cubic = jnp.concatenate([cubic[4 * j:4 * (j + 1)] for j in range(Y)], axis=1)
    out_ref[...] = (math.sqrt(D) * scale) * (1.5 * linear - 0.5 * cubic)
    finish()


def shards(src_emb, tgt_emb, rotation, src_ids, tgt_ids):
    vmem = pltpu.VMEM
    scratch = [
        vmem((D, W), BF16),
        vmem((ROWS, 128, W), BF16),
        vmem((W, D), BF16),
        vmem((D, D), BF16),
        vmem((W, D), BF16),
        vmem((W, W), BF16),
        vmem((W, W), BF16),
        vmem((2, 1, W), jnp.int32),
        vmem((ITERS, COLS, 1, W), F32),
        vmem((ITERS, ROWS, 1, W), F32),
        vmem((W, W), BF16),
        vmem((X, 128, W), BF16),
        vmem((2, 1, W), F32),
        vmem((2, W, W), BF16),
        vmem((PARTS, X - 1, ROWS_IN, W), BF16),
        vmem((PARTS, X - 1, ROWS_IN, W), BF16),
        vmem((PARTS, Y - 1, ROWS_IN, 256), BF16),
        vmem((PARTS, Y - 1, ROWS_IN, 256), BF16),
        vmem((PARTS, ROWS_IN, 256), F32),
        vmem((Z - 1, 16, 256), BF16),
        vmem((Z - 1, 16, 256), BF16),
        vmem((128, D), BF16),
        vmem((Y, 4, 256), F32),
        vmem((ROWS * Y, 4, 256), F32),
        vmem((32, D), F32),
        vmem((ROWS, 16, 256), F32),
        vmem((ROWS, 1, 128), F32),
        vmem((ROWS, 16, 256), BF16),
        vmem((ROWS, 16, 256), BF16),
        pltpu.SemaphoreType.DMA((5,)),
        pltpu.SemaphoreType.DMA((40,)),
        pltpu.SemaphoreType.DMA((28,)),
        pltpu.SemaphoreType.DMA((21,)),
        pltpu.SemaphoreType.DMA((21,)),
    ]
    hbm = pl.BlockSpec(memory_space=pltpu.HBM)
    here = pl.BlockSpec(memory_space=pltpu.VMEM)
    return pl.pallas_call(
        body,
        out_shape=pltpu.VMEM((4, D), F32),
        in_specs=[hbm] * 5,
        out_specs=here,
        scratch_shapes=scratch,
        compiler_params=pltpu.CompilerParams(
            collective_id=0, has_side_effects=True, vmem_limit_bytes=60 * 2**20
        ),
        name="procrustes",
    )(src_emb.T, tgt_emb, rotation, src_ids.reshape(1, W), tgt_ids.reshape(1, W))


def solution(mesh):
    return jax.shard_map(
        shards,
        mesh=mesh,
        in_specs=(P("row", "col"), P("col", "row"), P(), P("row"), P("col")),
        out_specs=P(("row", "col"), None),
        check_vma=False,
    )
```
